32 devices in a mesh: seq: 8 (over z, core), fsdp: 4 (over y, x).
Axes of the slice: x: 2, y: 2, z: 4, core: 2. Of those that a mesh axis runs over, the one named last changes fastest.
Arguments:
- tokens: bfloat16 [4, 1024, 2048], P('fsdp', 'seq'), may hold values from -6 to 6
- segments: int32 [4, 1024], P('fsdp'), may hold values from 0 to 5, never falling along the last dimension, each value on 1 to 512 neighbouring positions
- cotangent: bfloat16 [4, 1024, 2048], P('fsdp', 'seq'), may hold values from -6 to 6
- mix_weight: float32 [2048, 6144], P(('seq', 'fsdp')), may hold values from -0.125 to 0.125
- mix_moment: float32 [2048, 6144], P(('seq', 'fsdp')), may hold values from -112 to 112
- mix_average: float32 [2048, 6144], P(('seq', 'fsdp')), may hold values from -0.125 to 0.125
- out_weight: float32 [2048, 2048], P(('seq', 'fsdp')), may hold values from -0.375 to 0.375
- out_moment: float32 [2048, 2048], P(('seq', 'fsdp')), may hold values from -112 to 112
- out_average: float32 [2048, 2048], P(('seq', 'fsdp')), may hold values from -0.375 to 0.375
- up_weight: float32 [2048, 8192], P(('seq', 'fsdp')), may hold values from -0.125 to 0.125
- up_moment: float32 [2048, 8192], P(('seq', 'fsdp')), may hold values from -112 to 112
- up_average: float32 [2048, 8192], P(('seq', 'fsdp')), may hold values from -0.125 to 0.125
- down_weight: float32 [8192, 2048], P(('seq', 'fsdp')), may hold values from -0.0625 to 0.0625
- down_moment: float32 [8192, 2048], P(('seq', 'fsdp')), may hold values from -112 to 112
- down_average: float32 [8192, 2048], P(('seq', 'fsdp')), may hold values from -0.0625 to 0.0625
- norm_gains: float32 [2, 2048], P(None, ('seq', 'fsdp')), may hold values from 0.1 to 1.9
- gain_moment: float32 [2, 2048], P(None, ('seq', 'fsdp')), may hold values from -192 to 192
- gain_average: float32 [2, 2048], P(None, ('seq', 'fsdp')), may hold values from 0.1 to 1.9
- biases: float32 [10, 2048], P(None, ('seq', 'fsdp')), may hold values from -3 to 3
- bias_moment: float32 [10, 2048], P(None, ('seq', 'fsdp')), may hold values from -192 to 192
- bias_average: float32 [10, 2048], P(None, ('seq', 'fsdp')), may hold values from -3 to 3
Outputs:
- output: bfloat16 [4, 1024, 2048], P('fsdp', 'seq')
- tokens_grad: bfloat16 [4, 1024, 2048], P('fsdp', 'seq')
- mix_moment_new: float32 [2048, 6144], P(('seq', 'fsdp'))
- mix_weight_new: float32 [2048, 6144], P(('seq', 'fsdp'))
- mix_average_new: float32 [2048, 6144], P(('seq', 'fsdp'))
- out_moment_new: float32 [2048, 2048], P(('seq', 'fsdp'))
- out_weight_new: float32 [2048, 2048], P(('seq', 'fsdp'))
- out_average_new: float32 [2048, 2048], P(('seq', 'fsdp'))
- up_moment_new: float32 [2048, 8192], P(('seq', 'fsdp'))
- up_weight_new: float32 [2048, 8192], P(('seq', 'fsdp'))
- up_average_new: float32 [2048, 8192], P(('seq', 'fsdp'))
- down_moment_new: float32 [8192, 2048], P(('seq', 'fsdp'))
- down_weight_new: float32 [8192, 2048], P(('seq', 'fsdp'))
- down_average_new: float32 [8192, 2048], P(('seq', 'fsdp'))
- gain_moment_new: float32 [2, 2048], P(None, ('seq', 'fsdp'))
- gain_weight_new: float32 [2, 2048], P(None, ('seq', 'fsdp'))
- gain_average_new: float32 [2, 2048], P(None, ('seq', 'fsdp'))
- bias_moment_new: float32 [10, 2048], P(None, ('seq', 'fsdp'))
- bias_weight_new: float32 [10, 2048], P(None, ('seq', 'fsdp'))
- bias_average_new: float32 [10, 2048], P(None, ('seq', 'fsdp'))
The draws below stay inside these ranges and needn't reach their ends.
Inputs may be any that keep to these rules, and one draw needn't show every extreme that they name: `segments`: document numbers never fall along a sequence; each document holds 1 to 512 tokens, one exactly that many.
All inputs are finite; a program needn't handle non-finite values.
Results may differ from the reference program's by a relative error of at most 0.02.
Values may be sent and summed in bfloat16 or wider, within the bound.
A program may use at most 512 MiB of HBM per device.

```python
import math
import jax
import jax.numpy as jnp
import numpy as np
from jax import lax

D = 2048
HEADS = 32
HD = 64
FF = 8192
DOCS = 6
LENGTH = 1024
SEQS = 4
TOKENS = 4096


def block_levels(rng, dims, split, low, high):
    def one(axis_at, parts):
        heights = jax.random.uniform(jax.random.fold_in(jax.random.fold_in(rng, 6), axis_at), (parts,), jnp.float32, low / len(split), high / len(split))
        return jnp.repeat(jnp.exp(heights), dims[axis_at] // parts).reshape((-1,) + (1,) * (len(dims) - axis_at - 1))

    gain = one(*split[0])
    for cut in split[1:]:
        gain = gain * one(*cut)
    return gain


def profile(number_of, total, bound, skew):
    weights = [(1 << 20) // math.isqrt(standing ** skew) + 1 for standing in range(2, number_of + 1)]
    surplus, holding = total - bound - (number_of - 1), [1] * (number_of - 1)
    while surplus > 0:
        free = [i for i in range(number_of - 1) if holding[i] < bound]
        whole, remaining = sum([weights[i] for i in free]), surplus
        for i in free:
            more = min(bound - holding[i], max(1, remaining * weights[i] // whole), surplus)
            holding[i] = holding[i] + more
            surplus = surplus - more
    return np.array([bound] + holding)


def uneven(key, count, total, most, slope):
    if count == 2:
        one = jax.random.randint(key, (), max(1, total - most), min(most, total - 1) + 1)
        return jnp.stack([one, total - one])
    tallies = jnp.asarray(profile(count, total, most, slope), jnp.int32)
    twos = (count - 1) // 2
    donor, receiver = tallies[1:1 + 2 * twos:2], tallies[2:2 + 2 * twos:2]
    room = jnp.minimum(donor - 1, most - receiver)
    shifted = jax.random.randint(jax.random.fold_in(key, 1), (twos,), 0, 1 << 20) % (room + 1)
    tallies = tallies.at[1:1 + 2 * twos:2].set(donor - shifted).at[2:2 + 2 * twos:2].set(receiver + shifted)
    return tallies[jax.random.permutation(jax.random.fold_in(key, 2), count)]


def bell_draw(stream_key, extent, scale, bound, shards=(), kind=jnp.bfloat16):
    drawn = scale * jax.random.normal(stream_key, extent, jnp.float32)
    if shards:
        drawn = drawn * block_levels(stream_key, extent, shards, -0.22, 0.18)
    return jnp.clip(drawn, -bound, bound).astype(kind)


def setup_inputs(seed: int = 0) -> dict:
    splits = jax.random.split(jax.random.key(seed), 22)
    tokens = bell_draw(splits[0], (SEQS, LENGTH, D), 1.0, 6.0, ((0, 4), (1, 8)))
    segments = jax.vmap(lambda own: jnp.searchsorted(jnp.cumsum(uneven(own, DOCS, LENGTH, LENGTH // 2, 0)), jnp.arange(LENGTH), side="right"))(jax.random.split(splits[1], SEQS)).reshape((SEQS, LENGTH)).astype(jnp.int32)
    cotangent = bell_draw(splits[2], (SEQS, LENGTH, D), 1.0, 6.0, ((0, 4), (1, 8)))
    mix_weight = bell_draw(splits[3], (D, 3 * D), D ** -0.5, 0.125, ((0, 32),), jnp.float32)
    mix_moment = bell_draw(splits[4], (D, 3 * D), (0.3 * TOKENS ** 0.5), 112.0, ((0, 32),), jnp.float32)
    mix_average = bell_draw(splits[5], (D, 3 * D), D ** -0.5, 0.125, ((0, 32),), jnp.float32)
    out_weight = bell_draw(splits[6], (D, D), (D // 8) ** -0.5, 0.375, ((0, 32),), jnp.float32)
    out_moment = bell_draw(splits[7], (D, D), (0.3 * TOKENS ** 0.5), 112.0, ((0, 32),), jnp.float32)
    out_average = bell_draw(splits[8], (D, D), (D // 8) ** -0.5, 0.375, ((0, 32),), jnp.float32)
    up_weight = bell_draw(splits[9], (D, FF), D ** -0.5, 0.125, ((0, 32),), jnp.float32)
    up_moment = bell_draw(splits[10], (D, FF), (0.3 * TOKENS ** 0.5), 112.0, ((0, 32),), jnp.float32)
    up_average = bell_draw(splits[11], (D, FF), D ** -0.5, 0.125, ((0, 32),), jnp.float32)
    down_weight = bell_draw(splits[12], (FF, D), FF ** -0.5, 0.0625, ((0, 32),), jnp.float32)
    down_moment = bell_draw(splits[13], (FF, D), (0.3 * TOKENS ** 0.5), 112.0, ((0, 32),), jnp.float32)
    down_average = bell_draw(splits[14], (FF, D), FF ** -0.5, 0.0625, ((0, 32),), jnp.float32)
    norm_gains = jnp.clip(1.0 + 0.18 * jax.random.normal(splits[15], (2, D), jnp.float32), 0.1, 1.9)
    gain_moment = bell_draw(splits[16], (2, D), (0.5 * TOKENS ** 0.5), 192.0, ((1, 32),), jnp.float32)
    gain_average = jnp.clip(1.0 + 0.18 * jax.random.normal(splits[17], (2, D), jnp.float32), 0.1, 1.9)
    biases = bell_draw(splits[18], (10, D), 0.5, 3.0, ((1, 32),), jnp.float32)
    bias_moment = bell_draw(splits[19], (10, D), (0.5 * TOKENS ** 0.5), 192.0, ((1, 32),), jnp.float32)
    bias_average = bell_draw(splits[20], (10, D), 0.5, 3.0, ((1, 32),), jnp.float32)
    return {"tokens": tokens, "segments": segments, "cotangent": cotangent, "mix_weight": mix_weight, "mix_moment": mix_moment, "mix_average": mix_average, "out_weight": out_weight, "out_moment": out_moment, "out_average": out_average, "up_weight": up_weight, "up_moment": up_moment, "up_average": up_average, "down_weight": down_weight, "down_moment": down_moment, "down_average": down_average, "norm_gains": norm_gains, "gain_moment": gain_moment, "gain_average": gain_average, "biases": biases, "bias_moment": bias_moment, "bias_average": bias_average}


@jax.custom_vjp
def low(v):
    return lax.optimization_barrier(v.astype(jnp.bfloat16)).astype(jnp.float32)

@jax.custom_vjp
def low_back(v):
    return v

def low_keep(v):
    return (low(v), None)

def low_pass(kept, grad):
    return (grad,)

def back_keep(v):
    return (v, None)

def back_low(kept, grad):
    return (low(grad),)
low.defvjp(low_keep, low_pass)
low_back.defvjp(back_keep, back_low)
highest = lax.Precision.HIGHEST
epsilon = 1e-05
mom_decay = 0.5
avg_decay = 0.5
base_rate = 0.02
vector_rate = 0.1

def layer_norm(values, gain_row, shift_row):
    centred = values - lax.optimization_barrier(jnp.mean(values, axis=-1, keepdims=True))
    spread = lax.optimization_barrier(jnp.mean(centred * centred, axis=-1, keepdims=True))
    return centred * lax.rsqrt(spread + epsilon) * gain_row + shift_row

def product(left, right):
    return jnp.dot(left, right, precision=highest, preferred_element_type=jnp.float32)

def head_slopes():
    return jnp.exp2(-8.0 * (jnp.arange(HEADS, dtype=jnp.float32) + 1.0) / HEADS)

@jax.checkpoint
def attend_block(row_start, queries, key_heads, values, documents):
    block_rows = min(512, LENGTH)
    score_scale = HD ** (-0.5)
    slopes = head_slopes()
    key_position = jnp.arange(LENGTH, dtype=jnp.int32)
    query_block = lax.dynamic_slice_in_dim(queries, row_start, block_rows)
    query_docs = lax.dynamic_slice_in_dim(documents, row_start, block_rows)
    query_position = row_start + jnp.arange(block_rows, dtype=jnp.int32)
    raw_scores = jnp.einsum('qhd,khd->hqk', query_block, key_heads, precision=highest)
    distance = (query_position[:, None] - key_position[None, :]).astype(jnp.float32)
    logits = low_back(raw_scores * score_scale - slopes[:, None, None] * distance)
    allowed = (key_position[None, :] <= query_position[:, None]) & (query_docs[:, None] == documents[None, :])
    logits = jnp.where(allowed[None], logits, -1000000000.0)
    weights = low(jax.nn.softmax(logits, axis=-1))
    return jnp.einsum('hqk,khd->qhd', weights, values, precision=highest)

def attend_sequence(operands):
    queries, key_heads, values, documents = operands
    block_rows = min(512, LENGTH)
    starts = jnp.arange(LENGTH // block_rows, dtype=jnp.int32) * block_rows
    blocks = lax.map(lambda row_start: attend_block(row_start, queries, key_heads, values, documents), starts)
    return blocks.reshape(LENGTH, HEADS, HD)

def forward(tokens, mix_weight, out_weight, up_weight, down_weight, norm_gains, biases, segments):
    mix_weight = low(mix_weight)
    out_weight = low(out_weight)
    up_weight = low(up_weight)
    down_weight = low(down_weight)
    norm_gains = low(norm_gains)
    biases = low(biases)
    row_count = SEQS * LENGTH
    row_values = tokens.reshape(row_count, D)
    normed = low(layer_norm(row_values, norm_gains[0], biases[0]))
    mix_bias = jnp.concatenate([biases[1], jnp.zeros((D,), jnp.float32), biases[2]])
    mixed_rows = low_back(low(product(normed, mix_weight) + mix_bias)).reshape(SEQS, LENGTH, 3, HEADS, HD)
    attended = lax.map(jax.checkpoint(attend_sequence), (mixed_rows[:, :, 0], mixed_rows[:, :, 1], mixed_rows[:, :, 2], segments))
    attended = low_back(low(attended.reshape(row_count, D)))
    hidden_in = row_values + low_back(product(attended, out_weight)) + biases[3]
    normed_two = low(layer_norm(hidden_in, norm_gains[1], biases[4]))
    pre_act = low_back(product(normed_two, up_weight) + biases[6:10].reshape(FF))
    activated = low(jax.nn.gelu(pre_act, approximate=False))
    result = hidden_in + low_back(product(activated, down_weight)) + biases[5]
    return result.reshape(SEQS, LENGTH, D)

def reference(tokens, segments, cotangent, mix_weight, mix_moment, mix_average, out_weight, out_moment, out_average, up_weight, up_moment, up_average, down_weight, down_moment, down_average, norm_gains, gain_moment, gain_average, biases, bias_moment, bias_average):
    weight_list = (mix_weight, out_weight, up_weight, down_weight, norm_gains, biases)
    moment_list = (mix_moment, out_moment, up_moment, down_moment, gain_moment, bias_moment)
    average_list = (mix_average, out_average, up_average, down_average, gain_average, bias_average)

    def run_layer(inputs, *weights):
        return forward(inputs, *weights, segments)
    result, pullback = jax.vjp(run_layer, tokens.astype(jnp.float32), *weight_list)
    gradients = pullback(cotangent.astype(jnp.float32))
    step_rate = base_rate / TOKENS ** 0.5
    vector_step = vector_rate / TOKENS ** 0.5
    rate_list = (step_rate, step_rate, step_rate, step_rate, vector_step, vector_step)
    results = [result.astype(jnp.bfloat16), gradients[0].astype(jnp.bfloat16)]
    for weight, moment, average, gradient, rate in zip(weight_list, moment_list, average_list, gradients[1:], rate_list):
        new_moment = mom_decay * moment + gradient
        new_weight = weight - rate * (gradient + mom_decay * new_moment)
        new_average = avg_decay * average + (1.0 - avg_decay) * new_weight
        results += [new_moment, new_weight, new_average]
    return (results[0], results[1], results[2], results[3], results[4], results[5], results[6], results[7], results[8], results[9], results[10], results[11], results[12], results[13], results[14], results[15], results[16], results[17], results[18], results[19])
```

```python
import functools
import math

import jax
import jax.numpy as jnp
from jax import lax
from jax.experimental import pallas as pl
from jax.experimental.pallas import tpu as pltpu
from jax.sharding import PartitionSpec as P

D = 2048
HEADS = 32
HD = 64
FF = 8192

epsilon = 1e-05
mom_decay = 0.5
avg_decay = 0.5
base_rate = 0.02
vector_rate = 0.1

BF16 = jnp.bfloat16
F32 = jnp.float32
MESH = pl.DeviceIdType.MESH


class Net:
    def __init__(self, send, recv, near):
        self.send, self.recv, self.near = send, recv, near
        self.used = self.near_used = 0
        self.later = []

    def take(self, count):
        first = self.used
        self.used += count
        return first

    def copy(self, slot, src, dst, dev):
        return pltpu.make_async_remote_copy(
            src_ref=src,
            dst_ref=dst,
            send_sem=self.send.at[slot],
            recv_sem=self.recv.at[slot],
            device_id=dev,
            device_id_type=MESH,
        )

    def local(self, src, dst):
        made = pltpu.make_async_copy(src, dst, self.near.at[self.near_used])
        self.near_used += 1
        made.start()
        return made


def when(cond, act):
    if cond is None:
        act()
    else:
        pl.when(cond)(act)


def greet(partners):
    barrier = pltpu.get_barrier_semaphore()
    for cond, dev in partners:
        when(
            cond,
            functools.partial(
                pl.semaphore_signal, barrier, inc=1, device_id=dev, device_id_type=MESH
            ),
        )
    count = sum(1 for cond, _ in partners if cond is None)
    for cond, _ in partners:
        if cond is not None:
            count = count + jnp.where(cond, 1, 0)
    pl.semaphore_wait(barrier, count)


class Roles:
    def __init__(self, axis, length, place, side, stride, pair):
        self.axis, self.length, self.p, self.q = axis, length, place, side
        self.stride, self.pair = stride, pair

    def index(self, p, q):
        return p * self.stride + q * self.pair

    def dev(self, p, q):
        return {self.axis: self.index(p, q)}

    def partners(self):
        return [
            (None, self.dev(self.p, 1 - self.q)),
            (self.p + 1 < self.length, self.dev(self.p + 1, self.q)),
            (self.p > 0, self.dev(self.p - 1, self.q)),
        ]


def line_of(axis):
    me, size = lax.axis_index(axis), lax.axis_size(axis)
    return Roles(axis, size // 2, me // 2, me % 2, 2, 1)


def both_of(axis):
    me, size = lax.axis_index(axis), lax.axis_size(axis)
    first = line_of(axis)
    if size != 4:
        return first, first
    return first, Roles(axis, 2, me % 2, me // 2, 1, 2)


def everyone(axis):
    me, size = lax.axis_index(axis), lax.axis_size(axis)
    return [(None, {axis: (me + o) % size}) for o in range(1, size)]


def gather(net, ro, src, place):
    n, p, q = ro.length, ro.p, ro.q
    right, left = net.take(n - 1), net.take(n - 1)
    over_r, over_l, over_own = net.take(n - 1), net.take(n - 1), net.take(1)
    other = ro.dev(p, 1 - q)
    at = lambda k: place(ro.index(k, q))
    across = lambda k: place(ro.index(k, 1 - q))
    ref = lambda j, k: src if j == 0 else at(k)
    go_right = lambda j: net.copy(right + j, ref(j, p - j), at(p - j), ro.dev(p + 1, q))
    go_left = lambda j: net.copy(left + j, ref(j, p + j), at(p + j), ro.dev(p - 1, q))
    pass_r = lambda j: net.copy(over_r + j - 1, at(p - j), at(p - j), other)
    pass_l = lambda j: net.copy(over_l + j - 1, at(p + j), at(p + j), other)
    own = net.copy(over_own, src, at(p), other)
    pl.when(p + 1 < n)(lambda: go_right(0).start())
    pl.when(p > 0)(lambda: go_left(0).start())
    own.start()
    yield
    for j in range(1, n):

        @pl.when(p - j >= 0)
        def _():
            net.copy(right + j - 1, at(p - j), at(p - j), other).wait_recv()
            if j < n - 1:
                pl.when(p + 1 < n)(lambda: go_right(j).start())
            pass_r(j).start()

        @pl.when(p + j < n)
        def _():
            net.copy(left + j - 1, at(p + j), at(p + j), other).wait_recv()
            if j < n - 1:
                pl.when(p > 0)(lambda: go_left(j).start())
            pass_l(j).start()

        yield
    net.copy(over_own, src, across(p), other).wait_recv()
    for j in range(1, n):

        @pl.when(p - j >= 0)
        def _():
            net.copy(over_r + j - 1, across(p - j), across(p - j), other).wait_recv()

        @pl.when(p + j < n)
        def _():
            net.copy(over_l + j - 1, across(p + j), across(p + j), other).wait_recv()

    def finish():
        own.wait_send()
        for j in range(n):
            if j < n - 1:
                pl.when((p - j >= 0) & (p + 1 < n))(lambda: go_right(j).wait_send())
                pl.when((p + j < n) & (p > 0))(lambda: go_left(j).wait_send())
            if j > 0:
                pl.when(p - j >= 0)(lambda: pass_r(j).wait_send())
                pl.when(p + j < n)(lambda: pass_l(j).wait_send())

    net.later.append(finish)


def add_rows(dst, srcs, step=16):
    def one(i, _):
        at = pl.ds(pl.multiple_of(i * step, step), step)
        total = srcs[0][at, :].astype(F32)
        for s in srcs[1:]:
            total = total + s[at, :].astype(F32)
        dst[at, :] = total.astype(dst.dtype)
        return 0

    lax.fori_loop(0, dst.shape[0] // step, one, 0)


def scatter_scratch(ro_length, rows, cols):
    return [pltpu.VMEM((ro_length, rows, cols), BF16)] + [
        pltpu.VMEM((ro_length - 1, rows, cols), BF16)
    ] * 4


def scatter(net, ro, part, result, room):
    sib, out_r, in_r, out_l, in_l = room
    n, p, q = ro.length, ro.p, ro.q
    right, left, pair = net.take(n - 1), net.take(n - 1), net.take(n)
    other = ro.dev(p, 1 - q)
    order = []
    for j in range(n):
        order += [d for d in (n - 1 - j, j) if d not in order]
    mine = lambda d: part(ro.index(d, q))
    swap = lambda d: net.copy(pair + d, part(ro.index(d, 1 - q)), sib.at[d], other)
    send_r = lambda j: net.copy(right + j, out_r.at[j], in_r.at[j], ro.dev(p + 1, q))
    send_l = lambda j: net.copy(left + j, out_l.at[j], in_l.at[j], ro.dev(p - 1, q))
    for d in order:
        swap(d).start()
    yield
    for j in range(n - 1):
        dr, dl = n - 1 - j, j

        @pl.when(p < dr)
        def _():
            swap(dr).wait_recv()

            @pl.when(p > 0)
            def _():
                send_r(j).wait_recv()
                add_rows(out_r.at[j], [mine(dr), sib.at[dr], in_r.at[j]])

            @pl.when(p == 0)
            def _():
                add_rows(out_r.at[j], [mine(dr), sib.at[dr]])

            send_r(j).start()

        @pl.when(p > dl)
        def _():
            swap(dl).wait_recv()

            @pl.when(p < n - 1)
            def _():
                send_l(j).wait_recv()
                add_rows(out_l.at[j], [mine(dl), sib.at[dl], in_l.at[j]])

            @pl.when(p == n - 1)
            def _():
                add_rows(out_l.at[j], [mine(dl), sib.at[dl]])

            send_l(j).start()

        yield
    from_r, from_l = n - 1 - p, p
    swap(p).wait_recv()

    @pl.when(p > 0)
    def _():
        send_r(from_r).wait_recv()

    @pl.when(p < n - 1)
    def _():
        send_l(from_l).wait_recv()

    @pl.when(p == 0)
    def _():
        add_rows(result, [mine(p), sib.at[p], in_l.at[from_l]])

    @pl.when(p == n - 1)
    def _():
        add_rows(result, [mine(p), sib.at[p], in_r.at[from_r]])

    if n > 2:

        @pl.when((p > 0) & (p < n - 1))
        def _():
            add_rows(result, [mine(p), sib.at[p], in_r.at[from_r], in_l.at[from_l]])

    def finish():
        for d in order:
            swap(d).wait_send()
        for j in range(n - 1):
            pl.when(p < n - 1 - j)(lambda: send_r(j).wait_send())
            pl.when(p > j)(lambda: send_l(j).wait_send())

    net.later.append(finish)


def exchange(net, axis, src, place):
    me, n = lax.axis_index(axis), lax.axis_size(axis)
    slots = net.take(n - 1)
    near = net.local(src(me), place(me))
    sent = []
    for o in range(1, n):
        to = (me + o) % n
        sent.append(net.copy(slots + o - 1, src(to), place(me), {axis: to}))
        sent[-1].start()
    yield
    near.wait()
    for o in range(1, n):
        at = (me + n - o) % n
        net.copy(slots + o - 1, src(at), place(at), {axis: at}).wait_recv()
    net.later.append(lambda: [s.wait_send() for s in sent])


def together(*gens):
    live = list(gens)
    while live:
        for g in list(live):
            try:
                next(g)
            except StopIteration:
                live.remove(g)
        if live:
            yield


def then(first, makers):
    yield from first
    yield from together(*[m() for m in makers])


def run(net, *gens):
    for _ in together(*gens):
        pass
    for act in net.later:
        act()


VM = pl.BlockSpec(memory_space=pltpu.VMEM)
HB = pl.BlockSpec(memory_space=pl.ANY)


def comm_call(slots, kernel, cid, ins, in_specs, outs, out_specs, room):
    return pl.pallas_call(
        kernel,
        out_shape=[jax.ShapeDtypeStruct(*o) for o in outs],
        in_specs=in_specs,
        out_specs=out_specs,
        scratch_shapes=[
            pltpu.SemaphoreType.DMA((slots,)),
            pltpu.SemaphoreType.DMA((slots,)),
            pltpu.SemaphoreType.DMA((8,)),
        ]
        + room,
        compiler_params=pltpu.CompilerParams(
            collective_id=cid, has_side_effects=True, vmem_limit_bytes=56 << 20
        ),
    )(*ins)


def pair_masks():
    lane = lax.broadcasted_iota(jnp.int32, (1, 2 * HD), 1)
    return [lane < HD, lane >= HD]


def block_scores(key_rows, query_block, start_row, first, slope):
    count, width = key_rows.shape[0], query_block.shape[0]
    raw = lax.dot_general(
        key_rows, query_block, (((1,), (1,)), ((), ())), preferred_element_type=F32
    )
    key_at = lax.broadcasted_iota(jnp.int32, (count, width), 0)
    query_at = lax.broadcasted_iota(jnp.int32, (1, width), 1) + first
    scores = raw - slope * (query_at - key_at).astype(F32)
    allowed = (key_at <= query_at) & (key_at >= start_row)
    return jnp.where(allowed, scores, -1e30)


def attend_kernel(block, slopes_ref, start_ref, q_ref, k_ref, v_ref, out_ref, lse_ref):
    length = q_ref.shape[0]
    pair = pl.program_id(0)
    for half, mask in enumerate(pair_masks()):
        keys = jnp.where(mask, k_ref[...], 0)
        turned = jnp.where(mask, v_ref[...], 0).T
        slope = slopes_ref[2 * pair + half]
        for first in range(0, length, block):
            here, upto = slice(first, first + block), first + block
            query_block = q_ref[here, :] * BF16(HD**-0.5)
            scores = block_scores(
                keys[:upto], query_block, start_ref[:, here], first, slope
            )
            top = jnp.max(scores, axis=0, keepdims=True)
            weights = jnp.exp(scores - top)
            total = jnp.sum(weights, axis=0, keepdims=True)
            lse_ref[0, half : half + 1, here] = top + jnp.log(total)
            probs = (weights * (1.0 / total)).astype(BF16)
            got = jnp.dot(turned[:, :upto], probs, preferred_element_type=F32).T
            if half == 0:
                out_ref[here, :] = got.astype(BF16)
            else:
                out_ref[here, :] = out_ref[here, :] + got.astype(BF16)


def attend_back_kernel(
    block, slopes_ref, start_ref, q_ref, k_ref, v_ref, o_ref, g_ref, lse_ref, dq_ref, dk_ref, dv_ref, dk, dv
):
    length = q_ref.shape[0]
    pair = pl.program_id(0)
    dk[...] = jnp.zeros_like(dk)
    dv[...] = jnp.zeros_like(dv)
    masks = pair_masks()
    for half, mask in enumerate(masks):
        keys = jnp.where(mask, k_ref[...], 0)
        values = jnp.where(mask, v_ref[...], 0)
        turned = keys.T * BF16(HD**-0.5)
        slope = slopes_ref[2 * pair + half]
        for first in range(0, length, block):
            here, upto = slice(first, first + block), first + block
            query_block = jnp.where(mask, q_ref[here, :], 0) * BF16(HD**-0.5)
            grad_block = jnp.where(mask, g_ref[here, :], 0)
            product = o_ref[here, :].astype(F32) * grad_block.astype(F32)
            delta = jnp.sum(product.T, axis=0, keepdims=True)
            scores = block_scores(
                keys[:upto], query_block, start_ref[:, here], first, slope
            )
            probs = jnp.exp(scores - lse_ref[0, half : half + 1, here])
            prob_grad = lax.dot_general(
                values[:upto], grad_block, (((1,), (1,)), ((), ())), preferred_element_type=F32
            )
            score_grad = (probs * (prob_grad - delta)).astype(BF16)
            dv[:upto, :] += jnp.dot(
                probs.astype(BF16), grad_block, preferred_element_type=F32
            )
            dk[:upto, :] += jnp.dot(score_grad, query_block, preferred_element_type=F32)
            got = jnp.dot(turned[:, :upto], score_grad, preferred_element_type=F32).T
            if half == 0:
                dq_ref[here, :] = got.astype(BF16)
            else:
                dq_ref[here, :] = dq_ref[here, :] + got.astype(BF16)
    dk_ref[...] = dk[...].astype(BF16)
    dv_ref[...] = dv[...].astype(BF16)


def attend_specs(length, pairs):
    column = lambda k: pl.BlockSpec((length, 2 * HD), lambda i, k=k: (0, k * pairs + i))
    fixed = [
        pl.BlockSpec(memory_space=pltpu.SMEM),
        pl.BlockSpec((1, length), lambda i: (0, 0)),
    ]
    lse = pl.BlockSpec((1, 2, length), lambda i: (i, 0, 0))
    return column, fixed, lse


ATTEND = pltpu.CompilerParams(vmem_limit_bytes=48 << 20)


def attend(mixed, start, slopes):
    length, pairs = mixed.shape[0], mixed.shape[1] // (6 * HD)
    column, fixed, lse = attend_specs(length, pairs)
    return pl.pallas_call(
        functools.partial(attend_kernel, min(256, length)),
        grid=(pairs,),
        in_specs=fixed + [column(0), column(1), column(2)],
        out_specs=[column(0), lse],
        out_shape=[
            jax.ShapeDtypeStruct((length, pairs * 2 * HD), BF16),
            jax.ShapeDtypeStruct((pairs, 2, length), F32),
        ],
        compiler_params=ATTEND,
    )(slopes, start, mixed, mixed, mixed)


def attend_back(mixed, attended, upstream, log_sums, start, slopes):
    length, pairs = mixed.shape[0], mixed.shape[1] // (6 * HD)
    column, fixed, lse = attend_specs(length, pairs)
    wide = jax.ShapeDtypeStruct((length, pairs * 2 * HD), BF16)
    return pl.pallas_call(
        functools.partial(attend_back_kernel, min(256, length)),
        grid=(pairs,),
        in_specs=fixed + [column(0), column(1), column(2), column(0), column(0), lse],
        out_specs=[column(0)] * 3,
        out_shape=[wide] * 3,
        scratch_shapes=[pltpu.VMEM((length, 2 * HD), F32)] * 2,
        compiler_params=ATTEND,
    )(slopes, start, mixed, mixed, mixed, attended, upstream, log_sums)


def layer_norm(values, gain_row, shift_row):
    centred = values - jnp.mean(values, axis=-1, keepdims=True)
    spread = jnp.mean(centred * centred, axis=-1, keepdims=True)
    return centred * lax.rsqrt(spread + epsilon) * gain_row + shift_row


def gelu_exact(values):
    return jax.nn.gelu(values, approximate=False)


def body(
    tokens,
    segments,
    cotangent,
    mix_weight,
    mix_moment,
    mix_average,
    out_weight,
    out_moment,
    out_average,
    up_weight,
    up_moment,
    up_average,
    down_weight,
    down_moment,
    down_average,
    norm_gains,
    gain_moment,
    gain_average,
    biases,
    bias_moment,
    bias_average,
):
    S, F = lax.axis_size("seq"), lax.axis_size("fsdp")
    owners = S * F
    s_at = lax.axis_index("seq")
    T = tokens.shape[1]
    L = T * S
    R = D // owners
    RD = FF // owners
    W = D // S
    U = FF // S
    heads = HEADS // S
    slots = 12 * max(S, F)
    call = functools.partial(comm_call, slots)

    head_ids = s_at * heads + jnp.arange(heads, dtype=jnp.int32) + 1
    slopes = jnp.exp2(-8.0 * head_ids.astype(F32) / HEADS)
    documents = segments[0]
    start = jnp.sum(documents[:, None] < documents[None, :], axis=0, dtype=jnp.int32)[None]

    mix_low = mix_weight.astype(BF16).reshape(R, 3, S, W).transpose(2, 0, 1, 3).reshape(S, R, 3 * W)
    up_low = up_weight.astype(BF16).reshape(R, S, U).transpose(1, 0, 2)
    out_low = out_weight.astype(BF16)
    down_low = down_weight.astype(BF16)
    small = jnp.concatenate([norm_gains, biases], axis=0).astype(BF16).astype(F32)
    small = jnp.pad(small, ((0, 4), (0, 128 - R)))

    def first_kernel(tok, mix, out, vec, tok_f, mix_f, out_f, vec_f, send, recv, near):
        net = Net(send, recv, near)
        seq, sides = line_of("seq"), both_of("fsdp")
        s, f = lax.axis_index("seq"), lax.axis_index("fsdp")
        greet(everyone("seq") + everyone("fsdp"))
        owned = [
            net.local(tok, tok_f.at[s]),
            net.local(out, out_f.at[f]),
        ]
        vec_own = net.local(vec, vec_f.at[s, f])

        def mix_half(k):
            at = pl.ds(k * (S // 2), S // 2)
            return lambda: gather(net, sides[k], mix_f.at[at, f], lambda i: mix_f.at[at, i])

        def out_half(k):
            at = pl.ds(k * (D // 2), D // 2)
            return gather(net, sides[k], out.at[:, at], lambda i: out_f.at[i, :, at])

        def vec_next():
            vec_own.wait()
            return gather(net, sides[0], vec_f.at[:, f], lambda i: vec_f.at[:, i])

        run(
            net,
            then(
                exchange(net, "seq", lambda i: mix.at[i], lambda i: mix_f.at[i, f]),
                [mix_half(0), mix_half(1)],
            ),
            then(gather(net, seq, vec, lambda i: vec_f.at[i, f]), [vec_next]),
            out_half(0),
            out_half(1),
            gather(net, seq, tok, lambda i: tok_f.at[i]),
        )
        for o in owned:
            o.wait()

    tok_full, mix_full, out_full, vec_full = call(
        first_kernel,
        1,
        (tokens[0], mix_low, out_low, small),
        [HB] * 4,
        [
            ((S, T, D), BF16),
            ((S, F, R, 3 * W), BF16),
            ((F, R, D), BF16),
            ((S, F, 16, 128), F32),
        ],
        [HB] * 4,
        [],
    )
    vectors = vec_full[:, :, :12, :R].transpose(2, 0, 1, 3).reshape(12, D)
    gain_values, bias_values = vectors[:2], vectors[2:]
    mine = lambda row, width: lax.dynamic_slice_in_dim(row.reshape(-1), s_at * width, width)
    mix_own = mix_full.reshape(D, 3 * W)
    out_own = out_full.reshape(W, D)

    normed = layer_norm(
        tok_full.reshape(L, D).astype(F32), gain_values[0], bias_values[0]
    ).astype(BF16)
    mix_bias = jnp.concatenate(
        [mine(bias_values[1], W), jnp.zeros((W,), F32), mine(bias_values[2], W)]
    )
    mixed = (jnp.dot(normed, mix_own, preferred_element_type=F32) + mix_bias).astype(BF16)
    attended, log_sums = attend(mixed, start, slopes)
    out_part = jnp.dot(attended, out_own, preferred_element_type=F32).astype(BF16)

    def second_kernel(part, cot, up, down, total, cot_f, up_r, down_f, send, recv, near, *room):
        net = Net(send, recv, near)
        seq, sides = line_of("seq"), both_of("fsdp")
        s, f = lax.axis_index("seq"), lax.axis_index("fsdp")
        greet(everyone("seq") + everyone("fsdp"))
        owned = [net.local(cot, cot_f.at[s]), net.local(down, down_f.at[f])]

        def down_half(k):
            at = pl.ds(k * (RD // 2), RD // 2)
            return gather(net, sides[k], down.at[at], lambda i: down_f.at[i, at])

        run(
            net,
            scatter(net, seq, lambda i: part.at[i], total, room),
            down_half(0),
            down_half(1),
            gather(net, seq, cot, lambda i: cot_f.at[i]),
            exchange(net, "seq", lambda i: up.at[i], lambda i: up_r.at[i]),
        )
        for o in owned:
            o.wait()

    attn_sum, cot_full, up_mid, down_full = call(
        second_kernel,
        2,
        (out_part.reshape(S, T, D), cotangent[0], up_low, down_low),
        [VM, HB, HB, HB],
        [((T, D), F32), ((S, T, D), BF16), ((S, R, U), BF16), ((F, RD, D), BF16)],
        [VM, HB, HB, HB],
        scatter_scratch(S // 2, T, D),
    )
    row_values = tokens[0].astype(F32)
    hidden_in = row_values + attn_sum + bias_values[3]
    normed_two = layer_norm(hidden_in, gain_values[1], bias_values[4]).astype(BF16)

    def third_kernel(rows, up, rows_f, up_f, send, recv, near):
        net = Net(send, recv, near)
        seq, sides = line_of("seq"), both_of("fsdp")
        s, f = lax.axis_index("seq"), lax.axis_index("fsdp")
        greet(seq.partners() + everyone("fsdp"))
        owned = [net.local(rows, rows_f.at[s]), net.local(up, up_f.at[:, f])]

        def up_half(k):
            at = pl.ds(k * (S // 2), S // 2)
            return gather(net, sides[k], up.at[at], lambda i: up_f.at[at, i])

        run(
            net,
            up_half(0),
            up_half(1),
            gather(net, seq, rows, lambda i: rows_f.at[i]),
        )
        for o in owned:
            o.wait()

    two_full, up_full = call(
        third_kernel,
        3,
        (normed_two, up_mid),
        [HB, HB],
        [((S, T, D), BF16), ((S, F, R, U), BF16)],
        [HB, HB],
        [],
    )
    two_full = two_full.reshape(L, D)
    cot_full = cot_full.reshape(L, D)
    up_own = up_full.reshape(D, U)
    down_own = down_full.reshape(U, D)
    pre_act = jnp.dot(two_full, up_own, preferred_element_type=F32) + mine(bias_values[6:10], U)
    activated = gelu_exact(pre_act).astype(BF16)
    result_part = jnp.dot(activated, down_own, preferred_element_type=F32).astype(BF16)
    act_grad = jnp.einsum("td,fd->tf", cot_full, down_own, preferred_element_type=F32)
    pre_grad = jax.vjp(gelu_exact, pre_act)[1](act_grad)[0].astype(BF16)
    two_grad_part = jnp.einsum("tf,cf->tc", pre_grad, up_own, preferred_element_type=F32)
    down_part = jnp.einsum("tf,td->fd", activated, cot_full, preferred_element_type=F32)
    up_part = jnp.einsum("tc,tf->cf", two_full, pre_grad, preferred_element_type=F32)

    def fourth_kernel(part, grad, total, share, send, recv, near, *room):
        net = Net(send, recv, near)
        seq, sides = line_of("seq"), both_of("fsdp")
        greet(seq.partners() + everyone("fsdp"))

        def half(k):
            at = pl.ds(k * (D // 2), D // 2)
            return scatter(
                net, sides[k], lambda i: grad.at[i, :, at], share.at[:, at], room[5 + 5 * k : 10 + 5 * k]
            )

        run(net, scatter(net, seq, lambda i: part.at[i], total, room[:5]), half(0), half(1))

    two_grad, down_share = call(
        fourth_kernel,
        4,
        (two_grad_part.astype(BF16).reshape(S, T, D), down_part.astype(BF16).reshape(F, RD, D)),
        [VM, VM],
        [((T, D), F32), ((RD, D), F32)],
        [VM, VM],
        scatter_scratch(S // 2, T, D) + 2 * scatter_scratch(F // 2, RD, D // 2),
    )
    upstream_float = cotangent[0].astype(F32)
    second_pull = jax.vjp(layer_norm, hidden_in, gain_values[1], bias_values[4])[1]
    hidden_part, gain_two_gradient, shift_two_gradient = second_pull(two_grad)
    hidden_gradient = upstream_float + hidden_part
    hidden_low = hidden_gradient.astype(BF16)

    def fifth_kernel(rows, part, grad, rows_f, total, share, send, recv, near, *room):
        net = Net(send, recv, near)
        seq, sides = line_of("seq"), both_of("fsdp")
        s = lax.axis_index("seq")
        greet(seq.partners() + everyone("fsdp"))
        own = net.local(rows, rows_f.at[s])

        def half(k):
            at = pl.ds(k * (U // 2), U // 2)
            return scatter(
                net, sides[k], lambda i: grad.at[i, :, at], share.at[:, at], room[5 + 5 * k : 10 + 5 * k]
            )

        run(
            net,
            gather(net, seq, rows, lambda i: rows_f.at[i]),
            scatter(net, seq, lambda i: part.at[i], total, room[:5]),
            half(0),
            half(1),
        )
        own.wait()

    hidden_full, result_sum, up_mid_grad = call(
        fifth_kernel,
        5,
        (
            hidden_low,
            result_part.reshape(S, T, D),
            up_part.astype(BF16).reshape(S, F, R, U).transpose(1, 0, 2, 3).reshape(F, S * R, U),
        ),
        [HB, VM, VM],
        [((S, T, D), BF16), ((T, D), F32), ((S * R, U), BF16)],
        [HB, VM, VM],
        scatter_scratch(S // 2, T, D) + 2 * scatter_scratch(F // 2, S * R, U // 2),
    )
    output = (hidden_in + result_sum + bias_values[5]).astype(BF16)[None]
    hidden_full = hidden_full.reshape(L, D)
    attn_grad = jnp.einsum(
        "td,cd->tc", hidden_full, out_own, preferred_element_type=F32
    ).astype(BF16)
    query_grad, key_grad, value_grad = attend_back(
        mixed, attended, attn_grad, log_sums, start, slopes
    )
    mixed_grad = jnp.concatenate([query_grad, key_grad, value_grad], axis=1)
    one_grad_part = jnp.einsum("te,ce->tc", mixed_grad, mix_own, preferred_element_type=F32)
    out_grad = jnp.einsum("tc,td->cd", attended, hidden_full, preferred_element_type=F32)
    mix_grad = jnp.einsum("tc,te->ce", normed, mixed_grad, preferred_element_type=F32)

    def sixth_kernel(
        part, mix, out, up, total, mix_s, out_s, up_s, send, recv, near, mix_r, *room
    ):
        net = Net(send, recv, near)
        seq, sides = line_of("seq"), both_of("fsdp")
        greet(everyone("seq") + everyone("fsdp"))
        C = S * R // 2

        def mix_half(k):
            at = pl.ds(k * C, C)
            return scatter(
                net, sides[k], lambda i: mix.at[i, at], mix_r.at[at], room[5 + 5 * k : 10 + 5 * k]
            )

        def out_half(k):
            at = pl.ds(k * (D // 2), D // 2)
            return scatter(
                net, sides[k], lambda i: out.at[i, :, at], out_s.at[:, at], room[15 + 5 * k : 20 + 5 * k]
            )

        run(
            net,
            then(
                together(mix_half(0), mix_half(1)),
                [
                    lambda: exchange(
                        net, "seq", lambda i: mix_r.at[pl.ds(i * R, R)], lambda i: mix_s.at[i]
                    )
                ],
            ),
            scatter(net, seq, lambda i: part.at[i], total, room[:5]),
            exchange(net, "seq", lambda i: up.at[i], lambda i: up_s.at[i]),
            out_half(0),
            out_half(1),
        )

    one_grad, mix_share, out_share, up_share = call(
        sixth_kernel,
        6,
        (
            one_grad_part.astype(BF16).reshape(S, T, D),
            mix_grad.astype(BF16)
            .reshape(S, F, R, 3 * W)
            .transpose(1, 0, 2, 3)
            .reshape(F, S * R, 3 * W),
            out_grad.astype(BF16).reshape(F, R, D),
            up_mid_grad.reshape(S, R, U),
        ),
        [VM, VM, VM, HB],
        [((T, D), F32), ((S, R, 3 * W), BF16), ((R, D), F32), ((S, R, U), BF16)],
        [VM, HB, VM, HB],
        [pltpu.VMEM((S * R, 3 * W), BF16)]
        + scatter_scratch(S // 2, T, D)
        + 2 * scatter_scratch(F // 2, S * R // 2, 3 * W)
        + 2 * scatter_scratch(F // 2, R, D // 2),
    )
    first_pull = jax.vjp(layer_norm, row_values, gain_values[0], bias_values[0])[1]
    rows_part, gain_one_gradient, shift_one_gradient = first_pull(one_grad)
    tokens_grad = (hidden_gradient + rows_part).astype(BF16)[None]

    def spread(row, count):
        return lax.dynamic_update_slice_in_dim(
            jnp.zeros((count * S * row.shape[0] // count,), F32), row, s_at * row.shape[0], 0
        ).reshape(count, D)

    mixed_sum = jnp.sum(mixed_grad.astype(F32), axis=0)
    small_gradient = jnp.concatenate(
        [
            gain_one_gradient[None],
            gain_two_gradient[None],
            shift_one_gradient[None],
            spread(mixed_sum[:W], 1),
            spread(mixed_sum[2 * W :], 1),
            jnp.sum(hidden_gradient, axis=0)[None],
            shift_two_gradient[None],
            jnp.sum(upstream_float, axis=0)[None],
            spread(jnp.sum(pre_grad.astype(F32), axis=0), 4),
        ],
        axis=0,
    )
    small_gradient = jnp.pad(
        small_gradient.reshape(12, S, F, R).transpose(1, 2, 0, 3),
        ((0, 0), (0, 0), (0, 4), (0, 128 - R)),
    )

    def last_kernel(vec, total, send, recv, near, got, mid, got_two):
        net = Net(send, recv, near)
        greet(everyone("seq") + everyone("fsdp"))
        for _ in exchange(net, "seq", lambda i: vec.at[i], lambda i: got.at[i]):
            pass
        mid[...] = jnp.sum(got[...], axis=0)
        for _ in exchange(net, "fsdp", lambda i: mid.at[i], lambda i: got_two.at[i]):
            pass
        total[...] = jnp.sum(got_two[...], axis=0)
        run(net)

    (small_share,) = call(
        last_kernel,
        7,
        (small_gradient,),
        [VM],
        [((16, 128), F32)],
        [VM],
        [
            pltpu.VMEM((S, F, 16, 128), F32),
            pltpu.VMEM((F, 16, 128), F32),
            pltpu.VMEM((F, 16, 128), F32),
        ],
    )
    mix_final = mix_share.astype(F32).reshape(S, R, 3, W).transpose(1, 2, 0, 3).reshape(R, 3 * D)
    up_final = up_share.astype(F32).transpose(1, 0, 2).reshape(R, FF)
    step_rate = base_rate / math.sqrt(owners * T)
    vector_step = vector_rate / math.sqrt(owners * T)
    rate_list = (step_rate, step_rate, step_rate, step_rate, vector_step, vector_step)
    masters = (mix_weight, out_weight, up_weight, down_weight, norm_gains, biases)
    shares = (mix_final, out_share, up_final, down_share, small_share[:2, :R], small_share[2:12, :R])
    moments = (mix_moment, out_moment, up_moment, down_moment, gain_moment, bias_moment)
    averages = (mix_average, out_average, up_average, down_average, gain_average, bias_average)
    updated = []
    for master, moment, average, share, rate in zip(masters, moments, averages, shares, rate_list):
        new_moment = mom_decay * moment + share
        new_weight = master - rate * (share + mom_decay * new_moment)
        new_average = avg_decay * average + (1.0 - avg_decay) * new_weight
        updated += [new_moment, new_weight, new_average]
    return (output, tokens_grad, *updated)


def solution(mesh):
    rows = P("fsdp", "seq", None)
    param = P(("seq", "fsdp"), None)
    vector = P(None, ("seq", "fsdp"))
    return jax.shard_map(
        body,
        mesh=mesh,
        in_specs=(rows, P("fsdp", None), rows) + (param,) * 12 + (vector,) * 6,
        out_specs=(rows, rows) + (param,) * 12 + (vector,) * 6,
        check_vma=False,
    )
```

```python
import functools
import heapq
import math

import jax
import jax.numpy as jnp
from jax import lax
from jax.experimental import pallas as pl
from jax.experimental.pallas import tpu as pltpu
from jax.sharding import PartitionSpec as P

D = 2048
HEADS = 32
HD = 64
FF = 8192

epsilon = 1e-05
mom_decay = 0.5
avg_decay = 0.5
base_rate = 0.02
vector_rate = 0.1

BF16 = jnp.bfloat16
F32 = jnp.float32
MESH = pl.DeviceIdType.MESH


class Net:
    def __init__(self, send, recv, near):
        self.send, self.recv, self.near = send, recv, near
        self.used = self.near_used = 0
        self.later = []

    def take(self, count):
        first = self.used
        self.used += count
        return first

    def copy(self, slot, src, dst, dev):
        return pltpu.make_async_remote_copy(
            src_ref=src,
            dst_ref=dst,
            send_sem=self.send.at[slot],
            recv_sem=self.recv.at[slot],
            device_id=dev,
            device_id_type=MESH,
        )

    def local(self, src, dst):
        made = pltpu.make_async_copy(src, dst, self.near.at[self.near_used])
        self.near_used += 1
        made.start()
        return made


def when(cond, act):
    if cond is None:
        act()
    else:
        pl.when(cond)(act)


def greet(partners):
    barrier = pltpu.get_barrier_semaphore()
    for cond, dev in partners:
        when(
            cond,
            functools.partial(
                pl.semaphore_signal, barrier, inc=1, device_id=dev, device_id_type=MESH
            ),
        )
    count = sum(1 for cond, _ in partners if cond is None)
    for cond, _ in partners:
        if cond is not None:
            count = count + jnp.where(cond, 1, 0)
    pl.semaphore_wait(barrier, count)


class Roles:
    def __init__(self, axis, length, place, side, stride, pair):
        self.axis, self.length, self.p, self.q = axis, length, place, side
        self.stride, self.pair = stride, pair

    def index(self, p, q):
        return p * self.stride + q * self.pair

    def dev(self, p, q):
        return {self.axis: self.index(p, q)}

    def partners(self):
        return [
            (None, self.dev(self.p, 1 - self.q)),
            (self.p + 1 < self.length, self.dev(self.p + 1, self.q)),
            (self.p > 0, self.dev(self.p - 1, self.q)),
        ]


def line_of(axis):
    me, size = lax.axis_index(axis), lax.axis_size(axis)
    return Roles(axis, size // 2, me // 2, me % 2, 2, 1)


def both_of(axis):
    me, size = lax.axis_index(axis), lax.axis_size(axis)
    first = line_of(axis)
    if size != 4:
        return first, first
    return first, Roles(axis, 2, me % 2, me // 2, 1, 2)


def everyone(axis):
    me, size = lax.axis_index(axis), lax.axis_size(axis)
    return [(None, {axis: (me + o) % size}) for o in range(1, size)]


def gather(net, ro, src, place, at_us=0.0, hop=11.0, over=1.0, hold=False):
    n, p, q = ro.length, ro.p, ro.q
    right, left = net.take(n - 1), net.take(n - 1)
    over_r, over_l, over_own = net.take(n - 1), net.take(n - 1), net.take(1)
    other = ro.dev(p, 1 - q)
    if hold:
        yield at_us
    at = lambda k: place(ro.index(k, q))
    across = lambda k: place(ro.index(k, 1 - q))
    ref = lambda j, k: src if j == 0 else at(k)
    go_right = lambda j: net.copy(right + j, ref(j, p - j), at(p - j), ro.dev(p + 1, q))
    go_left = lambda j: net.copy(left + j, ref(j, p + j), at(p + j), ro.dev(p - 1, q))
    pass_r = lambda j: net.copy(over_r + j - 1, at(p - j), at(p - j), other)
    pass_l = lambda j: net.copy(over_l + j - 1, at(p + j), at(p + j), other)
    own = net.copy(over_own, src, at(p), other)
    pl.when(p + 1 < n)(lambda: go_right(0).start())
    pl.when(p > 0)(lambda: go_left(0).start())
    own.start()
    for j in range(1, n):
        yield at_us + hop * j

        @pl.when(p - j >= 0)
        def _():
            net.copy(right + j - 1, at(p - j), at(p - j), other).wait_recv()
            if j < n - 1:
                pl.when(p + 1 < n)(lambda: go_right(j).start())
            pass_r(j).start()

        @pl.when(p + j < n)
        def _():
            net.copy(left + j - 1, at(p + j), at(p + j), other).wait_recv()
            if j < n - 1:
                pl.when(p > 0)(lambda: go_left(j).start())
            pass_l(j).start()

    yield at_us + hop * (n - 1) + over
    net.copy(over_own, src, across(p), other).wait_recv()
    for j in range(1, n):

        @pl.when(p - j >= 0)
        def _():
            net.copy(over_r + j - 1, across(p - j), across(p - j), other).wait_recv()

        @pl.when(p + j < n)
        def _():
            net.copy(over_l + j - 1, across(p + j), across(p + j), other).wait_recv()

    def finish():
        own.wait_send()
        for j in range(n):
            if j < n - 1:
                pl.when((p - j >= 0) & (p + 1 < n))(lambda: go_right(j).wait_send())
                pl.when((p + j < n) & (p > 0))(lambda: go_left(j).wait_send())
            if j > 0:
                pl.when(p - j >= 0)(lambda: pass_r(j).wait_send())
                pl.when(p + j < n)(lambda: pass_l(j).wait_send())

    net.later.append(finish)


def add_rows(dst, srcs, step=16):
    def one(i, _):
        at = pl.ds(pl.multiple_of(i * step, step), step)
        total = srcs[0][at, :].astype(F32)
        for s in srcs[1:]:
            total = total + s[at, :].astype(F32)
        dst[at, :] = total.astype(dst.dtype)
        return 0

    if len(dst.shape) == 3:

        def layer(k, _):
            add_rows(dst.at[k], [s.at[k] for s in srcs], step)
            return 0

        lax.fori_loop(0, dst.shape[0], layer, 0)
    else:
        lax.fori_loop(0, dst.shape[0] // step, one, 0)


def scatter_scratch(ro_length, *shape):
    return [pltpu.VMEM((ro_length, *shape), BF16)] + [
        pltpu.VMEM((ro_length - 1, *shape), BF16)
    ] * 4


def scatter(net, ro, part, result, room, at_us=0.0, first=2.0, hop=11.0, hold=False):
    sib, out_r, in_r, out_l, in_l = room
    n, p, q = ro.length, ro.p, ro.q
    right, left, pair = net.take(n - 1), net.take(n - 1), net.take(n)
    other = ro.dev(p, 1 - q)
    order = []
    for j in range(n):
        order += [d for d in (n - 1 - j, j) if d not in order]
    mine = lambda d: part(ro.index(d, q))
    swap = lambda d: net.copy(pair + d, part(ro.index(d, 1 - q)), sib.at[d], other)
    send_r = lambda j: net.copy(right + j, out_r.at[j], in_r.at[j], ro.dev(p + 1, q))
    send_l = lambda j: net.copy(left + j, out_l.at[j], in_l.at[j], ro.dev(p - 1, q))
    if hold:
        yield at_us
    if n == 2:
        swap(1 - p).start()
        swap(p).start()
    else:
        for d in order:
            swap(d).start()
    for j in range(n - 1):
        yield at_us + first + hop * j
        dr, dl = n - 1 - j, j

        @pl.when(p < dr)
        def _():
            swap(dr).wait_recv()

            @pl.when(p > 0)
            def _():
                send_r(j).wait_recv()
                add_rows(out_r.at[j], [mine(dr), sib.at[dr], in_r.at[j]])

            @pl.when(p == 0)
            def _():
                add_rows(out_r.at[j], [mine(dr), sib.at[dr]])
                if j > 0:
                    send_r(j - 1).wait_send()

            send_r(j).start()

        @pl.when(p > dl)
        def _():
            swap(dl).wait_recv()

            @pl.when(p < n - 1)
            def _():
                send_l(j).wait_recv()
                add_rows(out_l.at[j], [mine(dl), sib.at[dl], in_l.at[j]])

            @pl.when(p == n - 1)
            def _():
                add_rows(out_l.at[j], [mine(dl), sib.at[dl]])
                if j > 0:
                    send_l(j - 1).wait_send()

            send_l(j).start()

    yield at_us + first + hop * (n - 1)
    from_r, from_l = n - 1 - p, p
    swap(p).wait_recv()

    @pl.when(p > 0)
    def _():
        send_r(from_r).wait_recv()

    @pl.when(p < n - 1)
    def _():
        send_l(from_l).wait_recv()

    @pl.when(p == 0)
    def _():
        add_rows(result, [mine(p), sib.at[p], in_l.at[from_l]])

    @pl.when(p == n - 1)
    def _():
        add_rows(result, [mine(p), sib.at[p], in_r.at[from_r]])

    if n > 2:

        @pl.when((p > 0) & (p < n - 1))
        def _():
            add_rows(result, [mine(p), sib.at[p], in_r.at[from_r], in_l.at[from_l]])

    def finish():
        for d in order:
            swap(d).wait_send()
        for j in range(n - 1):
            last = j == n - 2
            pl.when((p < n - 1 - j) & ((p > 0) | last))(lambda: send_r(j).wait_send())
            pl.when((p > j) & ((p < n - 1) | last))(lambda: send_l(j).wait_send())

    net.later.append(finish)


def exchange(net, axis, src, place, at_us=0.0, last=15.0, hold=False):
    me, n = lax.axis_index(axis), lax.axis_size(axis)
    slots = net.take(n - 1)
    if hold:
        yield at_us
    near = net.local(src(me), place(me))
    sent = []
    for o in range(1, n):
        to = (me + o) % n
        sent.append(net.copy(slots + o - 1, src(to), place(me), {axis: to}))
        sent[-1].start()
    yield at_us + last
    near.wait()
    for o in range(1, n):
        at = (me + n - o) % n
        net.copy(slots + o - 1, src(at), place(at), {axis: at}).wait_recv()
    net.later.append(lambda: [s.wait_send() for s in sent])


def run(net, *gens):
    waiting = []
    for order, g in enumerate(gens):
        heapq.heappush(waiting, (0.0, order, g))
    while waiting:
        now, order, g = heapq.heappop(waiting)
        step = next(g, None)
        if step is not None:
            heapq.heappush(waiting, (max(step, now), order, g))
    for act in net.later:
        act()


def merge(gens):
    steps = [next(g, None) for g in gens]
    while any(s is not None for s in steps):
        at, k = min((s, i) for i, s in enumerate(steps) if s is not None)
        yield at
        steps[k] = next(gens[k], None)


def follow(first, makers):
    yield from merge(first)
    yield from merge([m() for m in makers])


VM = pl.BlockSpec(memory_space=pltpu.VMEM)
HB = pl.BlockSpec(memory_space=pl.ANY)


def comm_call(slots, kernel, cid, ins, in_specs, outs, out_specs, room):
    return pl.pallas_call(
        kernel,
        out_shape=[jax.ShapeDtypeStruct(*o) for o in outs],
        in_specs=in_specs,
        out_specs=out_specs,
        scratch_shapes=[
            pltpu.SemaphoreType.DMA((slots,)),
            pltpu.SemaphoreType.DMA((slots,)),
            pltpu.SemaphoreType.DMA((40,)),
        ]
        + room,
        compiler_params=pltpu.CompilerParams(
            collective_id=cid, has_side_effects=True, vmem_limit_bytes=56 << 20
        ),
    )(*ins)


def pair_masks():
    lane = lax.broadcasted_iota(jnp.int32, (1, 2 * HD), 1)
    return [lane < HD, lane >= HD]


def block_scores(key_rows, query_block, start_row, first, slope):
    count, width = key_rows.shape[0], query_block.shape[0]
    raw = lax.dot_general(
        key_rows, query_block, (((1,), (1,)), ((), ())), preferred_element_type=F32
    )
    key_at = lax.broadcasted_iota(jnp.int32, (count, width), 0)
    query_at = lax.broadcasted_iota(jnp.int32, (1, width), 1) + first
    scores = raw - slope * (query_at - key_at).astype(F32)
    allowed = (key_at <= query_at) & (key_at >= start_row)
    return jnp.where(allowed, scores, -1e30)


def attend_kernel(block, slopes_ref, start_ref, q_ref, k_ref, v_ref, out_ref, lse_ref):
    length = q_ref.shape[0]
    pair = pl.program_id(0)
    for half, mask in enumerate(pair_masks()):
        keys = jnp.where(mask, k_ref[...], 0)
        turned = jnp.where(mask, v_ref[...], 0).T
        slope = slopes_ref[2 * pair + half]
        for first in range(0, length, block):
            here, upto = slice(first, first + block), first + block
            query_block = q_ref[here, :] * BF16(HD**-0.5)
            scores = block_scores(
                keys[:upto], query_block, start_ref[:, here], first, slope
            )
            top = jnp.max(scores, axis=0, keepdims=True)
            weights = jnp.exp(scores - top)
            total = jnp.sum(weights, axis=0, keepdims=True)
            lse_ref[0, half : half + 1, here] = top + jnp.log(total)
            probs = (weights * (1.0 / total)).astype(BF16)
            got = jnp.dot(turned[:, :upto], probs, preferred_element_type=F32).T
            if half == 0:
                out_ref[here, :] = got.astype(BF16)
            else:
                out_ref[here, :] = out_ref[here, :] + got.astype(BF16)


def attend_back_kernel(
    block, slopes_ref, start_ref, q_ref, k_ref, v_ref, o_ref, g_ref, lse_ref, dq_ref, dk_ref, dv_ref, dk, dv
):
    length = q_ref.shape[0]
    pair = pl.program_id(0)
    dk[...] = jnp.zeros_like(dk)
    dv[...] = jnp.zeros_like(dv)
    masks = pair_masks()
    for half, mask in enumerate(masks):
        keys = jnp.where(mask, k_ref[...], 0)
        values = jnp.where(mask, v_ref[...], 0)
        turned = keys.T * BF16(HD**-0.5)
        slope = slopes_ref[2 * pair + half]
        for first in range(0, length, block):
            here, upto = slice(first, first + block), first + block
            query_block = jnp.where(mask, q_ref[here, :], 0) * BF16(HD**-0.5)
            grad_block = jnp.where(mask, g_ref[here, :], 0)
            product = o_ref[here, :].astype(F32) * grad_block.astype(F32)
            delta = jnp.sum(product.T, axis=0, keepdims=True)
            scores = block_scores(
                keys[:upto], query_block, start_ref[:, here], first, slope
            )
            probs = jnp.exp(scores - lse_ref[0, half : half + 1, here])
            prob_grad = lax.dot_general(
                values[:upto], grad_block, (((1,), (1,)), ((), ())), preferred_element_type=F32
            )
            score_grad = (probs * (prob_grad - delta)).astype(BF16)
            dv[:upto, :] += jnp.dot(
                probs.astype(BF16), grad_block, preferred_element_type=F32
            )
            dk[:upto, :] += jnp.dot(score_grad, query_block, preferred_element_type=F32)
            got = jnp.dot(turned[:, :upto], score_grad, preferred_element_type=F32).T
            if half == 0:
                dq_ref[here, :] = got.astype(BF16)
            else:
                dq_ref[here, :] = dq_ref[here, :] + got.astype(BF16)
    dk_ref[...] = dk[...].astype(BF16)
    dv_ref[...] = dv[...].astype(BF16)


def attend_specs(length, pairs):
    column = lambda k: pl.BlockSpec((length, 2 * HD), lambda i, k=k: (0, k * pairs + i))
    fixed = [
        pl.BlockSpec(memory_space=pltpu.SMEM),
        pl.BlockSpec((1, length), lambda i: (0, 0)),
    ]
    lse = pl.BlockSpec((1, 2, length), lambda i: (i, 0, 0))
    return column, fixed, lse


ATTEND = pltpu.CompilerParams(vmem_limit_bytes=48 << 20)


def attend(mixed, start, slopes):
    length, pairs = mixed.shape[0], mixed.shape[1] // (6 * HD)
    column, fixed, lse = attend_specs(length, pairs)
    return pl.pallas_call(
        functools.partial(attend_kernel, min(256, length)),
        grid=(pairs,),
        in_specs=fixed + [column(0), column(1), column(2)],
        out_specs=[column(0), lse],
        out_shape=[
            jax.ShapeDtypeStruct((length, pairs * 2 * HD), BF16),
            jax.ShapeDtypeStruct((pairs, 2, length), F32),
        ],
        compiler_params=ATTEND,
    )(slopes, start, mixed, mixed, mixed)


def attend_back(mixed, attended, upstream, log_sums, start, slopes):
    length, pairs = mixed.shape[0], mixed.shape[1] // (6 * HD)
    column, fixed, lse = attend_specs(length, pairs)
    wide = jax.ShapeDtypeStruct((length, pairs * 2 * HD), BF16)
    return pl.pallas_call(
        functools.partial(attend_back_kernel, min(256, length)),
        grid=(pairs,),
        in_specs=fixed + [column(0), column(1), column(2), column(0), column(0), lse],
        out_specs=[column(0)] * 3,
        out_shape=[wide] * 3,
        scratch_shapes=[pltpu.VMEM((length, 2 * HD), F32)] * 2,
        compiler_params=ATTEND,
    )(slopes, start, mixed, mixed, mixed, attended, upstream, log_sums)


def layer_norm(values, gain_row, shift_row):
    centred = values - jnp.mean(values, axis=-1, keepdims=True)
    spread = jnp.mean(centred * centred, axis=-1, keepdims=True)
    return centred * lax.rsqrt(spread + epsilon) * gain_row + shift_row


def gelu_exact(values):
    return jax.nn.gelu(values, approximate=False)


def body(
    tokens,
    segments,
    cotangent,
    mix_weight,
    mix_moment,
    mix_average,
    out_weight,
    out_moment,
    out_average,
    up_weight,
    up_moment,
    up_average,
    down_weight,
    down_moment,
    down_average,
    norm_gains,
    gain_moment,
    gain_average,
    biases,
    bias_moment,
    bias_average,
):
    S, F = lax.axis_size("seq"), lax.axis_size("fsdp")
    owners = S * F
    s_at = lax.axis_index("seq")
    T = tokens.shape[1]
    L = T * S
    R = D // owners
    RD = FF // owners
    W = D // S
    U = FF // S
    heads = HEADS // S
    slots = 12 * max(S, F)
    call = functools.partial(comm_call, slots)

    head_ids = s_at * heads + jnp.arange(heads, dtype=jnp.int32) + 1
    slopes = jnp.exp2(-8.0 * head_ids.astype(F32) / HEADS)
    documents = segments[0]
    start = jnp.sum(documents[:, None] < documents[None, :], axis=0, dtype=jnp.int32)[None]

    mix_low = mix_weight.astype(BF16).reshape(R, 3, S, W).transpose(2, 0, 1, 3).reshape(S, R, 3 * W)
    up_low = up_weight.astype(BF16).reshape(R, S, U).transpose(1, 0, 2)
    out_low = out_weight.astype(BF16)
    down_low = down_weight.astype(BF16)
    small = jnp.concatenate([norm_gains, biases], axis=0).astype(BF16).astype(F32)
    small = jnp.pad(small, ((0, 4), (0, 128 - R)))

    def first_kernel(
        tok, mix, out, vec, up, tok_f, mix_f, out_f, vec_f, up_r, send, recv, near
    ):
        net = Net(send, recv, near)
        seq, sides = line_of("seq"), both_of("fsdp")
        s, f = lax.axis_index("seq"), lax.axis_index("fsdp")
        greet(everyone("seq") + everyone("fsdp"))
        owned = [
            net.local(tok, tok_f.at[s]),
            net.local(out, out_f.at[f]),
        ]
        vec_own = net.local(vec, vec_f.at[s, f])

        def mix_half(k):
            at = pl.ds(k * (S // 2), S // 2)
            return lambda: gather(
                net, sides[k], mix_f.at[at, f], lambda i: mix_f.at[at, i], 20, 13, 13
            )

        def out_half(k):
            at = pl.ds(k * (D // 2), D // 2)
            return gather(net, sides[k], out.at[:, at], lambda i: out_f.at[i, :, at], 0, 5, 5)

        def vec_next():
            vec_own.wait()
            return gather(net, sides[0], vec_f.at[:, f], lambda i: vec_f.at[:, i], 6, 1, 1)

        run(
            net,
            follow(
                [exchange(net, "seq", lambda i: mix.at[i], lambda i: mix_f.at[i, f], 0, 20)],
                [mix_half(0), mix_half(1)],
            ),
            follow([gather(net, seq, vec, lambda i: vec_f.at[i, f], 0, 2, 1)], [vec_next]),
            out_half(0),
            out_half(1),
            gather(net, seq, tok, lambda i: tok_f.at[i], 0, 15),
            exchange(net, "seq", lambda i: up.at[i], lambda i: up_r.at[i], 22, 60, True),
        )
        for o in owned:
            o.wait()

    tok_full, mix_full, out_full, vec_full, up_mid = call(
        first_kernel,
        1,
        (tokens[0], mix_low, out_low, small, up_low),
        [HB] * 5,
        [
            ((S, T, D), BF16),
            ((S, F, R, 3 * W), BF16),
            ((F, R, D), BF16),
            ((S, F, 16, 128), F32),
            ((S, R, U), BF16),
        ],
        [HB] * 5,
        [],
    )
    vectors = vec_full[:, :, :12, :R].transpose(2, 0, 1, 3).reshape(12, D)
    gain_values, bias_values = vectors[:2], vectors[2:]
    mine = lambda row, width: lax.dynamic_slice_in_dim(row.reshape(-1), s_at * width, width)
    mix_own = mix_full.reshape(D, 3 * W)
    out_own = out_full.reshape(W, D)

    normed = layer_norm(
        tok_full.reshape(L, D).astype(F32), gain_values[0], bias_values[0]
    ).astype(BF16)
    mix_bias = jnp.concatenate(
        [mine(bias_values[1], W), jnp.zeros((W,), F32), mine(bias_values[2], W)]
    )
    mixed = (jnp.dot(normed, mix_own, preferred_element_type=F32) + mix_bias).astype(BF16)
    attended, log_sums = attend(mixed, start, slopes)
    out_part = jnp.dot(attended, out_own, preferred_element_type=F32).astype(BF16)

    def second_kernel(part, cot, up, down, total, cot_f, up_f, down_f, send, recv, near, *room):
        net = Net(send, recv, near)
        seq, sides = line_of("seq"), both_of("fsdp")
        s, f = lax.axis_index("seq"), lax.axis_index("fsdp")
        greet(seq.partners() + everyone("fsdp"))
        owned = [
            net.local(cot, cot_f.at[s]),
            net.local(down, down_f.at[f]),
            net.local(up, up_f.at[:, f]),
        ]

        def up_half(k):
            at = pl.ds(k * (S // 2), S // 2)
            return gather(net, sides[k], up.at[at], lambda i: up_f.at[at, i], 0, 30, 34)

        def down_half(k):
            at = pl.ds(k * (RD // 2), RD // 2)
            return gather(net, sides[k], down.at[at], lambda i: down_f.at[i, at], 0, 29, 34)

        run(
            net,
            scatter(net, seq, lambda i: part.at[i], total, room, 0, 3, 13),
            down_half(0),
            down_half(1),
            gather(net, seq, cot, lambda i: cot_f.at[i], 0, 14),
            up_half(0),
            up_half(1),
        )
        for o in owned:
            o.wait()

    attn_sum, cot_full, up_full, down_full = call(
        second_kernel,
        2,
        (out_part.reshape(S, T, D), cotangent[0], up_mid, down_low),
        [VM, HB, HB, HB],
        [((T, D), F32), ((S, T, D), BF16), ((S, F, R, U), BF16), ((F, RD, D), BF16)],
        [VM, HB, HB, HB],
        scatter_scratch(S // 2, T, D),
    )
    row_values = tokens[0].astype(F32)
    hidden_in = row_values + attn_sum + bias_values[3]
    normed_two = layer_norm(hidden_in, gain_values[1], bias_values[4]).astype(BF16)

    B = 2 * T
    UT = min(256, U)
    G = D // S
    n = S // 2
    down_items, items = U // UT, U // UT + S
    per_step = -(-items // (n - 1))

    def middle_kernel(
        rows,
        up,
        down,
        cot,
        bias,
        total,
        result_out,
        up_out,
        down_out,
        sums,
        send,
        recv,
        near,
        two,
        up_v,
        down_v,
        cot_v,
        act,
        pre,
        turn,
        part_n,
        part_r,
        sib,
        in_r,
        in_l,
    ):
        net = Net(send, recv, near)
        ro = line_of("seq")
        p, q = ro.p, ro.q
        other = ro.dev(p, 1 - q)
        loads = [net.local(up, up_v), net.local(down, down_v), net.local(cot, cot_v)]
        sums[...] = jnp.zeros_like(sums)
        greet(ro.partners())
        block = lambda ref, i: ref.at[pl.ds(pl.multiple_of(i * T, T), T)]
        place = lambda k, side: block(two, ro.index(k, side))
        loads.append(net.local(rows, place(p, q)))
        ag_r, ag_l, over = net.take(n - 1), net.take(n - 1), net.take(n)
        rs_r, rs_l, pair = net.take(n - 1), net.take(n - 1), net.take(n)
        ag_right = lambda k, src: net.copy(ag_r + p - k, src, place(k, q), ro.dev(p + 1, q))
        ag_left = lambda k, src: net.copy(ag_l + k - p, src, place(k, q), ro.dev(p - 1, q))
        ag_over = lambda k, src: net.copy(over + k, src, place(k, q), other)
        mine = lambda d: block(part_n, ro.index(d, q))
        swap = lambda d: net.copy(pair + d, block(part_n, ro.index(d, 1 - q)), sib.at[d], other)
        move_r = lambda d: net.copy(rs_r + d - 1, in_r.at[d - 1], in_r.at[d - 1], ro.dev(p + 1, q))
        move_l = lambda d: net.copy(rs_l + d, in_l.at[d], in_l.at[d], ro.dev(p - 1, q))
        leave = lambda k: pltpu.make_async_copy(
            part_r.at[pl.ds(pl.multiple_of(k * B, B), B)],
            result_out.at[pl.ds(pl.multiple_of(k * B, B), B)],
            near.at[8 + k],
        )

        pl.when(p + 1 < n)(lambda: ag_right(p, rows).start())
        pl.when(p > 0)(lambda: ag_left(p, rows).start())
        ag_over(p, rows).start()
        for made in loads:
            made.wait()

        def arrive(e):
            @pl.when((e > 0) & (p - e >= 0))
            def _():
                k = p - e
                net.copy(ag_r + e - 1, place(k, q), place(k, q), other).wait_recv()
                pl.when(p + 1 < n)(lambda: ag_right(k, place(k, q)).start())
                ag_over(k, place(k, q)).start()

            @pl.when((e > 0) & (p + e < n))
            def _():
                k = p + e
                net.copy(ag_l + e - 1, place(k, q), place(k, q), other).wait_recv()
                pl.when(p > 0)(lambda: ag_left(k, place(k, q)).start())
                ag_over(k, place(k, q)).start()

        def send_on(ends, e):
            d = e - p

            @pl.when(((p == 0) if ends else (p > 0)) & (d > p) & (d < n))
            def _():
                swap(d).wait_recv()
                slot = in_r.at[d - 1]
                if ends:
                    add_rows(slot, [mine(d), sib.at[d]])
                else:
                    move_r(d).wait_recv()
                    add_rows(slot, [slot, mine(d), sib.at[d]])
                move_r(d).start()

            d2 = n - 1 - (e - (n - 1 - p))

            @pl.when(((p == n - 1) if ends else (p < n - 1)) & (d2 < p) & (d2 >= 0))
            def _():
                swap(d2).wait_recv()
                slot = in_l.at[d2]
                if ends:
                    add_rows(slot, [mine(d2), sib.at[d2]])
                else:
                    move_l(d2).wait_recv()
                    add_rows(slot, [slot, mine(d2), sib.at[d2]])
                move_l(d2).start()

        def feed_forward(k):
            net.copy(over + k, place(k, 1 - q), place(k, 1 - q), other).wait_recv()
            here = pl.ds(pl.multiple_of(k * B, B), B)

            def hidden(i, _):
                at = pl.ds(pl.multiple_of(i * UT, UT), UT)
                value = jnp.dot(two[here, :], up_v[:, at], preferred_element_type=F32) + bias[:, at]
                chance = 0.5 + 0.5 * lax.erf(value * 0.5**0.5)
                slope = chance + value * (jnp.exp(value * value * -0.5) * (2 * math.pi) ** -0.5)
                act[here, at] = (value * chance).astype(BF16)
                grad = lax.dot_general(
                    cot_v[here, :], down_v[at, :], (((1,), (1,)), ((), ())), preferred_element_type=F32
                )
                low = (grad * slope).astype(BF16)
                pre[here, at] = low
                sums[:, at] += jnp.sum(low.astype(F32), axis=0, keepdims=True)
                return 0

            lax.fori_loop(0, U // UT, hidden, 0)

            def back(i, _):
                at = pl.ds(pl.multiple_of(i * 512, 512), 512)
                part_n[here, at] = lax.dot_general(
                    pre[here, :], up_v[at, :], (((1,), (1,)), ((), ())), preferred_element_type=F32
                ).astype(BF16)
                return 0

            lax.fori_loop(0, D // 512, back, 0)
            swap(k).start()

            def forth(i, _):
                at = pl.ds(pl.multiple_of(i * 512, 512), 512)
                part_r[here, at] = jnp.dot(
                    act[here, :], down_v[:, at], preferred_element_type=F32
                ).astype(BF16)
                return 0

            lax.fori_loop(0, D // 512, forth, 0)
            leave(k).start()

        def outward(e, _):
            arrive(e)
            send_on(False, e)
            for side in (-1, 1):
                k = p + side * e
                pl.when((k >= 0) & (k < n) & ((e > 0) | (side > 0)))(lambda: feed_forward(k))
            send_on(True, e)
            return 0

        lax.fori_loop(0, n, outward, 0)
        up_leave = lambda i: pltpu.make_async_copy(
            up_v.at[pl.ds(pl.multiple_of(i * G, G), G)],
            up_out.at[pl.ds(pl.multiple_of(i * G, G), G)],
            near.at[16 + i],
        )
        down_leave = lambda i: pltpu.make_async_copy(
            down_v.at[pl.ds(pl.multiple_of(i * UT, UT), UT)],
            down_out.at[pl.ds(pl.multiple_of(i * UT, UT), UT)],
            near.at[4 + i],
        )

        def item(i, _):
            @pl.when(i < down_items)
            def _():
                here = pl.ds(pl.multiple_of(i * UT, UT), UT)
                turn[:UT, :] = act[:, here].T

                def one(j, _):
                    at = pl.ds(pl.multiple_of(j * 512, 512), 512)
                    down_v[here, at] = jnp.dot(
                        turn[:UT, :], cot_v[:, at], preferred_element_type=F32
                    ).astype(BF16)
                    return 0

                lax.fori_loop(0, D // 512, one, 0)
                down_leave(i).start()

            @pl.when((i >= down_items) & (i < items))
            def _():
                c = i - down_items
                here = pl.ds(pl.multiple_of(c * G, G), G)
                turn[:G, :] = two[:, here].T

                def one(j, _):
                    at = pl.ds(pl.multiple_of(j * UT, UT), UT)
                    up_v[here, at] = jnp.dot(
                        turn[:G, :], pre[:, at], preferred_element_type=F32
                    ).astype(BF16)
                    return 0

                lax.fori_loop(0, U // UT, one, 0)
                up_leave(c).start()

            return 0

        def inward(e, _):
            send_on(False, e)
            lax.fori_loop((e - n) * per_step, (e - n + 1) * per_step, item, 0)
            return 0

        lax.fori_loop(n, 2 * n - 1, inward, 0)
        swap(p).wait_recv()

        @pl.when(p > 0)
        def _():
            move_r(p).wait_recv()

        @pl.when(p < n - 1)
        def _():
            move_l(p).wait_recv()

        @pl.when(p == 0)
        def _():
            add_rows(total, [mine(p), sib.at[p], in_l.at[p]])

        @pl.when(p == n - 1)
        def _():
            add_rows(total, [mine(p), sib.at[p], in_r.at[p - 1]])

        @pl.when((p > 0) & (p < n - 1))
        def _():
            add_rows(total, [mine(p), sib.at[p], in_r.at[p - 1], in_l.at[p]])

        def last(k, _):
            ag_over(k, place(k, q)).wait_send()
            swap(k).wait_send()
            leave(k).wait()
            pl.when((k <= p) & (p + 1 < n))(lambda: ag_right(k, place(k, q)).wait_send())
            pl.when((k >= p) & (p > 0))(lambda: ag_left(k, place(k, q)).wait_send())
            pl.when(k > p)(lambda: move_r(k).wait_send())
            pl.when(k < p)(lambda: move_l(k).wait_send())
            return 0

        lax.fori_loop(0, n, last, 0)
        for i in range(down_items):
            down_leave(i).wait()
        for i in range(S):
            up_leave(i).wait()

    two_grad, result_part, up_part, down_part, pre_sum = call(
        middle_kernel,
        3,
        (
            normed_two,
            up_full.reshape(D, U),
            down_full.reshape(U, D),
            cot_full.reshape(L, D),
            mine(bias_values[6:10], U)[None],
        ),
        [HB] * 4 + [VM],
        [((T, D), F32), ((L, D), BF16), ((D, U), BF16), ((U, D), BF16), ((1, U), F32)],
        [VM, HB, HB, HB, VM],
        [
            pltpu.VMEM((L, D), BF16),
            pltpu.VMEM((D, U), BF16),
            pltpu.VMEM((U, D), BF16),
            pltpu.VMEM((L, D), BF16),
            pltpu.VMEM((L, U), BF16),
            pltpu.VMEM((L, U), BF16),
            pltpu.VMEM((256, L), BF16),
            pltpu.VMEM((L, D), BF16),
            pltpu.VMEM((L, D), BF16),
            pltpu.VMEM((n, T, D), BF16),
            pltpu.VMEM((n - 1, T, D), BF16),
            pltpu.VMEM((n - 1, T, D), BF16),
        ],
    )
    upstream_float = cotangent[0].astype(F32)
    second_pull = jax.vjp(layer_norm, hidden_in, gain_values[1], bias_values[4])[1]
    hidden_part, gain_two_gradient, shift_two_gradient = second_pull(two_grad)
    hidden_gradient = upstream_float + hidden_part
    hidden_low = hidden_gradient.astype(BF16)

    def fifth_kernel(
        rows, part, up, down, rows_f, total, up_s, down_s, send, recv, near, *room
    ):
        net = Net(send, recv, near)
        seq, sides = line_of("seq"), both_of("fsdp")
        s = lax.axis_index("seq")
        greet(seq.partners() + everyone("fsdp"))
        own = net.local(rows, rows_f.at[s])

        def up_half(k):
            at = pl.ds(k * (S // 2), S // 2)
            return scatter(
                net, sides[k], lambda i: up.at[at, i], up_s.at[at], room[5 + 5 * k : 10 + 5 * k], 0, 22, 44
            )

        def down_half(k):
            at = pl.ds(k * (D // 2), D // 2)
            return scatter(
                net,
                sides[k],
                lambda i: down.at[i, :, at],
                down_s.at[:, at],
                room[15 + 5 * k : 20 + 5 * k],
                0,
                22,
                44,
            )

        run(
            net,
            gather(net, seq, rows, lambda i: rows_f.at[i]),
            scatter(net, seq, lambda i: part.at[i], total, room[:5]),
            down_half(0),
            down_half(1),
            up_half(0),
            up_half(1),
        )
        own.wait()

    hidden_full, result_sum, up_mid_grad, down_share = call(
        fifth_kernel,
        5,
        (
            hidden_low,
            result_part.reshape(S, T, D),
            up_part.reshape(S, F, R, U),
            down_part.reshape(F, RD, D),
        ),
        [HB, VM, VM, VM],
        [((S, T, D), BF16), ((T, D), F32), ((S, R, U), BF16), ((RD, D), F32)],
        [HB, VM, VM, VM],
        scatter_scratch(S // 2, T, D)
        + 2 * scatter_scratch(F // 2, S // 2, R, U)
        + 2 * scatter_scratch(F // 2, RD, D // 2),
    )
    output = (hidden_in + result_sum + bias_values[5]).astype(BF16)[None]
    hidden_full = hidden_full.reshape(L, D)
    attn_grad = jnp.einsum(
        "td,cd->tc", hidden_full, out_own, preferred_element_type=F32
    ).astype(BF16)
    query_grad, key_grad, value_grad = attend_back(
        mixed, attended, attn_grad, log_sums, start, slopes
    )
    mixed_grad = jnp.concatenate([query_grad, key_grad, value_grad], axis=1)
    one_grad_part = jnp.einsum("te,ce->tc", mixed_grad, mix_own, preferred_element_type=F32)
    out_grad = jnp.einsum("tc,td->cd", attended, hidden_full, preferred_element_type=F32)
    mix_grad = jnp.einsum("tc,te->ce", normed, mixed_grad, preferred_element_type=F32)

    def sixth_kernel(
        part, mix, out, up, total, mix_s, out_s, up_s, send, recv, near, mix_r, *room
    ):
        net = Net(send, recv, near)
        seq, sides = line_of("seq"), both_of("fsdp")
        greet(everyone("seq") + everyone("fsdp"))

        def mix_half(k):
            at = pl.ds(k * (S // 2), S // 2)
            return scatter(
                net, sides[k], lambda i: mix.at[at, i], mix_r.at[at], room[5 + 5 * k : 10 + 5 * k], 0, 11, 22
            )

        def out_half(k):
            at = pl.ds(k * (D // 2), D // 2)
            return scatter(
                net, sides[k], lambda i: out.at[i, :, at], out_s.at[:, at], room[15 + 5 * k : 20 + 5 * k], 0, 11, 22
            )

        run(
            net,
            follow(
                [mix_half(0), mix_half(1)],
                [
                    lambda: exchange(
                        net, "seq", lambda i: mix_r.at[i], lambda i: mix_s.at[i], 34
                    )
                ],
            ),
            scatter(net, seq, lambda i: part.at[i], total, room[:5]),
            exchange(net, "seq", lambda i: up.at[i], lambda i: up_s.at[i], 0, 45),
            out_half(0),
            out_half(1),
        )

    one_grad, mix_share, out_share, up_share = call(
        sixth_kernel,
        6,
        (
            one_grad_part.astype(BF16).reshape(S, T, D),
            mix_grad.astype(BF16).reshape(S, F, R, 3 * W),
            out_grad.astype(BF16).reshape(F, R, D),
            up_mid_grad,
        ),
        [VM, VM, VM, HB],
        [((T, D), F32), ((S, R, 3 * W), BF16), ((R, D), F32), ((S, R, U), BF16)],
        [VM, HB, VM, HB],
        [pltpu.VMEM((S, R, 3 * W), BF16)]
        + scatter_scratch(S // 2, T, D)
        + 2 * scatter_scratch(F // 2, S // 2, R, 3 * W)
        + 2 * scatter_scratch(F // 2, R, D // 2),
    )
    first_pull = jax.vjp(layer_norm, row_values, gain_values[0], bias_values[0])[1]
    rows_part, gain_one_gradient, shift_one_gradient = first_pull(one_grad)
    tokens_grad = (hidden_gradient + rows_part).astype(BF16)[None]

    def spread(row, count):
        return lax.dynamic_update_slice_in_dim(
            jnp.zeros((count * S * row.shape[0] // count,), F32), row, s_at * row.shape[0], 0
        ).reshape(count, D)

    mixed_sum = jnp.sum(mixed_grad.astype(F32), axis=0)
    small_gradient = jnp.concatenate(
        [
            gain_one_gradient[None],
            gain_two_gradient[None],
            shift_one_gradient[None],
            spread(mixed_sum[:W], 1),
            spread(mixed_sum[2 * W :], 1),
            jnp.sum(hidden_gradient, axis=0)[None],
            shift_two_gradient[None],
            jnp.sum(upstream_float, axis=0)[None],
            spread(pre_sum[0], 4),
        ],
        axis=0,
    )
    small_gradient = jnp.pad(
        small_gradient.reshape(12, S, F, R).transpose(1, 2, 0, 3),
        ((0, 0), (0, 0), (0, 4), (0, 128 - R)),
    )

    def last_kernel(vec, total, send, recv, near, got, mid, got_two):
        net = Net(send, recv, near)
        greet(everyone("seq") + everyone("fsdp"))
        for _ in exchange(net, "seq", lambda i: vec.at[i], lambda i: got.at[i]):
            pass
        mid[...] = jnp.sum(got[...], axis=0)
        for _ in exchange(net, "fsdp", lambda i: mid.at[i], lambda i: got_two.at[i]):
            pass
        total[...] = jnp.sum(got_two[...], axis=0)
        run(net)

    (small_share,) = call(
        last_kernel,
        7,
        (small_gradient,),
        [VM],
        [((16, 128), F32)],
        [VM],
        [
            pltpu.VMEM((S, F, 16, 128), F32),
            pltpu.VMEM((F, 16, 128), F32),
            pltpu.VMEM((F, 16, 128), F32),
        ],
    )
    mix_final = mix_share.astype(F32).reshape(S, R, 3, W).transpose(1, 2, 0, 3).reshape(R, 3 * D)
    up_final = up_share.astype(F32).transpose(1, 0, 2).reshape(R, FF)
    step_rate = base_rate / math.sqrt(owners * T)
    vector_step = vector_rate / math.sqrt(owners * T)
    rate_list = (step_rate, step_rate, step_rate, step_rate, vector_step, vector_step)
    masters = (mix_weight, out_weight, up_weight, down_weight, norm_gains, biases)
    shares = (mix_final, out_share, up_final, down_share, small_share[:2, :R], small_share[2:12, :R])
    moments = (mix_moment, out_moment, up_moment, down_moment, gain_moment, bias_moment)
    averages = (mix_average, out_average, up_average, down_average, gain_average, bias_average)
    updated = []
    for master, moment, average, share, rate in zip(masters, moments, averages, shares, rate_list):
        new_moment = mom_decay * moment + share
        new_weight = master - rate * (share + mom_decay * new_moment)
        new_average = avg_decay * average + (1.0 - avg_decay) * new_weight
        updated += [new_moment, new_weight, new_average]
    return (output, tokens_grad, *updated)


def solution(mesh):
    rows = P("fsdp", "seq", None)
    param = P(("seq", "fsdp"), None)
    vector = P(None, ("seq", "fsdp"))
    return jax.shard_map(
        body,
        mesh=mesh,
        in_specs=(rows, P("fsdp", None), rows) + (param,) * 12 + (vector,) * 6,
        out_specs=(rows, rows) + (param,) * 12 + (vector,) * 6,
        check_vma=False,
    )
```

```python
import functools
import heapq
import math

import jax
import jax.numpy as jnp
from jax import lax
from jax.experimental import pallas as pl
from jax.experimental.pallas import tpu as pltpu
from jax.sharding import PartitionSpec as P

D = 2048
HEADS = 32
HD = 64
FF = 8192

epsilon = 1e-05
mom_decay = 0.5
avg_decay = 0.5
base_rate = 0.02
vector_rate = 0.1

BF16 = jnp.bfloat16
F32 = jnp.float32
MESH = pl.DeviceIdType.MESH


class Net:
    def __init__(self, send, recv, near):
        self.send, self.recv, self.near = send, recv, near
        self.used = self.near_used = 0
        self.later = []

    def take(self, count):
        first = self.used
        self.used += count
        assert self.used <= self.send.shape[0]
        return first

    def copy(self, slot, src, dst, dev):
        return pltpu.make_async_remote_copy(
            src_ref=src,
            dst_ref=dst,
            send_sem=self.send.at[slot],
            recv_sem=self.recv.at[slot],
            device_id=dev,
            device_id_type=MESH,
        )

    def local(self, src, dst):
        made = pltpu.make_async_copy(src, dst, self.near.at[self.near_used])
        self.near_used += 1
        made.start()
        return made


def when(cond, act):
    if cond is None:
        act()
    else:
        pl.when(cond)(act)


def greet(partners):
    barrier = pltpu.get_barrier_semaphore()
    for cond, dev in partners:
        when(
            cond,
            functools.partial(
                pl.semaphore_signal, barrier, inc=1, device_id=dev, device_id_type=MESH
            ),
        )
    count = sum(1 for cond, _ in partners if cond is None)
    for cond, _ in partners:
        if cond is not None:
            count = count + jnp.where(cond, 1, 0)
    pl.semaphore_wait(barrier, count)


class Roles:
    def __init__(self, axis, length, place, side, stride, pair):
        self.axis, self.length, self.p, self.q = axis, length, place, side
        self.stride, self.pair = stride, pair

    def index(self, p, q):
        return p * self.stride + q * self.pair

    def dev(self, p, q):
        return {self.axis: self.index(p, q)}

    def partners(self):
        return [
            (None, self.dev(self.p, 1 - self.q)),
            (self.p + 1 < self.length, self.dev(self.p + 1, self.q)),
            (self.p > 0, self.dev(self.p - 1, self.q)),
        ]


def line_of(axis):
    me, size = lax.axis_index(axis), lax.axis_size(axis)
    return Roles(axis, size // 2, me // 2, me % 2, 2, 1)


def both_of(axis):
    me, size = lax.axis_index(axis), lax.axis_size(axis)
    first = line_of(axis)
    if size != 4:
        return first, first
    return first, Roles(axis, 2, me % 2, me // 2, 1, 2)


def everyone(axis):
    me, size = lax.axis_index(axis), lax.axis_size(axis)
    return [(None, {axis: (me + o) % size}) for o in range(1, size)]


def gather(
    net, ro, src, place, at_us=0.0, hop=11.0, over=1.0, hold=False, landed=None
):
    n, p, q = ro.length, ro.p, ro.q
    right, left = net.take(n - 1), net.take(n - 1)
    over_r, over_l, over_own = net.take(n - 1), net.take(n - 1), net.take(1)
    other = ro.dev(p, 1 - q)
    at = lambda k: place(ro.index(k, q))
    across = lambda k: place(ro.index(k, 1 - q))
    ref = lambda j, k: src if j == 0 else at(k)
    go_right = lambda j: net.copy(right + j, ref(j, p - j), at(p - j), ro.dev(p + 1, q))
    go_left = lambda j: net.copy(left + j, ref(j, p + j), at(p + j), ro.dev(p - 1, q))
    pass_r = lambda j: net.copy(over_r + j - 1, at(p - j), at(p - j), other)
    pass_l = lambda j: net.copy(over_l + j - 1, at(p + j), at(p + j), other)
    own = net.copy(over_own, src, at(p), other)
    if hold:
        yield at_us
    pl.when(p + 1 < n)(lambda: go_right(0).start())
    pl.when(p > 0)(lambda: go_left(0).start())
    own.start()

    def complete(j):
        if j == 0:
            net.copy(over_own, src, across(p), other).wait_recv()
            if landed:
                landed(p)
            return

        @pl.when(p - j >= 0)
        def _():
            net.copy(over_r + j - 1, across(p - j), across(p - j), other).wait_recv()
            if landed:
                landed(p - j)

        @pl.when(p + j < n)
        def _():
            net.copy(over_l + j - 1, across(p + j), across(p + j), other).wait_recv()
            if landed:
                landed(p + j)

    for j in range(1, n):
        yield at_us + hop * j

        @pl.when(p - j >= 0)
        def _():
            net.copy(right + j - 1, at(p - j), at(p - j), other).wait_recv()
            if j < n - 1:
                pl.when(p + 1 < n)(lambda: go_right(j).start())
            pass_r(j).start()

        @pl.when(p + j < n)
        def _():
            net.copy(left + j - 1, at(p + j), at(p + j), other).wait_recv()
            if j < n - 1:
                pl.when(p > 0)(lambda: go_left(j).start())
            pass_l(j).start()

        if landed:
            complete(j - 1)

    yield at_us + hop * (n - 1) + over
    for j in range(n - 1 if landed else 0, n):
        complete(j)

    def finish():
        own.wait_send()
        for j in range(n):
            if j < n - 1:
                pl.when((p - j >= 0) & (p + 1 < n))(lambda: go_right(j).wait_send())
                pl.when((p + j < n) & (p > 0))(lambda: go_left(j).wait_send())
            if j > 0:
                pl.when(p - j >= 0)(lambda: pass_r(j).wait_send())
                pl.when(p + j < n)(lambda: pass_l(j).wait_send())

    net.later.append(finish)


def add_rows(dst, srcs, step=16):
    def one(i, _):
        at = pl.ds(pl.multiple_of(i * step, step), step)
        total = srcs[0][at, :].astype(F32)
        for s in srcs[1:]:
            total = total + s[at, :].astype(F32)
        dst[at, :] = total.astype(dst.dtype)
        return 0

    if len(dst.shape) == 3:

        def layer(k, _):
            add_rows(dst.at[k], [s.at[k] for s in srcs], step)
            return 0

        lax.fori_loop(0, dst.shape[0], layer, 0)
    else:
        lax.fori_loop(0, dst.shape[0] // step, one, 0)


def scatter_scratch(ro_length, *shape):
    return [pltpu.VMEM((ro_length, *shape), BF16)] + [
        pltpu.VMEM((ro_length - 1, *shape), BF16)
    ] * 2


def scatter(
    net, ro, part, result, room, at_us=0.0, first=2.0, hop=11.0, hold=False, ready=None
):
    sib, in_r, in_l = room
    n, p, q = ro.length, ro.p, ro.q
    right, left, pair = net.take(n - 1), net.take(n - 1), net.take(n)
    other = ro.dev(p, 1 - q)
    order = []
    for j in range(n):
        order += [d for d in (n - 1 - j, j) if d not in order]
    mine = lambda d: part(ro.index(d, q))
    swap = lambda d: net.copy(pair + d, part(ro.index(d, 1 - q)), sib.at[d], other)
    send_r = lambda j: net.copy(right + j, in_r.at[j], in_r.at[j], ro.dev(p + 1, q))
    send_l = lambda j: net.copy(left + j, in_l.at[j], in_l.at[j], ro.dev(p - 1, q))
    if hold:
        yield at_us
    if n == 2:
        order = [1 - p, p]
    for d in order:
        if ready:
            ready(d)
        swap(d).start()
    for j in range(n - 1):
        yield at_us + first + hop * j
        dr, dl = n - 1 - j, j

        @pl.when(p < dr)
        def _():
            swap(dr).wait_recv()

            @pl.when(p > 0)
            def _():
                send_r(j).wait_recv()
                add_rows(in_r.at[j], [mine(dr), sib.at[dr], in_r.at[j]])

            @pl.when(p == 0)
            def _():
                add_rows(in_r.at[j], [mine(dr), sib.at[dr]])

            send_r(j).start()

        @pl.when(p > dl)
        def _():
            swap(dl).wait_recv()

            @pl.when(p < n - 1)
            def _():
                send_l(j).wait_recv()
                add_rows(in_l.at[j], [mine(dl), sib.at[dl], in_l.at[j]])

            @pl.when(p == n - 1)
            def _():
                add_rows(in_l.at[j], [mine(dl), sib.at[dl]])

            send_l(j).start()

    yield at_us + first + hop * (n - 1)
    from_r, from_l = n - 1 - p, p
    swap(p).wait_recv()

    @pl.when(p > 0)
    def _():
        send_r(from_r).wait_recv()

    @pl.when(p < n - 1)
    def _():
        send_l(from_l).wait_recv()

    @pl.when(p == 0)
    def _():
        add_rows(result, [mine(p), sib.at[p], in_l.at[from_l]])

    @pl.when(p == n - 1)
    def _():
        add_rows(result, [mine(p), sib.at[p], in_r.at[from_r]])

    if n > 2:

        @pl.when((p > 0) & (p < n - 1))
        def _():
            add_rows(result, [mine(p), sib.at[p], in_r.at[from_r], in_l.at[from_l]])

    def finish():
        for d in range(n):
            swap(d).wait_send()
        for j in range(n - 1):
            pl.when(p < n - 1 - j)(lambda: send_r(j).wait_send())
            pl.when(p > j)(lambda: send_l(j).wait_send())

    net.later.append(finish)


def direct_scratch(ro_length, *shape):
    return [
        pltpu.VMEM((ro_length, *shape), BF16),
        pltpu.VMEM((ro_length - 1, *shape), BF16),
    ]


class Direct:
    def __init__(self, net, ro, part, room):
        self.net, self.ro, self.part = net, ro, part
        self.sib, self.came = room
        self.pair, self.slots = net.take(ro.length), net.take(ro.length - 1)

    def mine(self, d):
        return self.part(self.ro.index(d, self.ro.q))

    def swap(self, d):
        ro = self.ro
        away = self.part(ro.index(d, 1 - ro.q))
        return self.net.copy(self.pair + d, away, self.sib.at[d], ro.dev(ro.p, 1 - ro.q))

    def move(self, d):
        ro = self.ro
        k = (d - ro.p + ro.length) % ro.length - 1
        return self.net.copy(self.slots + k, self.mine(d), self.came.at[k], ro.dev(d, ro.q))

    def ship(self, d):
        self.swap(d).wait_recv()
        add_rows(self.mine(d), [self.mine(d), self.sib.at[d]])
        pl.when(d != self.ro.p)(lambda: self.move(d).start())

    def total(self, result):
        ro = self.ro
        for k in range(ro.length - 1):
            self.net.copy(
                self.slots + k, self.came.at[k], self.came.at[k], ro.dev(ro.p, 1 - ro.q)
            ).wait_recv()
        add_rows(result, [self.mine(ro.p)] + [self.came.at[k] for k in range(ro.length - 1)])

    def finish(self):
        for d in range(self.ro.length):
            self.swap(d).wait_send()
            pl.when(d != self.ro.p)(lambda: self.move(d).wait_send())


def direct(net, ro, part, result, room, ready, at_us, last, hold=False):
    work = Direct(net, ro, part, room)
    n = ro.length
    if hold:
        yield at_us
    order = [(ro.p + n // 2 + o) % n for o in range(n)]
    for d in order:
        ready(d)
        work.swap(d).start()
    for d in order:
        work.ship(d)
    yield at_us + last
    work.total(result)
    net.later.append(work.finish)


def direct_gather(net, ro, src, place, at_us=0.0, last=40.0, hold=False):
    n, p, q = ro.length, ro.p, ro.q
    slots, over = net.take(n - 1), net.take(n)
    other = ro.dev(p, 1 - q)
    at = lambda k: place(ro.index(k, q))
    if hold:
        yield at_us
    sent = []
    for o in range(1, n):
        to = (p + (o + n // 2 - 1) % (n - 1) + 1) % n
        slot = slots + (to - p + n) % n - 1
        sent.append(net.copy(slot, src, at(p), ro.dev(to, q)))
        sent[-1].start()
    sent.append(net.copy(over, src, at(p), other))
    sent[-1].start()
    yield at_us + last
    for o in range(1, n):
        k = (p - o + n) % n
        net.copy(slots + o - 1, at(k), at(k), other).wait_recv()
        sent.append(net.copy(over + o, at(k), at(k), other))
        sent[-1].start()
    yield at_us + last + 4
    for o in range(n):
        k = (p - o + n) % n
        away = place(ro.index(k, 1 - q))
        net.copy(over + o, away, away, other).wait_recv()
    net.later.append(lambda: [made.wait_send() for made in sent])


def exchange(net, axis, src, place, at_us=0.0, last=15.0, hold=False):
    me, n = lax.axis_index(axis), lax.axis_size(axis)
    slots = net.take(n - 1)
    if hold:
        yield at_us
    near = net.local(src(me), place(me))
    sent = []
    for o in range(1, n):
        to = (me + o) % n
        sent.append(net.copy(slots + o - 1, src(to), place(me), {axis: to}))
        sent[-1].start()
    yield at_us + last
    near.wait()
    for o in range(1, n):
        at = (me + n - o) % n
        net.copy(slots + o - 1, src(at), place(at), {axis: at}).wait_recv()
    net.later.append(lambda: [s.wait_send() for s in sent])


def run(net, *gens):
    waiting = []
    for order, g in enumerate(gens):
        heapq.heappush(waiting, (0.0, order, g))
    while waiting:
        now, order, g = heapq.heappop(waiting)
        step = next(g, None)
        if step is not None:
            heapq.heappush(waiting, (max(step, now), order, g))
    for act in net.later:
        act()


def merge(gens):
    steps = [next(g, None) for g in gens]
    while any(s is not None for s in steps):
        at, k = min((s, i) for i, s in enumerate(steps) if s is not None)
        yield at
        steps[k] = next(gens[k], None)


def follow(first, makers):
    yield from merge(first)
    yield from merge([m() for m in makers])


VM = pl.BlockSpec(memory_space=pltpu.VMEM)
HB = pl.BlockSpec(memory_space=pl.ANY)


def comm_call(slots, kernel, cid, ins, in_specs, outs, out_specs, room):
    return pl.pallas_call(
        kernel,
        out_shape=[jax.ShapeDtypeStruct(*o) for o in outs],
        in_specs=in_specs,
        out_specs=out_specs,
        scratch_shapes=[
            pltpu.SemaphoreType.DMA((slots,)),
            pltpu.SemaphoreType.DMA((slots,)),
            pltpu.SemaphoreType.DMA((40,)),
        ]
        + room,
        compiler_params=pltpu.CompilerParams(
            collective_id=cid, has_side_effects=True, vmem_limit_bytes=60 << 20
        ),
    )(*ins)


def pair_masks():
    lane = lax.broadcasted_iota(jnp.int32, (1, 2 * HD), 1)
    return [lane < HD, lane >= HD]


def block_scores(key_rows, query_block, start_row, first, slope):
    count, width = key_rows.shape[0], query_block.shape[0]
    raw = lax.dot_general(
        key_rows, query_block, (((1,), (1,)), ((), ())), preferred_element_type=F32
    )
    key_at = lax.broadcasted_iota(jnp.int32, (count, width), 0)
    query_at = lax.broadcasted_iota(jnp.int32, (1, width), 1) + first
    scores = raw - slope * (query_at - key_at).astype(F32)
    allowed = (key_at <= query_at) & (key_at >= start_row)
    return jnp.where(allowed, scores, -1e30)


def attend(block, slopes, start_ref, mixed, out, lse_ref):
    length, width = out.shape
    wide = 2 * HD

    def one_pair(pair, _):
        column = lambda k: pl.ds(pl.multiple_of(k * width + pair * wide, wide), wide)
        q_at, k_at, v_at = column(0), column(1), column(2)
        for half, mask in enumerate(pair_masks()):
            keys = jnp.where(mask, mixed[:, k_at], 0)
            turned = jnp.where(mask, mixed[:, v_at], 0).T
            slope = slopes[2 * pair + half]
            for first in range(0, length, block):
                here, upto = slice(first, first + block), first + block
                query_block = mixed[here, q_at] * BF16(HD**-0.5)
                scores = block_scores(
                    keys[:upto], query_block, start_ref[:, here], first, slope
                )
                top = jnp.max(scores, axis=0, keepdims=True)
                weights = jnp.exp(scores - top)
                total = jnp.sum(weights, axis=0, keepdims=True)
                lse_ref[pair, half : half + 1, here] = top + jnp.log(total)
                probs = (weights * (1.0 / total)).astype(BF16)
                got = jnp.dot(turned[:, :upto], probs, preferred_element_type=F32).T
                if half == 0:
                    out[here, q_at] = got.astype(BF16)
                else:
                    out[here, q_at] = out[here, q_at] + got.astype(BF16)
        return 0

    lax.fori_loop(0, width // wide, one_pair, 0)


def attend_back(block, slopes, start_ref, mixed, att, grad, lse_ref, out, dk, dv):
    length, width = att.shape
    wide = 2 * HD
    pairs = width // wide

    def one_pair(pair, _):
        column = lambda k: pl.ds(pl.multiple_of(k * width + pair * wide, wide), wide)
        q_at, k_at, v_at = column(0), column(1), column(2)
        dk[...] = jnp.zeros_like(dk)
        dv[...] = jnp.zeros_like(dv)
        for half, mask in enumerate(pair_masks()):
            keys = jnp.where(mask, mixed[:, k_at], 0)
            values = jnp.where(mask, mixed[:, v_at], 0)
            turned = keys.T * BF16(HD**-0.5)
            slope = slopes[2 * pair + half]
            for first in range(0, length, block):
                here, upto = slice(first, first + block), first + block
                query_block = jnp.where(mask, mixed[here, q_at], 0) * BF16(HD**-0.5)
                grad_block = jnp.where(mask, grad[here, q_at], 0)
                product = att[here, q_at].astype(F32) * grad_block.astype(F32)
                delta = jnp.sum(product.T, axis=0, keepdims=True)
                scores = block_scores(
                    keys[:upto], query_block, start_ref[:, here], first, slope
                )
                probs = jnp.exp(scores - lse_ref[pair, half : half + 1, here])
                prob_grad = lax.dot_general(
                    values[:upto], grad_block, (((1,), (1,)), ((), ())), preferred_element_type=F32
                )
                score_grad = (probs * (prob_grad - delta)).astype(BF16)
                dv[:upto, :] += jnp.dot(
                    probs.astype(BF16), grad_block, preferred_element_type=F32
                )
                dk[:upto, :] += jnp.dot(score_grad, query_block, preferred_element_type=F32)
                got = jnp.dot(turned[:, :upto], score_grad, preferred_element_type=F32).T
                if half == 0:
                    out[here, q_at] = got.astype(BF16)
                else:
                    out[here, q_at] = out[here, q_at] + got.astype(BF16)
        out[:, k_at] = dk[...].astype(BF16)
        out[:, v_at] = dv[...].astype(BF16)
        return 0

    lax.fori_loop(0, pairs, one_pair, 0)


def layer_norm(values, gain_row, shift_row):
    centred = values - jnp.mean(values, axis=-1, keepdims=True)
    spread = jnp.mean(centred * centred, axis=-1, keepdims=True)
    return centred * lax.rsqrt(spread + epsilon) * gain_row + shift_row


def gelu_exact(values):
    return jax.nn.gelu(values, approximate=False)


def body(
    tokens,
    segments,
    cotangent,
    mix_weight,
    mix_moment,
    mix_average,
    out_weight,
    out_moment,
    out_average,
    up_weight,
    up_moment,
    up_average,
    down_weight,
    down_moment,
    down_average,
    norm_gains,
    gain_moment,
    gain_average,
    biases,
    bias_moment,
    bias_average,
):
    S, F = lax.axis_size("seq"), lax.axis_size("fsdp")
    owners = S * F
    s_at = lax.axis_index("seq")
    T = tokens.shape[1]
    L = T * S
    R = D // owners
    RD = FF // owners
    W = D // S
    U = FF // S
    heads = HEADS // S
    slots = 20 * max(S, F)
    call = functools.partial(comm_call, slots)

    head_ids = s_at * heads + jnp.arange(heads, dtype=jnp.int32) + 1
    slopes = jnp.exp2(-8.0 * head_ids.astype(F32) / HEADS)
    documents = segments[0]
    start = jnp.sum(documents[:, None] < documents[None, :], axis=0, dtype=jnp.int32)[None]

    mix_low = mix_weight.astype(BF16).reshape(R, 3, S, W).transpose(2, 0, 1, 3).reshape(S, R, 3 * W)
    up_low = up_weight.astype(BF16).reshape(R, S, U).transpose(1, 0, 2)
    out_low = out_weight.astype(BF16)
    down_low = down_weight.astype(BF16)
    small = jnp.concatenate([norm_gains, biases], axis=0).astype(BF16).astype(F32)
    place_at = (s_at * F + lax.axis_index("fsdp")) * R % 128
    small = lax.dynamic_update_slice(jnp.zeros((16, 128), F32), small, (0, place_at))

    G = D // S
    n = S // 2

    def first_kernel(
        slope_values,
        tok,
        mix,
        out,
        vec,
        up,
        cot,
        down,
        begin,
        total,
        vecs,
        mix_out,
        out_w,
        up_f,
        down_f,
        cot_f,
        one_out,
        mixed,
        att,
        lse,
        send,
        recv,
        near,
        tok_v,
        one_v,
        mix_v,
        out_v,
        vec_f,
        up_r,
        part,
        *room,
    ):
        net = Net(send, recv, near)
        seq, sides = line_of("seq"), both_of("fsdp")
        s, f = lax.axis_index("seq"), lax.axis_index("fsdp")
        block = lambda ref, i: ref.at[pl.ds(pl.multiple_of(i * T, T), T)]
        owned = [net.local(out, out_v.at[f]), net.local(cot, cot_f.at[s]), net.local(down, down_f.at[f])]
        tok_own = net.local(tok, block(tok_v, s))
        vec_own = net.local(vec, vec_f.at[s, f])
        greet(everyone("seq") + everyone("fsdp"))

        def mix_half(k):
            at = pl.ds(k * (S // 2), S // 2)
            return lambda: gather(
                net, sides[k], mix_v.at[at, f], lambda i: mix_v.at[at, i], 20, 13, 13
            )

        def out_half(k):
            at = pl.ds(k * (D // 2), D // 2)
            return gather(net, sides[k], out.at[:, at], lambda i: out_v.at[i, :, at], 0, 5, 5)

        def down_half(k):
            at = pl.ds(k * (RD // 2), RD // 2)
            return gather(
                net, sides[k], down.at[at], lambda i: down_f.at[i, at], 46, 24, 28, True
            )

        def up_half(k):
            at = pl.ds(k * (S // 2), S // 2)
            return lambda: gather(
                net, sides[k], up_r.at[at], lambda i: up_f.at[at, i], 86, 17, 25
            )

        def vec_next():
            vec_own.wait()
            return gather(net, sides[0], vec_f.at[:, f], lambda i: vec_f.at[:, i], 6, 1, 1)

        def vec_all():
            yield from follow(
                [gather(net, seq, vec, lambda i: vec_f.at[i, f], 0, 2, 1)], [vec_next]
            )
            each = 128 // R
            for c in range(D // 128):
                pieces = [
                    vec_f[i // F, i % F] for i in range(c * each, (c + 1) * each)
                ]
                vecs[:, c * 128 : (c + 1) * 128] = functools.reduce(jnp.add, pieces)
            tok_own.wait()

        def norm(k):
            step = 32

            def one(i, _):
                here = pl.ds(pl.multiple_of(k * 2 * T + i * step, step), step)
                one_v[here, :] = layer_norm(
                    tok_v[here, :].astype(F32), vecs[0:1, :], vecs[2:3, :]
                ).astype(BF16)
                return 0

            lax.fori_loop(0, 2 * T // step, one, 0)

        leave = lambda: [
            pltpu.make_async_copy(one_v, one_out, near.at[30]),
            pltpu.make_async_copy(mix_v, mix_out, near.at[31]),
            pltpu.make_async_copy(out_v, out_w, near.at[32]),
        ]

        def project():
            yield 58.0
            owned[0].wait()
            for made in leave():
                made.start()
            for c in range(3):
                if c == 1:
                    bias = jnp.zeros((1, W), F32)
                else:
                    bias = vecs[3 + c // 2 : 4 + c // 2, pl.ds(pl.multiple_of(s * W, W), W)]
                at = slice(c * W, (c + 1) * W)

                def one(i, _):
                    here = pl.ds(pl.multiple_of(i * 2 * T, 2 * T), 2 * T)
                    mixed[here, at] = (
                        jnp.dot(
                            one_v[here, :],
                            mix_v[:, :, :, at].reshape(D, W),
                            preferred_element_type=F32,
                        )
                        + bias
                    ).astype(BF16)
                    return 0

                lax.fori_loop(0, n, one, 0)
            yield 62.0
            attend(min(256, L), slope_values, begin, mixed, att, lse)

        def ready(d):
            here = pl.ds(pl.multiple_of(d * 2 * T, 2 * T), 2 * T)

            def one(i, _):
                at = pl.ds(pl.multiple_of(i * 512, 512), 512)
                part[here, at] = jnp.dot(
                    att[here, :], out_v[:, :, at].reshape(W, 512), preferred_element_type=F32
                ).astype(BF16)
                return 0

            lax.fori_loop(0, D // 512, one, 0)

        run(
            net,
            follow(
                [exchange(net, "seq", lambda i: mix.at[i], lambda i: mix_v.at[i, f], 0, 18)],
                [mix_half(0), mix_half(1)],
            ),
            vec_all(),
            out_half(0),
            out_half(1),
            gather(net, seq, tok, lambda i: block(tok_v, i), 19, 12, 1, True, norm),
            down_half(0),
            down_half(1),
            follow(
                [exchange(net, "seq", lambda i: up.at[i], lambda i: up_r.at[i], 57, 28, True)],
                [up_half(0), up_half(1)],
            ),
            project(),
            gather(net, seq, cot, lambda i: cot_f.at[i], 57, 17, hold=True),
            direct(net, seq, lambda i: block(part, i), total, room, ready, 74, 60, True),
        )
        up_own = [net.local(up_r, up_f.at[:, f])]
        for made in owned[1:] + leave() + up_own:
            made.wait()

    (
        attn_sum,
        vectors,
        mix_full,
        out_full,
        up_full,
        down_full,
        cot_full,
        normed,
        mixed,
        attended,
        log_sums,
    ) = call(
        first_kernel,
        1,
        (
            slopes,
            tokens[0],
            mix_low,
            out_low,
            small,
            up_low,
            cotangent[0],
            down_low,
            start,
        ),
        [pl.BlockSpec(memory_space=pltpu.SMEM), HB, HB, HB, VM, HB, HB, HB, VM],
        [
            ((T, D), F32),
            ((16, D), F32),
            ((S, F, R, 3 * W), BF16),
            ((F, R, D), BF16),
            ((S, F, R, U), BF16),
            ((F, RD, D), BF16),
            ((S, T, D), BF16),
            ((L, D), BF16),
            ((L, 3 * W), BF16),
            ((L, W), BF16),
            ((heads // 2, 2, L), F32),
        ],
        [VM, VM, HB, HB, HB, HB, HB, HB, VM, VM, VM],
        [
            pltpu.VMEM((L, D), BF16),
            pltpu.VMEM((L, D), BF16),
            pltpu.VMEM((S, F, R, 3 * W), BF16),
            pltpu.VMEM((F, R, D), BF16),
            pltpu.VMEM((S, F, 16, 128), F32),
            pltpu.VMEM((S, R, U), BF16),
            pltpu.VMEM((L, D), BF16),
        ]
        + direct_scratch(n, T, D),
    )
    gain_values, bias_values = vectors[:2], vectors[2:12]
    mine = lambda row, width: lax.dynamic_slice_in_dim(row.reshape(-1), s_at * width, width)
    mix_own = mix_full.reshape(D, 3 * W)
    out_own = out_full.reshape(W, D)
    row_values = tokens[0].astype(F32)
    hidden_in = row_values + attn_sum + bias_values[3]
    normed_two = layer_norm(hidden_in, gain_values[1], bias_values[4]).astype(BF16)

    B = 2 * T
    UT = min(256, U)
    down_items, items = U // UT, U // UT + S

    def middle_kernel(
        rows,
        up,
        down,
        cot,
        bias,
        total,
        result_out,
        up_out,
        down_out,
        sums,
        send,
        recv,
        near,
        two,
        up_v,
        down_v,
        cot_v,
        act,
        pre,
        turn,
        part_n,
        part_r,
        *room,
    ):
        net = Net(send, recv, near)
        ro = line_of("seq")
        p, q = ro.p, ro.q
        other = ro.dev(p, 1 - q)
        loads = [net.local(up, up_v), net.local(down, down_v), net.local(cot, cot_v)]
        sums[...] = jnp.zeros_like(sums)
        greet(ro.partners())
        block = lambda ref, i: ref.at[pl.ds(pl.multiple_of(i * T, T), T)]
        place = lambda k, side: block(two, ro.index(k, side))
        loads.append(net.local(rows, place(p, q)))
        ag_r, ag_l, over = net.take(n - 1), net.take(n - 1), net.take(n)
        sums_of = Direct(net, ro, lambda i: block(part_n, i), room)
        ag_right = lambda k, src: net.copy(ag_r + p - k, src, place(k, q), ro.dev(p + 1, q))
        ag_left = lambda k, src: net.copy(ag_l + k - p, src, place(k, q), ro.dev(p - 1, q))
        ag_over = lambda k, src: net.copy(over + k, src, place(k, q), other)
        leave = lambda k: pltpu.make_async_copy(
            part_r.at[pl.ds(pl.multiple_of(k * B, B), B)],
            result_out.at[pl.ds(pl.multiple_of(k * B, B), B)],
            near.at[8 + k],
        )

        pl.when(p + 1 < n)(lambda: ag_right(p, rows).start())
        pl.when(p > 0)(lambda: ag_left(p, rows).start())
        ag_over(p, rows).start()
        for made in loads:
            made.wait()

        def arrive(e):
            @pl.when((e > 0) & (p - e >= 0))
            def _():
                k = p - e
                net.copy(ag_r + e - 1, place(k, q), place(k, q), other).wait_recv()
                pl.when(p + 1 < n)(lambda: ag_right(k, place(k, q)).start())
                ag_over(k, place(k, q)).start()

            @pl.when((e > 0) & (p + e < n))
            def _():
                k = p + e
                net.copy(ag_l + e - 1, place(k, q), place(k, q), other).wait_recv()
                pl.when(p > 0)(lambda: ag_left(k, place(k, q)).start())
                ag_over(k, place(k, q)).start()

        def feed_forward(k):
            net.copy(over + k, place(k, 1 - q), place(k, 1 - q), other).wait_recv()
            here = pl.ds(pl.multiple_of(k * B, B), B)

            def hidden(i, _):
                at = pl.ds(pl.multiple_of(i * UT, UT), UT)
                value = jnp.dot(two[here, :], up_v[:, at], preferred_element_type=F32) + bias[:, at]
                chance = 0.5 + 0.5 * lax.erf(value * 0.5**0.5)
                slope = chance + value * (jnp.exp(value * value * -0.5) * (2 * math.pi) ** -0.5)
                act[here, at] = (value * chance).astype(BF16)
                grad = lax.dot_general(
                    cot_v[here, :], down_v[at, :], (((1,), (1,)), ((), ())), preferred_element_type=F32
                )
                low = (grad * slope).astype(BF16)
                pre[here, at] = low
                sums[:, at] += jnp.sum(low.astype(F32), axis=0, keepdims=True)
                return 0

            lax.fori_loop(0, U // UT, hidden, 0)

            def back(i, _):
                at = pl.ds(pl.multiple_of(i * 512, 512), 512)
                part_n[here, at] = lax.dot_general(
                    pre[here, :], up_v[at, :], (((1,), (1,)), ((), ())), preferred_element_type=F32
                ).astype(BF16)
                return 0

            lax.fori_loop(0, D // 512, back, 0)
            sums_of.swap(k).start()

            def forth(i, _):
                at = pl.ds(pl.multiple_of(i * 512, 512), 512)
                part_r[here, at] = jnp.dot(
                    act[here, :], down_v[:, at], preferred_element_type=F32
                ).astype(BF16)
                return 0

            lax.fori_loop(0, D // 512, forth, 0)
            leave(k).start()
            sums_of.ship(k)

        def outward(e, _):
            arrive(e)
            for side in (-1, 1):
                k = p + side * e
                pl.when((k >= 0) & (k < n) & ((e > 0) | (side > 0)))(lambda: feed_forward(k))
            return 0

        lax.fori_loop(0, n, outward, 0)
        up_leave = lambda i: pltpu.make_async_copy(
            up_v.at[pl.ds(pl.multiple_of(i * G, G), G)],
            up_out.at[pl.ds(pl.multiple_of(i * G, G), G)],
            near.at[16 + i],
        )
        down_leave = lambda i: pltpu.make_async_copy(
            down_v.at[pl.ds(pl.multiple_of(i * UT, UT), UT)],
            down_out.at[pl.ds(pl.multiple_of(i * UT, UT), UT)],
            near.at[4 + i],
        )

        def item(i, _):
            @pl.when(i < down_items)
            def _():
                here = pl.ds(pl.multiple_of(i * UT, UT), UT)
                turn[:UT, :] = act[:, here].T

                def one(j, _):
                    at = pl.ds(pl.multiple_of(j * 512, 512), 512)
                    down_v[here, at] = jnp.dot(
                        turn[:UT, :], cot_v[:, at], preferred_element_type=F32
                    ).astype(BF16)
                    return 0

                lax.fori_loop(0, D // 512, one, 0)
                down_leave(i).start()

            @pl.when((i >= down_items) & (i < items))
            def _():
                c = i - down_items
                here = pl.ds(pl.multiple_of(c * G, G), G)
                turn[:G, :] = two[:, here].T

                def one(j, _):
                    at = pl.ds(pl.multiple_of(j * UT, UT), UT)
                    up_v[here, at] = jnp.dot(
                        turn[:G, :], pre[:, at], preferred_element_type=F32
                    ).astype(BF16)
                    return 0

                lax.fori_loop(0, U // UT, one, 0)
                up_leave(c).start()

            return 0

        lax.fori_loop(0, items, item, 0)
        sums_of.total(total)

        def last(k, _):
            ag_over(k, place(k, q)).wait_send()
            leave(k).wait()
            pl.when((k <= p) & (p + 1 < n))(lambda: ag_right(k, place(k, q)).wait_send())
            pl.when((k >= p) & (p > 0))(lambda: ag_left(k, place(k, q)).wait_send())
            return 0

        lax.fori_loop(0, n, last, 0)
        sums_of.finish()
        for i in range(down_items):
            down_leave(i).wait()
        for i in range(S):
            up_leave(i).wait()

    two_grad, result_part, up_part, down_part, pre_sum = call(
        middle_kernel,
        3,
        (
            normed_two,
            up_full.reshape(D, U),
            down_full.reshape(U, D),
            cot_full.reshape(L, D),
            mine(bias_values[6:10], U)[None],
        ),
        [HB] * 4 + [VM],
        [((T, D), F32), ((L, D), BF16), ((D, U), BF16), ((U, D), BF16), ((1, U), F32)],
        [VM, HB, HB, HB, VM],
        [
            pltpu.VMEM((L, D), BF16),
            pltpu.VMEM((D, U), BF16),
            pltpu.VMEM((U, D), BF16),
            pltpu.VMEM((L, D), BF16),
            pltpu.VMEM((L, U), BF16),
            pltpu.VMEM((L, U), BF16),
            pltpu.VMEM((256, L), BF16),
            pltpu.VMEM((L, D), BF16),
            pltpu.VMEM((L, D), BF16),
        ]
        + direct_scratch(n, T, D),
    )
    upstream_float = cotangent[0].astype(F32)
    second_pull = jax.vjp(layer_norm, hidden_in, gain_values[1], bias_values[4])[1]
    hidden_part, gain_two_gradient, shift_two_gradient = second_pull(two_grad)
    hidden_gradient = upstream_float + hidden_part
    hidden_low = hidden_gradient.astype(BF16)

    def fifth_kernel(
        slope_values,
        rows,
        part,
        up,
        down,
        out_w,
        mixed_v,
        att,
        lse,
        begin,
        total,
        up_s,
        down_s,
        grads,
        out_p,
        send,
        recv,
        near,
        hidden,
        att_grad,
        dk,
        dv,
        up_r,
        *room,
    ):
        net = Net(send, recv, near)
        seq, sides = line_of("seq"), both_of("fsdp")
        s = lax.axis_index("seq")
        greet(everyone("seq") + everyone("fsdp"))
        block = lambda i: hidden.at[pl.ds(pl.multiple_of(i * T, T), T)]
        own = net.local(rows, block(s))

        def up_half(k):
            at = pl.ds(k * (S // 2), S // 2)
            return scatter(
                net, sides[k], lambda i: up.at[at, i], up_r.at[at], room[2 + 3 * k : 5 + 3 * k], 0, 12, 20
            )

        def down_half(k):
            at = pl.ds(k * (D // 2), D // 2)
            return scatter(
                net,
                sides[k],
                lambda i: down.at[i, :, at],
                down_s.at[:, at],
                room[8 + 3 * k : 11 + 3 * k],
                28,
                14,
                60,
                True,
            )

        def work():
            yield 49.0
            own.wait()

            def one(i, _):
                here = pl.ds(pl.multiple_of(i * 2 * T, 2 * T), 2 * T)
                att_grad[here, :] = lax.dot_general(
                    hidden[here, :], out_w[...], (((1,), (1,)), ((), ())), preferred_element_type=F32
                ).astype(BF16)
                return 0

            lax.fori_loop(0, S // 2, one, 0)
            attend_back(
                min(256, L), slope_values, begin, mixed_v, att, att_grad, lse, grads, dk, dv
            )

            def two(i, _):
                at = pl.ds(pl.multiple_of(i * 256, 256), 256)
                out_p[:, at] = lax.dot_general(
                    att[...], hidden[:, at], (((0,), (0,)), ((), ())), preferred_element_type=F32
                ).astype(BF16)
                return 0

            lax.fori_loop(0, D // 256, two, 0)

        run(
            net,
            gather(net, seq, rows, block, 0, 14),
            direct(net, seq, lambda i: part.at[i], total, room[:2], lambda d: None, 30, 500, True),
            follow(
                [up_half(0), up_half(1)],
                [lambda: exchange(net, "seq", lambda i: up_r.at[i], lambda i: up_s.at[i], 0, 300)],
            ),
            down_half(0),
            down_half(1),
            work(),
        )

    result_sum, up_share, down_share, mixed_grad, out_grad = call(
        fifth_kernel,
        5,
        (
            slopes,
            hidden_low,
            result_part.reshape(S, T, D),
            up_part.reshape(S, F, R, U),
            down_part.reshape(F, RD, D),
            out_own,
            mixed,
            attended,
            log_sums,
            start,
        ),
        [pl.BlockSpec(memory_space=pltpu.SMEM), HB] + [VM] * 8,
        [
            ((T, D), F32),
            ((S, R, U), BF16),
            ((RD, D), F32),
            ((L, 3 * W), BF16),
            ((W, D), BF16),
        ],
        [VM, HB, VM, VM, VM],
        [
            pltpu.VMEM((L, D), BF16),
            pltpu.VMEM((L, W), BF16),
            pltpu.VMEM((L, 2 * HD), F32),
            pltpu.VMEM((L, 2 * HD), F32),
            pltpu.VMEM((S, R, U), BF16),
        ]
        + direct_scratch(S // 2, T, D)
        + 2 * scatter_scratch(F // 2, S // 2, R, U)
        + 2 * scatter_scratch(F // 2, RD, D // 2),
    )
    output = (hidden_in + result_sum + bias_values[5]).astype(BF16)[None]

    def sixth_kernel(
        grads,
        mix_w,
        first,
        out_p,
        total,
        mix_s,
        out_s,
        sums,
        send,
        recv,
        near,
        one_v,
        part,
        turn,
        mix_p,
        mix_r,
        *room,
    ):
        net = Net(send, recv, near)
        seq, sides = line_of("seq"), both_of("fsdp")
        greet(everyone("seq") + everyone("fsdp"))
        load = net.local(first, one_v)
        block = lambda i: part.at[pl.ds(pl.multiple_of(i * T, T), T)]

        def ready(d):
            here = pl.ds(pl.multiple_of(d * 2 * T, 2 * T), 2 * T)

            def one(i, _):
                at = pl.ds(pl.multiple_of(i * 512, 512), 512)
                part[here, at] = lax.dot_general(
                    grads[here, :], mix_w[at, :], (((1,), (1,)), ((), ())), preferred_element_type=F32
                ).astype(BF16)
                return 0

            lax.fori_loop(0, D // 512, one, 0)

        def mix_half(k):
            at = pl.ds(k * (S // 2), S // 2)
            yield 9.0 + 2 * k
            if k == 0:
                load.wait()

            def one(i, _):
                turn[...] = one_v[:, pl.ds(pl.multiple_of(i * G, G), G)].T
                got = jnp.dot(turn[...], grads[...], preferred_element_type=F32).astype(BF16)
                for f in range(F):
                    mix_p[i, f] = got[f * R : (f + 1) * R]
                return 0

            lax.fori_loop(k * (S // 2), (k + 1) * (S // 2), one, 0)
            yield from scatter(
                net, sides[k], lambda i: mix_p.at[at, i], mix_r.at[at], room[2 + 3 * k : 5 + 3 * k], 14, 8, 14
            )

        def out_half(k):
            at = pl.ds(k * (D // 2), D // 2)
            return scatter(
                net,
                sides[k],
                lambda i: out_p.at[i, :, at],
                out_s.at[:, at],
                room[8 + 3 * k : 11 + 3 * k],
                30,
                12,
                20,
                True,
            )

        def columns():
            yield 16.0
            sums[...] = jnp.zeros_like(sums)

            def one(i, _):
                here = pl.ds(pl.multiple_of(i * T, T), T)
                sums[...] += jnp.sum(grads[here, :].astype(F32), axis=0, keepdims=True)
                return 0

            lax.fori_loop(0, S, one, 0)

        run(
            net,
            direct(net, seq, block, total, room[:2], ready, 0, 75),
            follow(
                [mix_half(0), mix_half(1)],
                [lambda: exchange(net, "seq", lambda i: mix_r.at[i], lambda i: mix_s.at[i], 0, 60)],
            ),
            out_half(0),
            out_half(1),
            columns(),
        )

    one_grad, mix_share, out_share, mixed_sum = call(
        sixth_kernel,
        6,
        (mixed_grad, mix_own, normed, out_grad.reshape(F, R, D)),
        [VM, VM, HB, VM],
        [((T, D), F32), ((S, R, 3 * W), BF16), ((R, D), F32), ((1, 3 * W), F32)],
        [VM, HB, VM, VM],
        [
            pltpu.VMEM((L, D), BF16),
            pltpu.VMEM((L, D), BF16),
            pltpu.VMEM((G, L), BF16),
            pltpu.VMEM((S, F, R, 3 * W), BF16),
            pltpu.VMEM((S, R, 3 * W), BF16),
        ]
        + direct_scratch(S // 2, T, D)
        + 2 * scatter_scratch(F // 2, S // 2, R, 3 * W)
        + 2 * scatter_scratch(F // 2, R, D // 2),
    )
    mixed_sum = mixed_sum[0]
    first_pull = jax.vjp(layer_norm, row_values, gain_values[0], bias_values[0])[1]
    rows_part, gain_one_gradient, shift_one_gradient = first_pull(one_grad)
    tokens_grad = (hidden_gradient + rows_part).astype(BF16)[None]

    def spread(row, count):
        return lax.dynamic_update_slice_in_dim(
            jnp.zeros((count * S * row.shape[0] // count,), F32), row, s_at * row.shape[0], 0
        ).reshape(count, D)

    small_gradient = jnp.concatenate(
        [
            gain_one_gradient[None],
            gain_two_gradient[None],
            shift_one_gradient[None],
            spread(mixed_sum[:W], 1),
            spread(mixed_sum[2 * W :], 1),
            jnp.sum(hidden_gradient, axis=0)[None],
            shift_two_gradient[None],
            jnp.sum(upstream_float, axis=0)[None],
            spread(pre_sum[0], 4),
        ],
        axis=0,
    )
    small_gradient = jnp.pad(
        small_gradient.reshape(12, S, F, R).transpose(1, 2, 0, 3),
        ((0, 0), (0, 0), (0, 4), (0, 128 - R)),
    )

    def last_kernel(vec, total, send, recv, near, got, mid, got_two):
        net = Net(send, recv, near)
        greet(everyone("seq") + everyone("fsdp"))
        for _ in exchange(net, "seq", lambda i: vec.at[i], lambda i: got.at[i]):
            pass
        mid[...] = jnp.sum(got[...], axis=0)
        for _ in exchange(net, "fsdp", lambda i: mid.at[i], lambda i: got_two.at[i]):
            pass
        total[...] = jnp.sum(got_two[...], axis=0)
        run(net)

    (small_share,) = call(
        last_kernel,
        7,
        (small_gradient,),
        [VM],
        [((16, 128), F32)],
        [VM],
        [
            pltpu.VMEM((S, F, 16, 128), F32),
            pltpu.VMEM((F, 16, 128), F32),
            pltpu.VMEM((F, 16, 128), F32),
        ],
    )
    mix_final = mix_share.astype(F32).reshape(S, R, 3, W).transpose(1, 2, 0, 3).reshape(R, 3 * D)
    up_final = up_share.astype(F32).transpose(1, 0, 2).reshape(R, FF)
    step_rate = base_rate / math.sqrt(owners * T)
    vector_step = vector_rate / math.sqrt(owners * T)
    rate_list = (step_rate, step_rate, step_rate, step_rate, vector_step, vector_step)
    masters = (mix_weight, out_weight, up_weight, down_weight, norm_gains, biases)
    shares = (mix_final, out_share, up_final, down_share, small_share[:2, :R], small_share[2:12, :R])
    moments = (mix_moment, out_moment, up_moment, down_moment, gain_moment, bias_moment)
    averages = (mix_average, out_average, up_average, down_average, gain_average, bias_average)
    updated = []
    for master, moment, average, share, rate in zip(masters, moments, averages, shares, rate_list):
        new_moment = mom_decay * moment + share
        new_weight = master - rate * (share + mom_decay * new_moment)
        new_average = avg_decay * average + (1.0 - avg_decay) * new_weight
        updated += [new_moment, new_weight, new_average]
    return (output, tokens_grad, *updated)


def solution(mesh):
    rows = P("fsdp", "seq", None)
    param = P(("seq", "fsdp"), None)
    vector = P(None, ("seq", "fsdp"))
    return jax.shard_map(
        body,
        mesh=mesh,
        in_specs=(rows, P("fsdp", None), rows) + (param,) * 12 + (vector,) * 6,
        out_specs=(rows, rows) + (param,) * 12 + (vector,) * 6,
        check_vma=False,
    )
```

```python
import functools
import heapq
import math

import jax
import jax.numpy as jnp
from jax import lax
from jax.experimental import pallas as pl
from jax.experimental.pallas import tpu as pltpu
from jax.sharding import PartitionSpec as P

D = 2048
HEADS = 32
HD = 64
FF = 8192

epsilon = 1e-05
mom_decay = 0.5
avg_decay = 0.5
base_rate = 0.02
vector_rate = 0.1

BF16 = jnp.bfloat16
F32 = jnp.float32
MESH = pl.DeviceIdType.MESH


class Net:
    def __init__(self, send, recv, near):
        self.send, self.recv, self.near = send, recv, near
        self.used = self.near_used = 0
        self.later = []

    def take(self, count):
        first = self.used
        self.used += count
        assert self.used <= self.send.shape[0]
        return first

    def copy(self, slot, src, dst, dev):
        return pltpu.make_async_remote_copy(
            src_ref=src,
            dst_ref=dst,
            send_sem=self.send.at[slot],
            recv_sem=self.recv.at[slot],
            device_id=dev,
            device_id_type=MESH,
        )

    def local(self, src, dst):
        made = pltpu.make_async_copy(src, dst, self.near.at[self.near_used])
        self.near_used += 1
        made.start()
        return made


def when(cond, act):
    if cond is None:
        act()
    else:
        pl.when(cond)(act)


def greet(partners):
    barrier = pltpu.get_barrier_semaphore()
    for cond, dev in partners:
        when(
            cond,
            functools.partial(
                pl.semaphore_signal, barrier, inc=1, device_id=dev, device_id_type=MESH
            ),
        )
    count = sum(1 for cond, _ in partners if cond is None)
    for cond, _ in partners:
        if cond is not None:
            count = count + jnp.where(cond, 1, 0)
    pl.semaphore_wait(barrier, count)


class Roles:
    def __init__(self, axis, length, place, side, stride, pair):
        self.axis, self.length, self.p, self.q = axis, length, place, side
        self.stride, self.pair = stride, pair

    def index(self, p, q):
        return p * self.stride + q * self.pair

    def dev(self, p, q):
        return {self.axis: self.index(p, q)}

    def partners(self):
        return [
            (None, self.dev(self.p, 1 - self.q)),
            (self.p + 1 < self.length, self.dev(self.p + 1, self.q)),
            (self.p > 0, self.dev(self.p - 1, self.q)),
        ]


def line_of(axis):
    me, size = lax.axis_index(axis), lax.axis_size(axis)
    return Roles(axis, size // 2, me // 2, me % 2, 2, 1)


def both_of(axis):
    me, size = lax.axis_index(axis), lax.axis_size(axis)
    first = line_of(axis)
    if size != 4:
        return first, first
    return first, Roles(axis, 2, me % 2, me // 2, 1, 2)


def everyone(axis):
    me, size = lax.axis_index(axis), lax.axis_size(axis)
    return [(None, {axis: (me + o) % size}) for o in range(1, size)]


def gather(
    net, ro, src, place, at_us=0.0, hop=11.0, over=1.0, hold=False, landed=None
):
    n, p, q = ro.length, ro.p, ro.q
    right, left = net.take(n - 1), net.take(n - 1)
    over_r, over_l, over_own = net.take(n - 1), net.take(n - 1), net.take(1)
    other = ro.dev(p, 1 - q)
    at = lambda k: place(ro.index(k, q))
    across = lambda k: place(ro.index(k, 1 - q))
    ref = lambda j, k: src if j == 0 else at(k)
    go_right = lambda j: net.copy(right + j, ref(j, p - j), at(p - j), ro.dev(p + 1, q))
    go_left = lambda j: net.copy(left + j, ref(j, p + j), at(p + j), ro.dev(p - 1, q))
    pass_r = lambda j: net.copy(over_r + j - 1, at(p - j), at(p - j), other)
    pass_l = lambda j: net.copy(over_l + j - 1, at(p + j), at(p + j), other)
    own = net.copy(over_own, src, at(p), other)
    if hold:
        yield at_us
    pl.when(p + 1 < n)(lambda: go_right(0).start())
    pl.when(p > 0)(lambda: go_left(0).start())
    own.start()

    def complete(j):
        if j == 0:
            net.copy(over_own, src, across(p), other).wait_recv()
            if landed:
                landed(p)
            return

        @pl.when(p - j >= 0)
        def _():
            net.copy(over_r + j - 1, across(p - j), across(p - j), other).wait_recv()
            if landed:
                landed(p - j)

        @pl.when(p + j < n)
        def _():
            net.copy(over_l + j - 1, across(p + j), across(p + j), other).wait_recv()
            if landed:
                landed(p + j)

    for j in range(1, n):
        yield at_us + hop * j

        @pl.when(p - j >= 0)
        def _():
            net.copy(right + j - 1, at(p - j), at(p - j), other).wait_recv()
            if j < n - 1:
                pl.when(p + 1 < n)(lambda: go_right(j).start())
            pass_r(j).start()

        @pl.when(p + j < n)
        def _():
            net.copy(left + j - 1, at(p + j), at(p + j), other).wait_recv()
            if j < n - 1:
                pl.when(p > 0)(lambda: go_left(j).start())
            pass_l(j).start()

        if landed:
            complete(j - 1)

    yield at_us + hop * (n - 1) + over
    for j in range(n - 1 if landed else 0, n):
        complete(j)

    def finish():
        own.wait_send()
        for j in range(n):
            if j < n - 1:
                pl.when((p - j >= 0) & (p + 1 < n))(lambda: go_right(j).wait_send())
                pl.when((p + j < n) & (p > 0))(lambda: go_left(j).wait_send())
            if j > 0:
                pl.when(p - j >= 0)(lambda: pass_r(j).wait_send())
                pl.when(p + j < n)(lambda: pass_l(j).wait_send())

    net.later.append(finish)


def add_rows(dst, srcs, step=16):
    def one(i, _):
        at = pl.ds(pl.multiple_of(i * step, step), step)
        total = srcs[0][at, :].astype(F32)
        for s in srcs[1:]:
            total = total + s[at, :].astype(F32)
        dst[at, :] = total.astype(dst.dtype)
        return 0

    if len(dst.shape) == 3:

        def layer(k, _):
            add_rows(dst.at[k], [s.at[k] for s in srcs], step)
            return 0

        lax.fori_loop(0, dst.shape[0], layer, 0)
    else:
        lax.fori_loop(0, dst.shape[0] // step, one, 0)


def scatter_scratch(ro_length, *shape):
    return [pltpu.VMEM((ro_length, *shape), BF16)] + [
        pltpu.VMEM((ro_length - 1, *shape), BF16)
    ] * 2


def scatter(
    net, ro, part, result, room, at_us=0.0, first=2.0, hop=11.0, hold=False, ready=None
):
    sib, in_r, in_l = room
    n, p, q = ro.length, ro.p, ro.q
    right, left, pair = net.take(n - 1), net.take(n - 1), net.take(n)
    other = ro.dev(p, 1 - q)
    order = []
    for j in range(n):
        order += [d for d in (n - 1 - j, j) if d not in order]
    mine = lambda d: part(ro.index(d, q))
    swap = lambda d: net.copy(pair + d, part(ro.index(d, 1 - q)), sib.at[d], other)
    send_r = lambda j: net.copy(right + j, in_r.at[j], in_r.at[j], ro.dev(p + 1, q))
    send_l = lambda j: net.copy(left + j, in_l.at[j], in_l.at[j], ro.dev(p - 1, q))
    if hold:
        yield at_us
    if n == 2:
        order = [1 - p, p]
    for d in order:
        if ready:
            ready(d)
        swap(d).start()
    for j in range(n - 1):
        yield at_us + first + hop * j
        dr, dl = n - 1 - j, j

        @pl.when(p < dr)
        def _():
            swap(dr).wait_recv()

            @pl.when(p > 0)
            def _():
                send_r(j).wait_recv()
                add_rows(in_r.at[j], [mine(dr), sib.at[dr], in_r.at[j]])

            @pl.when(p == 0)
            def _():
                add_rows(in_r.at[j], [mine(dr), sib.at[dr]])

            send_r(j).start()

        @pl.when(p > dl)
        def _():
            swap(dl).wait_recv()

            @pl.when(p < n - 1)
            def _():
                send_l(j).wait_recv()
                add_rows(in_l.at[j], [mine(dl), sib.at[dl], in_l.at[j]])

            @pl.when(p == n - 1)
            def _():
                add_rows(in_l.at[j], [mine(dl), sib.at[dl]])

            send_l(j).start()

    yield at_us + first + hop * (n - 1)
    from_r, from_l = n - 1 - p, p
    swap(p).wait_recv()

    @pl.when(p > 0)
    def _():
        send_r(from_r).wait_recv()

    @pl.when(p < n - 1)
    def _():
        send_l(from_l).wait_recv()

    @pl.when(p == 0)
    def _():
        add_rows(result, [mine(p), sib.at[p], in_l.at[from_l]])

    @pl.when(p == n - 1)
    def _():
        add_rows(result, [mine(p), sib.at[p], in_r.at[from_r]])

    if n > 2:

        @pl.when((p > 0) & (p < n - 1))
        def _():
            add_rows(result, [mine(p), sib.at[p], in_r.at[from_r], in_l.at[from_l]])

    def finish():
        for d in range(n):
            swap(d).wait_send()
        for j in range(n - 1):
            pl.when(p < n - 1 - j)(lambda: send_r(j).wait_send())
            pl.when(p > j)(lambda: send_l(j).wait_send())

    net.later.append(finish)


def direct_scratch(ro_length, *shape):
    return [
        pltpu.VMEM((ro_length, *shape), BF16),
        pltpu.VMEM((ro_length - 1, *shape), BF16),
    ]


class Direct:
    def __init__(self, net, ro, part, room):
        self.net, self.ro, self.part = net, ro, part
        self.sib, self.came = room
        self.pair, self.slots = net.take(ro.length), net.take(ro.length - 1)

    def mine(self, d):
        return self.part(self.ro.index(d, self.ro.q))

    def swap(self, d):
        ro = self.ro
        away = self.part(ro.index(d, 1 - ro.q))
        return self.net.copy(self.pair + d, away, self.sib.at[d], ro.dev(ro.p, 1 - ro.q))

    def move(self, d):
        ro = self.ro
        k = (d - ro.p + ro.length) % ro.length - 1
        return self.net.copy(self.slots + k, self.mine(d), self.came.at[k], ro.dev(d, ro.q))

    def ship(self, d):
        self.swap(d).wait_recv()
        add_rows(self.mine(d), [self.mine(d), self.sib.at[d]])
        pl.when(d != self.ro.p)(lambda: self.move(d).start())

    def total(self, result):
        ro = self.ro
        for k in range(ro.length - 1):
            self.net.copy(
                self.slots + k, self.came.at[k], self.came.at[k], ro.dev(ro.p, 1 - ro.q)
            ).wait_recv()
        add_rows(result, [self.mine(ro.p)] + [self.came.at[k] for k in range(ro.length - 1)])

    def finish(self):
        for d in range(self.ro.length):
            self.swap(d).wait_send()
            pl.when(d != self.ro.p)(lambda: self.move(d).wait_send())


def direct(net, ro, part, result, room, ready, at_us, last, hold=False):
    work = Direct(net, ro, part, room)
    n = ro.length
    if hold:
        yield at_us
    order = [(ro.p + n // 2 + o) % n for o in range(n)]
    for d in order:
        if ready:
            ready(d)
        work.swap(d).start()
    for d in order:
        work.ship(d)
    yield at_us + last
    work.total(result)
    net.later.append(work.finish)


def relay_scratch(ro_length, *shape):
    if ro_length != 4:
        return direct_scratch(ro_length, *shape) + [pltpu.VMEM((8, 128), BF16)]
    return [pltpu.VMEM((k, *shape), BF16) for k in (4, 2, 2)]


def relay(net, ro, part, result, room, ready, at_us, hop, last, hold=False):
    if ro.length != 4:
        yield from direct(net, ro, part, result, room[:2], ready, at_us, last, hold)
        return
    sib, came, passed = room
    p, q = ro.p, ro.q
    pair, slots, relays = net.take(4), net.take(2), net.take(2)
    other = ro.dev(p, 1 - q)
    mine = lambda d: part(ro.index(d, q))
    swap = lambda d: net.copy(pair + d, part(ro.index(d, 1 - q)), sib.at[d], other)
    inner = (p == 1) | (p == 2)
    mate = (p // 2) * 2 + 1 - p % 2
    pass_on = lambda k: net.copy(relays + k, mine((1 - p // 2) * 2 + k), passed.at[k], ro.dev(mate, q))
    move = lambda d: net.copy(
        slots + jnp.where(d // 2 == p // 2, 0, 1),
        mine(d),
        came.at[jnp.where(d // 2 == p // 2, 0, 1)],
        ro.dev(d, q),
    )
    if hold:
        yield at_us
    far = (1 - p // 2) * 2
    order = [far, far + 1, mate, p]
    for d in order:
        if ready:
            ready(d)
        swap(d).start()
    for d in order:
        swap(d).wait_recv()
        add_rows(mine(d), [mine(d), sib.at[d]])
        if d is far or d is order[1]:
            k = 0 if d is far else 1
            pl.when(jnp.logical_not(inner))(lambda: pass_on(k).start())
        elif d is mate:
            move(d).start()
    for k in range(2):
        yield at_us + hop * (k + 1)

        @pl.when(inner)
        def _():
            pass_on(k).wait_recv()
            add_rows(mine(far + k), [mine(far + k), passed.at[k]])
            move(far + k).start()

    yield at_us + last
    for k in range(2):
        net.copy(slots + k, came.at[k], came.at[k], other).wait_recv()
    add_rows(result, [mine(p), came.at[0], came.at[1]])

    def finish():
        for d in range(4):
            swap(d).wait_send()
        move(mate).wait_send()
        for k in range(2):
            pl.when(inner)(lambda: move(far + k).wait_send())
            pl.when(jnp.logical_not(inner))(lambda: pass_on(k).wait_send())

    net.later.append(finish)


def exchange(net, axis, src, place, at_us=0.0, last=15.0, hold=False):
    me, n = lax.axis_index(axis), lax.axis_size(axis)
    slots = net.take(n - 1)
    if hold:
        yield at_us
    near = net.local(src(me), place(me))
    sent = []
    for o in range(1, n):
        to = (me + o) % n
        sent.append(net.copy(slots + o - 1, src(to), place(me), {axis: to}))
        sent[-1].start()
    yield at_us + last
    near.wait()
    for o in range(1, n):
        at = (me + n - o) % n
        net.copy(slots + o - 1, src(at), place(at), {axis: at}).wait_recv()
    net.later.append(lambda: [s.wait_send() for s in sent])


def run(net, *gens):
    waiting = []
    for order, g in enumerate(gens):
        heapq.heappush(waiting, (0.0, order, g))
    while waiting:
        now, order, g = heapq.heappop(waiting)
        step = next(g, None)
        if step is not None:
            heapq.heappush(waiting, (max(step, now), order, g))
    for act in net.later:
        act()


def merge(gens):
    steps = [next(g, None) for g in gens]
    while any(s is not None for s in steps):
        at, k = min((s, i) for i, s in enumerate(steps) if s is not None)
        yield at
        steps[k] = next(gens[k], None)


def follow(first, makers):
    yield from merge(first)
    yield from merge([m() for m in makers])


VM = pl.BlockSpec(memory_space=pltpu.VMEM)
HB = pl.BlockSpec(memory_space=pl.ANY)


def comm_call(slots, kernel, cid, ins, in_specs, outs, out_specs, room):
    return pl.pallas_call(
        kernel,
        out_shape=[jax.ShapeDtypeStruct(*o) for o in outs],
        in_specs=in_specs,
        out_specs=out_specs,
        scratch_shapes=[
            pltpu.SemaphoreType.DMA((slots,)),
            pltpu.SemaphoreType.DMA((slots,)),
            pltpu.SemaphoreType.DMA((40,)),
        ]
        + room,
        compiler_params=pltpu.CompilerParams(
            collective_id=cid, has_side_effects=True, vmem_limit_bytes=60 << 20
        ),
    )(*ins)


def pair_masks():
    lane = lax.broadcasted_iota(jnp.int32, (1, 2 * HD), 1)
    return [lane < HD, lane >= HD]


def block_scores(key_rows, query_block, start_row, first, slope):
    count, width = key_rows.shape[0], query_block.shape[0]
    raw = lax.dot_general(
        key_rows, query_block, (((1,), (1,)), ((), ())), preferred_element_type=F32
    )
    key_at = lax.broadcasted_iota(jnp.int32, (count, width), 0)
    query_at = lax.broadcasted_iota(jnp.int32, (1, width), 1) + first
    scores = raw - slope * (query_at - key_at).astype(F32)
    allowed = (key_at <= query_at) & (key_at >= start_row)
    return jnp.where(allowed, scores, -1e30)


def attend(block, slopes, start_ref, mixed, out, lse_ref):
    length, width = out.shape
    wide = 2 * HD

    def one_pair(pair, _):
        column = lambda k: pl.ds(pl.multiple_of(k * width + pair * wide, wide), wide)
        q_at, k_at, v_at = column(0), column(1), column(2)
        for half, mask in enumerate(pair_masks()):
            keys = jnp.where(mask, mixed[:, k_at], 0)
            turned = jnp.where(mask, mixed[:, v_at], 0).T
            slope = slopes[2 * pair + half]
            for first in range(0, length, block):
                here, upto = slice(first, first + block), first + block
                query_block = mixed[here, q_at] * BF16(HD**-0.5)
                scores = block_scores(
                    keys[:upto], query_block, start_ref[:, here], first, slope
                )
                top = jnp.max(scores, axis=0, keepdims=True)
                weights = jnp.exp(scores - top)
                total = jnp.sum(weights, axis=0, keepdims=True)
                lse_ref[pair, half : half + 1, here] = top + jnp.log(total)
                probs = (weights * (1.0 / total)).astype(BF16)
                got = jnp.dot(turned[:, :upto], probs, preferred_element_type=F32).T
                if half == 0:
                    out[here, q_at] = got.astype(BF16)
                else:
                    out[here, q_at] = out[here, q_at] + got.astype(BF16)
        return 0

    lax.fori_loop(0, width // wide, one_pair, 0)


def attend_back(block, slopes, start_ref, mixed, att, grad, lse_ref, out, dk, dv):
    length, width = att.shape
    wide = 2 * HD
    pairs = width // wide

    def one_pair(pair, _):
        column = lambda k: pl.ds(pl.multiple_of(k * width + pair * wide, wide), wide)
        q_at, k_at, v_at = column(0), column(1), column(2)
        dk[...] = jnp.zeros_like(dk)
        dv[...] = jnp.zeros_like(dv)
        for half, mask in enumerate(pair_masks()):
            keys = jnp.where(mask, mixed[:, k_at], 0)
            values = jnp.where(mask, mixed[:, v_at], 0)
            turned = keys.T * BF16(HD**-0.5)
            slope = slopes[2 * pair + half]
            for first in range(0, length, block):
                here, upto = slice(first, first + block), first + block
                query_block = jnp.where(mask, mixed[here, q_at], 0) * BF16(HD**-0.5)
                grad_block = jnp.where(mask, grad[here, q_at], 0)
                product = att[here, q_at].astype(F32) * grad_block.astype(F32)
                delta = jnp.sum(product.T, axis=0, keepdims=True)
                scores = block_scores(
                    keys[:upto], query_block, start_ref[:, here], first, slope
                )
                probs = jnp.exp(scores - lse_ref[pair, half : half + 1, here])
                prob_grad = lax.dot_general(
                    values[:upto], grad_block, (((1,), (1,)), ((), ())), preferred_element_type=F32
                )
                score_grad = (probs * (prob_grad - delta)).astype(BF16)
                dv[:upto, :] += jnp.dot(
                    probs.astype(BF16), grad_block, preferred_element_type=F32
                )
                dk[:upto, :] += jnp.dot(score_grad, query_block, preferred_element_type=F32)
                got = jnp.dot(turned[:, :upto], score_grad, preferred_element_type=F32).T
                if half == 0:
                    out[here, q_at] = got.astype(BF16)
                else:
                    out[here, q_at] = out[here, q_at] + got.astype(BF16)
        out[:, k_at] = dk[...].astype(BF16)
        out[:, v_at] = dv[...].astype(BF16)
        return 0

    lax.fori_loop(0, pairs, one_pair, 0)


def layer_norm(values, gain_row, shift_row):
    centred = values - jnp.mean(values, axis=-1, keepdims=True)
    spread = jnp.mean(centred * centred, axis=-1, keepdims=True)
    return centred * lax.rsqrt(spread + epsilon) * gain_row + shift_row


def gelu_exact(values):
    return jax.nn.gelu(values, approximate=False)


def body(
    tokens,
    segments,
    cotangent,
    mix_weight,
    mix_moment,
    mix_average,
    out_weight,
    out_moment,
    out_average,
    up_weight,
    up_moment,
    up_average,
    down_weight,
    down_moment,
    down_average,
    norm_gains,
    gain_moment,
    gain_average,
    biases,
    bias_moment,
    bias_average,
):
    S, F = lax.axis_size("seq"), lax.axis_size("fsdp")
    owners = S * F
    s_at = lax.axis_index("seq")
    T = tokens.shape[1]
    L = T * S
    R = D // owners
    RD = FF // owners
    W = D // S
    U = FF // S
    heads = HEADS // S
    slots = 20 * max(S, F)
    call = functools.partial(comm_call, slots)

    head_ids = s_at * heads + jnp.arange(heads, dtype=jnp.int32) + 1
    slopes = jnp.exp2(-8.0 * head_ids.astype(F32) / HEADS)
    documents = segments[0]
    start = jnp.sum(documents[:, None] < documents[None, :], axis=0, dtype=jnp.int32)[None]

    mix_low = mix_weight.astype(BF16).reshape(R, 3, S, W).transpose(2, 0, 1, 3).reshape(S, R, 3 * W)
    up_low = up_weight.astype(BF16).reshape(R, S, U).transpose(1, 0, 2)
    out_low = out_weight.astype(BF16)
    down_low = down_weight.astype(BF16)
    small = jnp.concatenate([norm_gains, biases], axis=0).astype(BF16).astype(F32)
    place_at = (s_at * F + lax.axis_index("fsdp")) * R % 128
    small = lax.dynamic_update_slice(jnp.zeros((16, 128), F32), small, (0, place_at))

    G = D // S
    n = S // 2

    def first_kernel(
        slope_values,
        tok,
        mix,
        out,
        vec,
        up,
        cot,
        down,
        begin,
        total,
        vecs,
        mix_out,
        out_w,
        up_f,
        down_f,
        cot_f,
        one_out,
        mixed,
        att,
        lse,
        send,
        recv,
        near,
        tok_v,
        one_v,
        mix_v,
        out_v,
        vec_f,
        up_r,
        part,
        *room,
    ):
        net = Net(send, recv, near)
        seq, sides = line_of("seq"), both_of("fsdp")
        s, f = lax.axis_index("seq"), lax.axis_index("fsdp")
        block = lambda ref, i: ref.at[pl.ds(pl.multiple_of(i * T, T), T)]
        owned = [net.local(out, out_v.at[f]), net.local(cot, cot_f.at[s]), net.local(down, down_f.at[f])]
        tok_own = net.local(tok, block(tok_v, s))
        vec_own = net.local(vec, vec_f.at[s, f])
        greet(everyone("seq") + everyone("fsdp"))

        def mix_half(k):
            at = pl.ds(k * (S // 2), S // 2)
            return lambda: gather(
                net, sides[k], mix_v.at[at, f], lambda i: mix_v.at[at, i], 20, 13, 13
            )

        def out_half(k):
            at = pl.ds(k * (D // 2), D // 2)
            return gather(net, sides[k], out.at[:, at], lambda i: out_v.at[i, :, at], 0, 5, 5)

        def down_half(k):
            at = pl.ds(k * (RD // 2), RD // 2)
            return gather(
                net, sides[k], down.at[at], lambda i: down_f.at[i, at], 46, 24, 28, True
            )

        def up_half(k):
            at = pl.ds(k * (S // 2), S // 2)
            return lambda: gather(
                net, sides[k], up_r.at[at], lambda i: up_f.at[at, i], 86, 17, 25
            )

        def vec_next():
            vec_own.wait()
            return gather(net, sides[0], vec_f.at[:, f], lambda i: vec_f.at[:, i], 6, 1, 1)

        def vec_all():
            yield from follow(
                [gather(net, seq, vec, lambda i: vec_f.at[i, f], 0, 2, 1)], [vec_next]
            )
            each = 128 // R
            for c in range(D // 128):
                pieces = [
                    vec_f[i // F, i % F] for i in range(c * each, (c + 1) * each)
                ]
                vecs[:, c * 128 : (c + 1) * 128] = functools.reduce(jnp.add, pieces)
            tok_own.wait()

        def norm(k):
            step = 32

            def one(i, _):
                here = pl.ds(pl.multiple_of(k * 2 * T + i * step, step), step)
                one_v[here, :] = layer_norm(
                    tok_v[here, :].astype(F32), vecs[0:1, :], vecs[2:3, :]
                ).astype(BF16)
                return 0

            lax.fori_loop(0, 2 * T // step, one, 0)

        leave = lambda: [
            pltpu.make_async_copy(one_v, one_out, near.at[30]),
            pltpu.make_async_copy(mix_v, mix_out, near.at[31]),
            pltpu.make_async_copy(out_v, out_w, near.at[32]),
        ]

        def project():
            yield 58.0
            owned[0].wait()
            for made in leave():
                made.start()
            for c in range(3):
                if c == 1:
                    bias = jnp.zeros((1, W), F32)
                else:
                    bias = vecs[3 + c // 2 : 4 + c // 2, pl.ds(pl.multiple_of(s * W, W), W)]
                at = slice(c * W, (c + 1) * W)

                def one(i, _):
                    here = pl.ds(pl.multiple_of(i * 2 * T, 2 * T), 2 * T)
                    mixed[here, at] = (
                        jnp.dot(
                            one_v[here, :],
                            mix_v[:, :, :, at].reshape(D, W),
                            preferred_element_type=F32,
                        )
                        + bias
                    ).astype(BF16)
                    return 0

                lax.fori_loop(0, n, one, 0)
            yield 62.0
            attend(min(256, L), slope_values, begin, mixed, att, lse)

        def ready(d):
            here = pl.ds(pl.multiple_of(d * 2 * T, 2 * T), 2 * T)

            def one(i, _):
                at = pl.ds(pl.multiple_of(i * 512, 512), 512)
                part[here, at] = jnp.dot(
                    att[here, :], out_v[:, :, at].reshape(W, 512), preferred_element_type=F32
                ).astype(BF16)
                return 0

            lax.fori_loop(0, D // 512, one, 0)

        run(
            net,
            follow(
                [exchange(net, "seq", lambda i: mix.at[i], lambda i: mix_v.at[i, f], 0, 18)],
                [mix_half(0), mix_half(1)],
            ),
            vec_all(),
            out_half(0),
            out_half(1),
            gather(net, seq, tok, lambda i: block(tok_v, i), 19, 12, 1, True, norm),
            down_half(0),
            down_half(1),
            follow(
                [exchange(net, "seq", lambda i: up.at[i], lambda i: up_r.at[i], 57, 28, True)],
                [up_half(0), up_half(1)],
            ),
            project(),
            gather(net, seq, cot, lambda i: cot_f.at[i], 57, 17, hold=True),
            relay(net, seq, lambda i: block(part, i), total, room, ready, 74, 16, 60, True),
        )
        up_own = [net.local(up_r, up_f.at[:, f])]
        for made in owned[1:] + leave() + up_own:
            made.wait()

    (
        attn_sum,
        vectors,
        mix_full,
        out_full,
        up_full,
        down_full,
        cot_full,
        normed,
        mixed,
        attended,
        log_sums,
    ) = call(
        first_kernel,
        1,
        (
            slopes,
            tokens[0],
            mix_low,
            out_low,
            small,
            up_low,
            cotangent[0],
            down_low,
            start,
        ),
        [pl.BlockSpec(memory_space=pltpu.SMEM), HB, HB, HB, VM, HB, HB, HB, VM],
        [
            ((T, D), F32),
            ((16, D), F32),
            ((S, F, R, 3 * W), BF16),
            ((F, R, D), BF16),
            ((S, F, R, U), BF16),
            ((F, RD, D), BF16),
            ((S, T, D), BF16),
            ((L, D), BF16),
            ((L, 3 * W), BF16),
            ((L, W), BF16),
            ((heads // 2, 2, L), F32),
        ],
        [VM, VM, HB, HB, HB, HB, HB, HB, VM, VM, VM],
        [
            pltpu.VMEM((L, D), BF16),
            pltpu.VMEM((L, D), BF16),
            pltpu.VMEM((S, F, R, 3 * W), BF16),
            pltpu.VMEM((F, R, D), BF16),
            pltpu.VMEM((S, F, 16, 128), F32),
            pltpu.VMEM((S, R, U), BF16),
            pltpu.VMEM((L, D), BF16),
        ]
        + relay_scratch(n, T, D),
    )
    gain_values, bias_values = vectors[:2], vectors[2:12]
    mine = lambda row, width: lax.dynamic_slice_in_dim(row.reshape(-1), s_at * width, width)
    mix_own = mix_full.reshape(D, 3 * W)
    out_own = out_full.reshape(W, D)
    row_values = tokens[0].astype(F32)
    hidden_in = row_values + attn_sum + bias_values[3]
    normed_two = layer_norm(hidden_in, gain_values[1], bias_values[4]).astype(BF16)

    B = 2 * T
    UT = min(256, U)
    down_items, items = U // UT, U // UT + S

    def middle_kernel(
        rows,
        up,
        down,
        cot,
        bias,
        total,
        result_out,
        up_out,
        down_out,
        sums,
        send,
        recv,
        near,
        two,
        up_v,
        down_v,
        cot_v,
        act,
        pre,
        turn,
        part_n,
        part_r,
        *room,
    ):
        net = Net(send, recv, near)
        ro = line_of("seq")
        p, q = ro.p, ro.q
        other = ro.dev(p, 1 - q)
        loads = [net.local(up, up_v), net.local(down, down_v), net.local(cot, cot_v)]
        sums[...] = jnp.zeros_like(sums)
        greet(ro.partners())
        block = lambda ref, i: ref.at[pl.ds(pl.multiple_of(i * T, T), T)]
        place = lambda k, side: block(two, ro.index(k, side))
        loads.append(net.local(rows, place(p, q)))
        ag_r, ag_l, over = net.take(n - 1), net.take(n - 1), net.take(n)
        sums_of = Direct(net, ro, lambda i: block(part_n, i), room)
        ag_right = lambda k, src: net.copy(ag_r + p - k, src, place(k, q), ro.dev(p + 1, q))
        ag_left = lambda k, src: net.copy(ag_l + k - p, src, place(k, q), ro.dev(p - 1, q))
        ag_over = lambda k, src: net.copy(over + k, src, place(k, q), other)
        leave = lambda k: pltpu.make_async_copy(
            part_r.at[pl.ds(pl.multiple_of(k * B, B), B)],
            result_out.at[pl.ds(pl.multiple_of(k * B, B), B)],
            near.at[8 + k],
        )

        pl.when(p + 1 < n)(lambda: ag_right(p, rows).start())
        pl.when(p > 0)(lambda: ag_left(p, rows).start())
        ag_over(p, rows).start()
        for made in loads:
            made.wait()

        def arrive(e):
            @pl.when((e > 0) & (p - e >= 0))
            def _():
                k = p - e
                net.copy(ag_r + e - 1, place(k, q), place(k, q), other).wait_recv()
                pl.when(p + 1 < n)(lambda: ag_right(k, place(k, q)).start())
                ag_over(k, place(k, q)).start()

            @pl.when((e > 0) & (p + e < n))
            def _():
                k = p + e
                net.copy(ag_l + e - 1, place(k, q), place(k, q), other).wait_recv()
                pl.when(p > 0)(lambda: ag_left(k, place(k, q)).start())
                ag_over(k, place(k, q)).start()

        def feed_forward(k):
            net.copy(over + k, place(k, 1 - q), place(k, 1 - q), other).wait_recv()
            here = pl.ds(pl.multiple_of(k * B, B), B)

            def hidden(i, _):
                at = pl.ds(pl.multiple_of(i * UT, UT), UT)
                value = jnp.dot(two[here, :], up_v[:, at], preferred_element_type=F32) + bias[:, at]
                chance = 0.5 + 0.5 * lax.erf(value * 0.5**0.5)
                slope = chance + value * (jnp.exp(value * value * -0.5) * (2 * math.pi) ** -0.5)
                act[here, at] = (value * chance).astype(BF16)
                grad = lax.dot_general(
                    cot_v[here, :], down_v[at, :], (((1,), (1,)), ((), ())), preferred_element_type=F32
                )
                low = (grad * slope).astype(BF16)
                pre[here, at] = low
                sums[:, at] += jnp.sum(low.astype(F32), axis=0, keepdims=True)
                return 0

            lax.fori_loop(0, U // UT, hidden, 0)

            def back(i, _):
                at = pl.ds(pl.multiple_of(i * 512, 512), 512)
                part_n[here, at] = lax.dot_general(
                    pre[here, :], up_v[at, :], (((1,), (1,)), ((), ())), preferred_element_type=F32
                ).astype(BF16)
                return 0

            lax.fori_loop(0, D // 512, back, 0)
            sums_of.swap(k).start()

            def forth(i, _):
                at = pl.ds(pl.multiple_of(i * 512, 512), 512)
                part_r[here, at] = jnp.dot(
                    act[here, :], down_v[:, at], preferred_element_type=F32
                ).astype(BF16)
                return 0

            lax.fori_loop(0, D // 512, forth, 0)
            leave(k).start()
            sums_of.ship(k)

        def outward(e, _):
            arrive(e)
            for side in (-1, 1):
                k = p + side * e
                pl.when((k >= 0) & (k < n) & ((e > 0) | (side > 0)))(lambda: feed_forward(k))
            return 0

        lax.fori_loop(0, n, outward, 0)
        up_leave = lambda i: pltpu.make_async_copy(
            up_v.at[pl.ds(pl.multiple_of(i * G, G), G)],
            up_out.at[pl.ds(pl.multiple_of(i * G, G), G)],
            near.at[16 + i],
        )
        down_leave = lambda i: pltpu.make_async_copy(
            down_v.at[pl.ds(pl.multiple_of(i * UT, UT), UT)],
            down_out.at[pl.ds(pl.multiple_of(i * UT, UT), UT)],
            near.at[4 + i],
        )

        def item(i, _):
            @pl.when(i < down_items)
            def _():
                here = pl.ds(pl.multiple_of(i * UT, UT), UT)
                turn[:UT, :] = act[:, here].T

                def one(j, _):
                    at = pl.ds(pl.multiple_of(j * 512, 512), 512)
                    down_v[here, at] = jnp.dot(
                        turn[:UT, :], cot_v[:, at], preferred_element_type=F32
                    ).astype(BF16)
                    return 0

                lax.fori_loop(0, D // 512, one, 0)
                down_leave(i).start()

            @pl.when((i >= down_items) & (i < items))
            def _():
                c = i - down_items
                here = pl.ds(pl.multiple_of(c * G, G), G)
                turn[:G, :] = two[:, here].T

                def one(j, _):
                    at = pl.ds(pl.multiple_of(j * UT, UT), UT)
                    up_v[here, at] = jnp.dot(
                        turn[:G, :], pre[:, at], preferred_element_type=F32
                    ).astype(BF16)
                    return 0

                lax.fori_loop(0, U // UT, one, 0)
                up_leave(c).start()

            return 0

        lax.fori_loop(0, items, item, 0)
        sums_of.total(total)

        def last(k, _):
            ag_over(k, place(k, q)).wait_send()
            leave(k).wait()
            pl.when((k <= p) & (p + 1 < n))(lambda: ag_right(k, place(k, q)).wait_send())
            pl.when((k >= p) & (p > 0))(lambda: ag_left(k, place(k, q)).wait_send())
            return 0

        lax.fori_loop(0, n, last, 0)
        sums_of.finish()
        for i in range(down_items):
            down_leave(i).wait()
        for i in range(S):
            up_leave(i).wait()

    two_grad, result_part, up_part, down_part, pre_sum = call(
        middle_kernel,
        3,
        (
            normed_two,
            up_full.reshape(D, U),
            down_full.reshape(U, D),
            cot_full.reshape(L, D),
            mine(bias_values[6:10], U)[None],
        ),
        [HB] * 4 + [VM],
        [((T, D), F32), ((L, D), BF16), ((D, U), BF16), ((U, D), BF16), ((1, U), F32)],
        [VM, HB, HB, HB, VM],
        [
            pltpu.VMEM((L, D), BF16),
            pltpu.VMEM((D, U), BF16),
            pltpu.VMEM((U, D), BF16),
            pltpu.VMEM((L, D), BF16),
            pltpu.VMEM((L, U), BF16),
            pltpu.VMEM((L, U), BF16),
            pltpu.VMEM((256, L), BF16),
            pltpu.VMEM((L, D), BF16),
            pltpu.VMEM((L, D), BF16),
        ]
        + direct_scratch(n, T, D),
    )
    upstream_float = cotangent[0].astype(F32)
    second_pull = jax.vjp(layer_norm, hidden_in, gain_values[1], bias_values[4])[1]
    hidden_part, gain_two_gradient, shift_two_gradient = second_pull(two_grad)
    hidden_gradient = upstream_float + hidden_part
    hidden_low = hidden_gradient.astype(BF16)

    def fifth_kernel(
        slope_values,
        rows,
        part,
        up,
        down,
        out_w,
        mixed_v,
        att,
        lse,
        begin,
        total,
        up_s,
        down_s,
        grads,
        out_p,
        send,
        recv,
        near,
        hidden,
        att_grad,
        dk,
        dv,
        up_r,
        *room,
    ):
        net = Net(send, recv, near)
        seq, sides = line_of("seq"), both_of("fsdp")
        s = lax.axis_index("seq")
        greet(everyone("seq") + everyone("fsdp"))
        block = lambda i: hidden.at[pl.ds(pl.multiple_of(i * T, T), T)]
        own = net.local(rows, block(s))

        def up_half(k):
            at = pl.ds(k * (S // 2), S // 2)
            return scatter(
                net, sides[k], lambda i: up.at[at, i], up_r.at[at], room[3 + 3 * k : 6 + 3 * k], 0, 12, 20
            )

        def down_half(k):
            at = pl.ds(k * (D // 2), D // 2)
            return scatter(
                net,
                sides[k],
                lambda i: down.at[i, :, at],
                down_s.at[:, at],
                room[9 + 3 * k : 12 + 3 * k],
                28,
                14,
                60,
                True,
            )

        def work():
            yield 49.0
            own.wait()

            def one(i, _):
                here = pl.ds(pl.multiple_of(i * 2 * T, 2 * T), 2 * T)
                att_grad[here, :] = lax.dot_general(
                    hidden[here, :], out_w[...], (((1,), (1,)), ((), ())), preferred_element_type=F32
                ).astype(BF16)
                return 0

            lax.fori_loop(0, S // 2, one, 0)
            attend_back(
                min(256, L), slope_values, begin, mixed_v, att, att_grad, lse, grads, dk, dv
            )

            def two(i, _):
                at = pl.ds(pl.multiple_of(i * 256, 256), 256)
                out_p[:, at] = lax.dot_general(
                    att[...], hidden[:, at], (((0,), (0,)), ((), ())), preferred_element_type=F32
                ).astype(BF16)
                return 0

            lax.fori_loop(0, D // 256, two, 0)

        run(
            net,
            gather(net, seq, rows, block, 0, 14),
            relay(net, seq, lambda i: part.at[i], total, room[:3], None, 30, 14, 500, True),
            follow(
                [up_half(0), up_half(1)],
                [lambda: exchange(net, "seq", lambda i: up_r.at[i], lambda i: up_s.at[i], 0, 300)],
            ),
            down_half(0),
            down_half(1),
            work(),
        )

    result_sum, up_share, down_share, mixed_grad, out_grad = call(
        fifth_kernel,
        5,
        (
            slopes,
            hidden_low,
            result_part.reshape(S, T, D),
            up_part.reshape(S, F, R, U),
            down_part.reshape(F, RD, D),
            out_own,
            mixed,
            attended,
            log_sums,
            start,
        ),
        [pl.BlockSpec(memory_space=pltpu.SMEM), HB] + [VM] * 8,
        [
            ((T, D), F32),
            ((S, R, U), BF16),
            ((RD, D), F32),
            ((L, 3 * W), BF16),
            ((W, D), BF16),
        ],
        [VM, HB, VM, VM, VM],
        [
            pltpu.VMEM((L, D), BF16),
            pltpu.VMEM((L, W), BF16),
            pltpu.VMEM((L, 2 * HD), F32),
            pltpu.VMEM((L, 2 * HD), F32),
            pltpu.VMEM((S, R, U), BF16),
        ]
        + relay_scratch(S // 2, T, D)
        + 2 * scatter_scratch(F // 2, S // 2, R, U)
        + 2 * scatter_scratch(F // 2, RD, D // 2),
    )
    output = (hidden_in + result_sum + bias_values[5]).astype(BF16)[None]

    def sixth_kernel(
        grads,
        mix_w,
        first,
        out_p,
        total,
        mix_s,
        out_s,
        sums,
        send,
        recv,
        near,
        one_v,
        part,
        turn,
        mix_p,
        mix_r,
        *room,
    ):
        net = Net(send, recv, near)
        seq, sides = line_of("seq"), both_of("fsdp")
        greet(everyone("seq") + everyone("fsdp"))
        load = net.local(first, one_v)
        block = lambda i: part.at[pl.ds(pl.multiple_of(i * T, T), T)]

        def ready(d):
            here = pl.ds(pl.multiple_of(d * 2 * T, 2 * T), 2 * T)

            def one(i, _):
                at = pl.ds(pl.multiple_of(i * 512, 512), 512)
                part[here, at] = lax.dot_general(
                    grads[here, :], mix_w[at, :], (((1,), (1,)), ((), ())), preferred_element_type=F32
                ).astype(BF16)
                return 0

            lax.fori_loop(0, D // 512, one, 0)

        def mix_half(k):
            at = pl.ds(k * (S // 2), S // 2)
            yield 9.0 + 2 * k
            if k == 0:
                load.wait()

            def one(i, _):
                turn[...] = one_v[:, pl.ds(pl.multiple_of(i * G, G), G)].T
                got = jnp.dot(turn[...], grads[...], preferred_element_type=F32).astype(BF16)
                for f in range(F):
                    mix_p[i, f] = got[f * R : (f + 1) * R]
                return 0

            lax.fori_loop(k * (S // 2), (k + 1) * (S // 2), one, 0)
            yield from scatter(
                net, sides[k], lambda i: mix_p.at[at, i], mix_r.at[at], room[3 + 3 * k : 6 + 3 * k], 14, 8, 14
            )

        def out_half(k):
            at = pl.ds(k * (D // 2), D // 2)
            return scatter(
                net,
                sides[k],
                lambda i: out_p.at[i, :, at],
                out_s.at[:, at],
                room[9 + 3 * k : 12 + 3 * k],
                30,
                12,
                20,
                True,
            )

        def columns():
            yield 16.0
            sums[...] = jnp.zeros_like(sums)

            def one(i, _):
                here = pl.ds(pl.multiple_of(i * T, T), T)
                sums[...] += jnp.sum(grads[here, :].astype(F32), axis=0, keepdims=True)
                return 0

            lax.fori_loop(0, S, one, 0)

        run(
            net,
            relay(net, seq, block, total, room[:3], ready, 0, 15, 75),
            follow(
                [mix_half(0), mix_half(1)],
                [lambda: exchange(net, "seq", lambda i: mix_r.at[i], lambda i: mix_s.at[i], 0, 60)],
            ),
            out_half(0),
            out_half(1),
            columns(),
        )

    one_grad, mix_share, out_share, mixed_sum = call(
        sixth_kernel,
        6,
        (mixed_grad, mix_own, normed, out_grad.reshape(F, R, D)),
        [VM, VM, HB, VM],
        [((T, D), F32), ((S, R, 3 * W), BF16), ((R, D), F32), ((1, 3 * W), F32)],
        [VM, HB, VM, VM],
        [
            pltpu.VMEM((L, D), BF16),
            pltpu.VMEM((L, D), BF16),
            pltpu.VMEM((G, L), BF16),
            pltpu.VMEM((S, F, R, 3 * W), BF16),
            pltpu.VMEM((S, R, 3 * W), BF16),
        ]
        + relay_scratch(S // 2, T, D)
        + 2 * scatter_scratch(F // 2, S // 2, R, 3 * W)
        + 2 * scatter_scratch(F // 2, R, D // 2),
    )
    mixed_sum = mixed_sum[0]
    first_pull = jax.vjp(layer_norm, row_values, gain_values[0], bias_values[0])[1]
    rows_part, gain_one_gradient, shift_one_gradient = first_pull(one_grad)
    tokens_grad = (hidden_gradient + rows_part).astype(BF16)[None]

    def spread(row, count):
        return lax.dynamic_update_slice_in_dim(
            jnp.zeros((count * S * row.shape[0] // count,), F32), row, s_at * row.shape[0], 0
        ).reshape(count, D)

    small_gradient = jnp.concatenate(
        [
            gain_one_gradient[None],
            gain_two_gradient[None],
            shift_one_gradient[None],
            spread(mixed_sum[:W], 1),
            spread(mixed_sum[2 * W :], 1),
            jnp.sum(hidden_gradient, axis=0)[None],
            shift_two_gradient[None],
            jnp.sum(upstream_float, axis=0)[None],
            spread(pre_sum[0], 4),
        ],
        axis=0,
    )
    small_gradient = jnp.pad(
        small_gradient.reshape(12, S, F, R).transpose(1, 2, 0, 3),
        ((0, 0), (0, 0), (0, 4), (0, 128 - R)),
    )

    def last_kernel(vec, total, send, recv, near, got, mid, got_two):
        net = Net(send, recv, near)
        greet(everyone("seq") + everyone("fsdp"))
        for _ in exchange(net, "seq", lambda i: vec.at[i], lambda i: got.at[i]):
            pass
        mid[...] = jnp.sum(got[...], axis=0)
        for _ in exchange(net, "fsdp", lambda i: mid.at[i], lambda i: got_two.at[i]):
            pass
        total[...] = jnp.sum(got_two[...], axis=0)
        run(net)

    (small_share,) = call(
        last_kernel,
        7,
        (small_gradient,),
        [VM],
        [((16, 128), F32)],
        [VM],
        [
            pltpu.VMEM((S, F, 16, 128), F32),
            pltpu.VMEM((F, 16, 128), F32),
            pltpu.VMEM((F, 16, 128), F32),
        ],
    )
    mix_final = mix_share.astype(F32).reshape(S, R, 3, W).transpose(1, 2, 0, 3).reshape(R, 3 * D)
    up_final = up_share.astype(F32).transpose(1, 0, 2).reshape(R, FF)
    step_rate = base_rate / math.sqrt(owners * T)
    vector_step = vector_rate / math.sqrt(owners * T)
    rate_list = (step_rate, step_rate, step_rate, step_rate, vector_step, vector_step)
    masters = (mix_weight, out_weight, up_weight, down_weight, norm_gains, biases)
    shares = (mix_final, out_share, up_final, down_share, small_share[:2, :R], small_share[2:12, :R])
    moments = (mix_moment, out_moment, up_moment, down_moment, gain_moment, bias_moment)
    averages = (mix_average, out_average, up_average, down_average, gain_average, bias_average)
    updated = []
    for master, moment, average, share, rate in zip(masters, moments, averages, shares, rate_list):
        new_moment = mom_decay * moment + share
        new_weight = master - rate * (share + mom_decay * new_moment)
        new_average = avg_decay * average + (1.0 - avg_decay) * new_weight
        updated += [new_moment, new_weight, new_average]
    return (output, tokens_grad, *updated)


def solution(mesh):
    rows = P("fsdp", "seq", None)
    param = P(("seq", "fsdp"), None)
    vector = P(None, ("seq", "fsdp"))
    return jax.shard_map(
        body,
        mesh=mesh,
        in_specs=(rows, P("fsdp", None), rows) + (param,) * 12 + (vector,) * 6,
        out_specs=(rows, rows) + (param,) * 12 + (vector,) * 6,
        check_vma=False,
    )
```

```python
import functools
import heapq
import math

import jax
import jax.numpy as jnp
from jax import lax
from jax.experimental import pallas as pl
from jax.experimental.pallas import tpu as pltpu
from jax.sharding import PartitionSpec as P

D = 2048
HEADS = 32
HD = 64
FF = 8192

epsilon = 1e-05
mom_decay = 0.5
avg_decay = 0.5
base_rate = 0.02
vector_rate = 0.1

BF16 = jnp.bfloat16
F32 = jnp.float32
MESH = pl.DeviceIdType.MESH


class Net:
    def __init__(self, send, recv, near):
        self.send, self.recv, self.near = send, recv, near
        self.used = self.near_used = 0
        self.later = []

    def take(self, count):
        first = self.used
        self.used += count
        assert self.used <= self.send.shape[0]
        return first

    def copy(self, slot, src, dst, dev):
        return pltpu.make_async_remote_copy(
            src_ref=src,
            dst_ref=dst,
            send_sem=self.send.at[slot],
            recv_sem=self.recv.at[slot],
            device_id=dev,
            device_id_type=MESH,
        )

    def local(self, src, dst):
        made = pltpu.make_async_copy(src, dst, self.near.at[self.near_used])
        self.near_used += 1
        made.start()
        return made


def when(cond, act):
    if cond is None:
        act()
    else:
        pl.when(cond)(act)


def greet(partners):
    barrier = pltpu.get_barrier_semaphore()
    for cond, dev in partners:
        when(
            cond,
            functools.partial(
                pl.semaphore_signal, barrier, inc=1, device_id=dev, device_id_type=MESH
            ),
        )
    count = sum(1 for cond, _ in partners if cond is None)
    for cond, _ in partners:
        if cond is not None:
            count = count + jnp.where(cond, 1, 0)
    pl.semaphore_wait(barrier, count)


class Roles:
    def __init__(self, axis, length, place, side, stride, pair):
        self.axis, self.length, self.p, self.q = axis, length, place, side
        self.stride, self.pair = stride, pair

    def index(self, p, q):
        return p * self.stride + q * self.pair

    def dev(self, p, q):
        return {self.axis: self.index(p, q)}

    def partners(self):
        return [
            (None, self.dev(self.p, 1 - self.q)),
            (self.p + 1 < self.length, self.dev(self.p + 1, self.q)),
            (self.p > 0, self.dev(self.p - 1, self.q)),
        ]


def line_of(axis):
    me, size = lax.axis_index(axis), lax.axis_size(axis)
    return Roles(axis, size // 2, me // 2, me % 2, 2, 1)


def both_of(axis):
    me, size = lax.axis_index(axis), lax.axis_size(axis)
    first = line_of(axis)
    if size != 4:
        return first, first
    return first, Roles(axis, 2, me % 2, me // 2, 1, 2)


def everyone(axis):
    me, size = lax.axis_index(axis), lax.axis_size(axis)
    return [(None, {axis: (me + o) % size}) for o in range(1, size)]


def gather(
    net, ro, src, place, at_us=0.0, hop=11.0, over=1.0, hold=False, landed=None
):
    n, p, q = ro.length, ro.p, ro.q
    right, left = net.take(n - 1), net.take(n - 1)
    over_r, over_l, over_own = net.take(n - 1), net.take(n - 1), net.take(1)
    other = ro.dev(p, 1 - q)
    at = lambda k: place(ro.index(k, q))
    across = lambda k: place(ro.index(k, 1 - q))
    ref = lambda j, k: src if j == 0 else at(k)
    go_right = lambda j: net.copy(right + j, ref(j, p - j), at(p - j), ro.dev(p + 1, q))
    go_left = lambda j: net.copy(left + j, ref(j, p + j), at(p + j), ro.dev(p - 1, q))
    pass_r = lambda j: net.copy(over_r + j - 1, at(p - j), at(p - j), other)
    pass_l = lambda j: net.copy(over_l + j - 1, at(p + j), at(p + j), other)
    own = net.copy(over_own, src, at(p), other)
    if hold:
        yield at_us
    pl.when(p + 1 < n)(lambda: go_right(0).start())
    pl.when(p > 0)(lambda: go_left(0).start())
    own.start()

    def complete(j):
        if j == 0:
            net.copy(over_own, src, across(p), other).wait_recv()
            if landed:
                landed(p)
            return

        @pl.when(p - j >= 0)
        def _():
            net.copy(over_r + j - 1, across(p - j), across(p - j), other).wait_recv()
            if landed:
                landed(p - j)

        @pl.when(p + j < n)
        def _():
            net.copy(over_l + j - 1, across(p + j), across(p + j), other).wait_recv()
            if landed:
                landed(p + j)

    for j in range(1, n):
        yield at_us + hop * j

        @pl.when(p - j >= 0)
        def _():
            net.copy(right + j - 1, at(p - j), at(p - j), other).wait_recv()
            if j < n - 1:
                pl.when(p + 1 < n)(lambda: go_right(j).start())
            pass_r(j).start()

        @pl.when(p + j < n)
        def _():
            net.copy(left + j - 1, at(p + j), at(p + j), other).wait_recv()
            if j < n - 1:
                pl.when(p > 0)(lambda: go_left(j).start())
            pass_l(j).start()

        if landed:
            complete(j - 1)

    yield at_us + hop * (n - 1) + over
    for j in range(n - 1 if landed else 0, n):
        complete(j)

    def finish():
        own.wait_send()
        for j in range(n):
            if j < n - 1:
                pl.when((p - j >= 0) & (p + 1 < n))(lambda: go_right(j).wait_send())
                pl.when((p + j < n) & (p > 0))(lambda: go_left(j).wait_send())
            if j > 0:
                pl.when(p - j >= 0)(lambda: pass_r(j).wait_send())
                pl.when(p + j < n)(lambda: pass_l(j).wait_send())

    net.later.append(finish)


def add_rows(dst, srcs, step=16):
    def one(i, _):
        at = pl.ds(pl.multiple_of(i * step, step), step)
        total = srcs[0][at, :].astype(F32)
        for s in srcs[1:]:
            total = total + s[at, :].astype(F32)
        dst[at, :] = total.astype(dst.dtype)
        return 0

    if len(dst.shape) == 3:

        def layer(k, _):
            add_rows(dst.at[k], [s.at[k] for s in srcs], step)
            return 0

        lax.fori_loop(0, dst.shape[0], layer, 0)
    else:
        lax.fori_loop(0, dst.shape[0] // step, one, 0)


def scatter_scratch(ro_length, *shape):
    return [pltpu.VMEM((ro_length, *shape), BF16)] + [
        pltpu.VMEM((ro_length - 1, *shape), BF16)
    ] * 2


def scatter(
    net, ro, part, result, room, at_us=0.0, first=2.0, hop=11.0, hold=False, ready=None
):
    sib, in_r, in_l = room
    n, p, q = ro.length, ro.p, ro.q
    right, left, pair = net.take(n - 1), net.take(n - 1), net.take(n)
    other = ro.dev(p, 1 - q)
    order = []
    for j in range(n):
        order += [d for d in (n - 1 - j, j) if d not in order]
    mine = lambda d: part(ro.index(d, q))
    swap = lambda d: net.copy(pair + d, part(ro.index(d, 1 - q)), sib.at[d], other)
    send_r = lambda j: net.copy(right + j, in_r.at[j], in_r.at[j], ro.dev(p + 1, q))
    send_l = lambda j: net.copy(left + j, in_l.at[j], in_l.at[j], ro.dev(p - 1, q))
    if hold:
        yield at_us
    if n == 2:
        order = [1 - p, p]
    for d in order:
        if ready:
            ready(d)
        swap(d).start()
    for j in range(n - 1):
        yield at_us + first + hop * j
        dr, dl = n - 1 - j, j

        @pl.when(p < dr)
        def _():
            swap(dr).wait_recv()

            @pl.when(p > 0)
            def _():
                send_r(j).wait_recv()
                add_rows(in_r.at[j], [mine(dr), sib.at[dr], in_r.at[j]])

            @pl.when(p == 0)
            def _():
                add_rows(in_r.at[j], [mine(dr), sib.at[dr]])

            send_r(j).start()

        @pl.when(p > dl)
        def _():
            swap(dl).wait_recv()

            @pl.when(p < n - 1)
            def _():
                send_l(j).wait_recv()
                add_rows(in_l.at[j], [mine(dl), sib.at[dl], in_l.at[j]])

            @pl.when(p == n - 1)
            def _():
                add_rows(in_l.at[j], [mine(dl), sib.at[dl]])

            send_l(j).start()

    yield at_us + first + hop * (n - 1)
    from_r, from_l = n - 1 - p, p
    swap(p).wait_recv()

    @pl.when(p > 0)
    def _():
        send_r(from_r).wait_recv()

    @pl.when(p < n - 1)
    def _():
        send_l(from_l).wait_recv()

    @pl.when(p == 0)
    def _():
        add_rows(result, [mine(p), sib.at[p], in_l.at[from_l]])

    @pl.when(p == n - 1)
    def _():
        add_rows(result, [mine(p), sib.at[p], in_r.at[from_r]])

    if n > 2:

        @pl.when((p > 0) & (p < n - 1))
        def _():
            add_rows(result, [mine(p), sib.at[p], in_r.at[from_r], in_l.at[from_l]])

    def finish():
        for d in range(n):
            swap(d).wait_send()
        for j in range(n - 1):
            pl.when(p < n - 1 - j)(lambda: send_r(j).wait_send())
            pl.when(p > j)(lambda: send_l(j).wait_send())

    net.later.append(finish)


def direct_scratch(ro_length, *shape):
    return [
        pltpu.VMEM((ro_length, *shape), BF16),
        pltpu.VMEM((ro_length - 1, *shape), BF16),
    ]


class Direct:
    def __init__(self, net, ro, part, room):
        self.net, self.ro, self.part = net, ro, part
        self.sib, self.came = room
        self.pair, self.slots = net.take(ro.length), net.take(ro.length - 1)

    def mine(self, d):
        return self.part(self.ro.index(d, self.ro.q))

    def swap(self, d):
        ro = self.ro
        away = self.part(ro.index(d, 1 - ro.q))
        return self.net.copy(self.pair + d, away, self.sib.at[d], ro.dev(ro.p, 1 - ro.q))

    def move(self, d):
        ro = self.ro
        k = (d - ro.p + ro.length) % ro.length - 1
        return self.net.copy(self.slots + k, self.mine(d), self.came.at[k], ro.dev(d, ro.q))

    def ship(self, d):
        self.swap(d).wait_recv()
        add_rows(self.mine(d), [self.mine(d), self.sib.at[d]])
        pl.when(d != self.ro.p)(lambda: self.move(d).start())

    def total(self, result):
        ro = self.ro
        for k in range(ro.length - 1):
            self.net.copy(
                self.slots + k, self.came.at[k], self.came.at[k], ro.dev(ro.p, 1 - ro.q)
            ).wait_recv()
        add_rows(result, [self.mine(ro.p)] + [self.came.at[k] for k in range(ro.length - 1)])

    def finish(self):
        for d in range(self.ro.length):
            self.swap(d).wait_send()
            pl.when(d != self.ro.p)(lambda: self.move(d).wait_send())


def direct(net, ro, part, result, room, ready, at_us, last, hold=False):
    work = Direct(net, ro, part, room)
    n = ro.length
    if hold:
        yield at_us
    order = [(ro.p + n // 2 + o) % n for o in range(n)]
    for d in order:
        if ready:
            ready(d)
        work.swap(d).start()
    for d in order:
        work.ship(d)
    yield at_us + last
    work.total(result)
    net.later.append(work.finish)


def relay_scratch(ro_length, *shape):
    if ro_length != 4:
        return direct_scratch(ro_length, *shape) + [pltpu.VMEM((8, 128), BF16)]
    return [pltpu.VMEM((k, *shape), BF16) for k in (4, 2, 2)]


def relay(net, ro, part, result, room, ready, at_us, hop, last, hold=False):
    if ro.length != 4:
        yield from direct(net, ro, part, result, room[:2], ready, at_us, last, hold)
        return
    sib, came, passed = room
    p, q = ro.p, ro.q
    pair, slots, relays = net.take(4), net.take(2), net.take(2)
    other = ro.dev(p, 1 - q)
    mine = lambda d: part(ro.index(d, q))
    swap = lambda d: net.copy(pair + d, part(ro.index(d, 1 - q)), sib.at[d], other)
    inner = (p == 1) | (p == 2)
    mate = (p // 2) * 2 + 1 - p % 2
    pass_on = lambda k: net.copy(relays + k, mine((1 - p // 2) * 2 + k), passed.at[k], ro.dev(mate, q))
    move = lambda d: net.copy(
        slots + jnp.where(d // 2 == p // 2, 0, 1),
        mine(d),
        came.at[jnp.where(d // 2 == p // 2, 0, 1)],
        ro.dev(d, q),
    )
    if hold:
        yield at_us
    far = (1 - p // 2) * 2
    order = [far, far + 1, mate, p]
    for d in order:
        if ready:
            ready(d)
        swap(d).start()
    for d in order:
        swap(d).wait_recv()
        add_rows(mine(d), [mine(d), sib.at[d]])
        if d is far or d is order[1]:
            k = 0 if d is far else 1
            pl.when(jnp.logical_not(inner))(lambda: pass_on(k).start())
        elif d is mate:
            move(d).start()
    for k in range(2):
        yield at_us + hop * (k + 1)

        @pl.when(inner)
        def _():
            pass_on(k).wait_recv()
            add_rows(mine(far + k), [mine(far + k), passed.at[k]])
            move(far + k).start()

    yield at_us + last
    for k in range(2):
        net.copy(slots + k, came.at[k], came.at[k], other).wait_recv()
    add_rows(result, [mine(p), came.at[0], came.at[1]])

    def finish():
        for d in range(4):
            swap(d).wait_send()
        move(mate).wait_send()
        for k in range(2):
            pl.when(inner)(lambda: move(far + k).wait_send())
            pl.when(jnp.logical_not(inner))(lambda: pass_on(k).wait_send())

    net.later.append(finish)


def exchange(net, axis, src, place, at_us=0.0, last=15.0, hold=False):
    me, n = lax.axis_index(axis), lax.axis_size(axis)
    slots = net.take(n - 1)
    if hold:
        yield at_us
    near = net.local(src(me), place(me))
    sent = []
    for o in range(1, n):
        to = (me + o) % n
        sent.append(net.copy(slots + o - 1, src(to), place(me), {axis: to}))
        sent[-1].start()
    yield at_us + last
    near.wait()
    for o in range(1, n):
        at = (me + n - o) % n
        net.copy(slots + o - 1, src(at), place(at), {axis: at}).wait_recv()
    net.later.append(lambda: [s.wait_send() for s in sent])


def run(net, *gens):
    waiting = []
    for order, g in enumerate(gens):
        heapq.heappush(waiting, (0.0, order, g))
    while waiting:
        now, order, g = heapq.heappop(waiting)
        step = next(g, None)
        if step is not None:
            heapq.heappush(waiting, (max(step, now), order, g))
    for act in net.later:
        act()


def merge(gens):
    steps = [next(g, None) for g in gens]
    while any(s is not None for s in steps):
        at, k = min((s, i) for i, s in enumerate(steps) if s is not None)
        yield at
        steps[k] = next(gens[k], None)


def follow(first, makers):
    yield from merge(first)
    yield from merge([m() for m in makers])


VM = pl.BlockSpec(memory_space=pltpu.VMEM)
HB = pl.BlockSpec(memory_space=pl.ANY)


def comm_call(slots, kernel, cid, ins, in_specs, outs, out_specs, room):
    return pl.pallas_call(
        kernel,
        out_shape=[jax.ShapeDtypeStruct(*o) for o in outs],
        in_specs=in_specs,
        out_specs=out_specs,
        scratch_shapes=[
            pltpu.SemaphoreType.DMA((slots,)),
            pltpu.SemaphoreType.DMA((slots,)),
            pltpu.SemaphoreType.DMA((40,)),
        ]
        + room,
        compiler_params=pltpu.CompilerParams(
            collective_id=cid, has_side_effects=True, vmem_limit_bytes=60 << 20
        ),
    )(*ins)


def pair_masks():
    lane = lax.broadcasted_iota(jnp.int32, (1, 2 * HD), 1)
    return [lane < HD, lane >= HD]


def block_scores(key_rows, query_block, start_row, first, slope):
    count, width = key_rows.shape[0], query_block.shape[0]
    raw = lax.dot_general(
        key_rows, query_block, (((1,), (1,)), ((), ())), preferred_element_type=F32
    )
    key_at = lax.broadcasted_iota(jnp.int32, (count, width), 0)
    query_at = lax.broadcasted_iota(jnp.int32, (1, width), 1) + first
    scores = raw - slope * (query_at - key_at).astype(F32)
    allowed = (key_at <= query_at) & (key_at >= start_row)
    return jnp.where(allowed, scores, -1e30)


def attend(block, slopes, start_ref, mixed, out, lse_ref):
    length, width = out.shape
    wide = 2 * HD

    def one_pair(pair, _):
        column = lambda k: pl.ds(pl.multiple_of(k * width + pair * wide, wide), wide)
        q_at, k_at, v_at = column(0), column(1), column(2)
        for half, mask in enumerate(pair_masks()):
            keys = jnp.where(mask, mixed[:, k_at], 0)
            turned = jnp.where(mask, mixed[:, v_at], 0).T
            slope = slopes[2 * pair + half]
            for first in range(0, length, block):
                here, upto = slice(first, first + block), first + block
                query_block = mixed[here, q_at] * BF16(HD**-0.5)
                scores = block_scores(
                    keys[:upto], query_block, start_ref[:, here], first, slope
                )
                top = jnp.max(scores, axis=0, keepdims=True)
                weights = jnp.exp(scores - top)
                total = jnp.sum(weights, axis=0, keepdims=True)
                lse_ref[pair, half : half + 1, here] = top + jnp.log(total)
                probs = (weights * (1.0 / total)).astype(BF16)
                got = jnp.dot(turned[:, :upto], probs, preferred_element_type=F32).T
                if half == 0:
                    out[here, q_at] = got.astype(BF16)
                else:
                    out[here, q_at] = out[here, q_at] + got.astype(BF16)
        return 0

    lax.fori_loop(0, width // wide, one_pair, 0)


def attend_back(block, slopes, start_ref, mixed, att, grad, lse_ref, out, dk, dv):
    length, width = att.shape
    wide = 2 * HD
    pairs = width // wide

    def one_pair(pair, _):
        column = lambda k: pl.ds(pl.multiple_of(k * width + pair * wide, wide), wide)
        q_at, k_at, v_at = column(0), column(1), column(2)
        dk[...] = jnp.zeros_like(dk)
        dv[...] = jnp.zeros_like(dv)
        for half, mask in enumerate(pair_masks()):
            keys = jnp.where(mask, mixed[:, k_at], 0)
            values = jnp.where(mask, mixed[:, v_at], 0)
            turned = keys.T * BF16(HD**-0.5)
            slope = slopes[2 * pair + half]
            for first in range(0, length, block):
                here, upto = slice(first, first + block), first + block
                query_block = jnp.where(mask, mixed[here, q_at], 0) * BF16(HD**-0.5)
                grad_block = jnp.where(mask, grad[here, q_at], 0)
                product = att[here, q_at].astype(F32) * grad_block.astype(F32)
                delta = jnp.sum(product.T, axis=0, keepdims=True)
                scores = block_scores(
                    keys[:upto], query_block, start_ref[:, here], first, slope
                )
                probs = jnp.exp(scores - lse_ref[pair, half : half + 1, here])
                prob_grad = lax.dot_general(
                    values[:upto], grad_block, (((1,), (1,)), ((), ())), preferred_element_type=F32
                )
                score_grad = (probs * (prob_grad - delta)).astype(BF16)
                dv[:upto, :] += jnp.dot(
                    probs.astype(BF16), grad_block, preferred_element_type=F32
                )
                dk[:upto, :] += jnp.dot(score_grad, query_block, preferred_element_type=F32)
                got = jnp.dot(turned[:, :upto], score_grad, preferred_element_type=F32).T
                if half == 0:
                    out[here, q_at] = got.astype(BF16)
                else:
                    out[here, q_at] = out[here, q_at] + got.astype(BF16)
        out[:, k_at] = dk[...].astype(BF16)
        out[:, v_at] = dv[...].astype(BF16)
        return 0

    lax.fori_loop(0, pairs, one_pair, 0)


def layer_norm(values, gain_row, shift_row):
    centred = values - jnp.mean(values, axis=-1, keepdims=True)
    spread = jnp.mean(centred * centred, axis=-1, keepdims=True)
    return centred * lax.rsqrt(spread + epsilon) * gain_row + shift_row


def gelu_exact(values):
    return jax.nn.gelu(values, approximate=False)


def body(
    tokens,
    segments,
    cotangent,
    mix_weight,
    mix_moment,
    mix_average,
    out_weight,
    out_moment,
    out_average,
    up_weight,
    up_moment,
    up_average,
    down_weight,
    down_moment,
    down_average,
    norm_gains,
    gain_moment,
    gain_average,
    biases,
    bias_moment,
    bias_average,
):
    S, F = lax.axis_size("seq"), lax.axis_size("fsdp")
    owners = S * F
    s_at = lax.axis_index("seq")
    T = tokens.shape[1]
    L = T * S
    R = D // owners
    RD = FF // owners
    W = D // S
    U = FF // S
    heads = HEADS // S
    slots = 20 * max(S, F)
    call = functools.partial(comm_call, slots)

    head_ids = s_at * heads + jnp.arange(heads, dtype=jnp.int32) + 1
    slopes = jnp.exp2(-8.0 * head_ids.astype(F32) / HEADS)
    documents = segments[0]
    start = jnp.sum(documents[:, None] < documents[None, :], axis=0, dtype=jnp.int32)[None]

    mix_low = mix_weight.astype(BF16).reshape(R, 3, S, W).transpose(2, 0, 1, 3).reshape(S, R, 3 * W)
    up_low = up_weight.astype(BF16).reshape(R, S, U).transpose(1, 0, 2)
    out_low = out_weight.astype(BF16)
    down_low = down_weight.astype(BF16)
    small = jnp.concatenate([norm_gains, biases], axis=0).astype(BF16).astype(F32)
    place_at = (s_at * F + lax.axis_index("fsdp")) * R % 128
    small = lax.dynamic_update_slice(jnp.zeros((16, 128), F32), small, (0, place_at))

    G = D // S
    n = S // 2

    def first_kernel(
        slope_values,
        tok,
        mix,
        out,
        vec,
        up,
        cot,
        down,
        begin,
        total,
        vecs,
        mix_out,
        out_w,
        up_f,
        down_f,
        cot_f,
        one_out,
        mixed,
        att,
        lse,
        send,
        recv,
        near,
        tok_v,
        one_v,
        mix_v,
        out_v,
        vec_f,
        up_r,
        part,
        *room,
    ):
        net = Net(send, recv, near)
        seq, sides = line_of("seq"), both_of("fsdp")
        s, f = lax.axis_index("seq"), lax.axis_index("fsdp")
        block = lambda ref, i: ref.at[pl.ds(pl.multiple_of(i * T, T), T)]
        owned = [net.local(out, out_v.at[f]), net.local(cot, cot_f.at[s]), net.local(down, down_f.at[f])]
        tok_own = net.local(tok, block(tok_v, s))
        vec_own = net.local(vec, vec_f.at[s, f])
        greet(everyone("seq") + everyone("fsdp"))

        def mix_half(k):
            at = pl.ds(k * (S // 2), S // 2)
            return lambda: gather(
                net, sides[k], mix_v.at[at, f], lambda i: mix_v.at[at, i], 20, 13, 13
            )

        def out_half(k):
            at = pl.ds(k * (D // 2), D // 2)
            return gather(net, sides[k], out.at[:, at], lambda i: out_v.at[i, :, at], 0, 5, 5)

        def down_half(k):
            at = pl.ds(k * (RD // 2), RD // 2)
            return gather(
                net, sides[k], down.at[at], lambda i: down_f.at[i, at], 46, 24, 28, True
            )

        def up_half(k):
            at = pl.ds(k * (S // 2), S // 2)
            return lambda: gather(
                net, sides[k], up_r.at[at], lambda i: up_f.at[at, i], 86, 17, 25
            )

        def vec_next():
            vec_own.wait()
            return gather(net, sides[0], vec_f.at[:, f], lambda i: vec_f.at[:, i], 6, 1, 1)

        def vec_all():
            yield from follow(
                [gather(net, seq, vec, lambda i: vec_f.at[i, f], 0, 2, 1)], [vec_next]
            )
            each = 128 // R
            for c in range(D // 128):
                pieces = [
                    vec_f[i // F, i % F] for i in range(c * each, (c + 1) * each)
                ]
                vecs[:, c * 128 : (c + 1) * 128] = functools.reduce(jnp.add, pieces)
            tok_own.wait()

        def norm(k):
            step = 32

            def one(i, _):
                here = pl.ds(pl.multiple_of(k * 2 * T + i * step, step), step)
                one_v[here, :] = layer_norm(
                    tok_v[here, :].astype(F32), vecs[0:1, :], vecs[2:3, :]
                ).astype(BF16)
                return 0

            lax.fori_loop(0, 2 * T // step, one, 0)

        leave = lambda: [
            pltpu.make_async_copy(one_v, one_out, near.at[30]),
            pltpu.make_async_copy(mix_v, mix_out, near.at[31]),
            pltpu.make_async_copy(out_v, out_w, near.at[32]),
        ]

        def project():
            yield 58.0
            owned[0].wait()
            for made in leave():
                made.start()
            for c in range(3):
                if c == 1:
                    bias = jnp.zeros((1, W), F32)
                else:
                    bias = vecs[3 + c // 2 : 4 + c // 2, pl.ds(pl.multiple_of(s * W, W), W)]
                at = slice(c * W, (c + 1) * W)

                def one(i, _):
                    here = pl.ds(pl.multiple_of(i * 2 * T, 2 * T), 2 * T)
                    mixed[here, at] = (
                        jnp.dot(
                            one_v[here, :],
                            mix_v[:, :, :, at].reshape(D, W),
                            preferred_element_type=F32,
                        )
                        + bias
                    ).astype(BF16)
                    return 0

                lax.fori_loop(0, n, one, 0)
            yield 62.0
            attend(min(256, L), slope_values, begin, mixed, att, lse)

        def ready(d):
            here = pl.ds(pl.multiple_of(d * 2 * T, 2 * T), 2 * T)

            def one(i, _):
                at = pl.ds(pl.multiple_of(i * 512, 512), 512)
                part[here, at] = jnp.dot(
                    att[here, :], out_v[:, :, at].reshape(W, 512), preferred_element_type=F32
                ).astype(BF16)
                return 0

            lax.fori_loop(0, D // 512, one, 0)

        run(
            net,
            follow(
                [exchange(net, "seq", lambda i: mix.at[i], lambda i: mix_v.at[i, f], 0, 18)],
                [mix_half(0), mix_half(1)],
            ),
            vec_all(),
            out_half(0),
            out_half(1),
            gather(net, seq, tok, lambda i: block(tok_v, i), 8, 15, 1, True, norm),
            down_half(0),
            down_half(1),
            follow(
                [exchange(net, "seq", lambda i: up.at[i], lambda i: up_r.at[i], 57, 28, True)],
                [up_half(0), up_half(1)],
            ),
            project(),
            gather(net, seq, cot, lambda i: cot_f.at[i], 57, 17, hold=True),
            relay(net, seq, lambda i: block(part, i), total, room, ready, 74, 16, 60, True),
        )
        up_own = [net.local(up_r, up_f.at[:, f])]
        for made in owned[1:] + leave() + up_own:
            made.wait()

    (
        attn_sum,
        vectors,
        mix_full,
        out_full,
        up_full,
        down_full,
        cot_full,
        normed,
        mixed,
        attended,
        log_sums,
    ) = call(
        first_kernel,
        1,
        (
            slopes,
            tokens[0],
            mix_low,
            out_low,
            small,
            up_low,
            cotangent[0],
            down_low,
            start,
        ),
        [pl.BlockSpec(memory_space=pltpu.SMEM), HB, HB, HB, VM, HB, HB, HB, VM],
        [
            ((T, D), F32),
            ((16, D), F32),
            ((S, F, R, 3 * W), BF16),
            ((F, R, D), BF16),
            ((S, F, R, U), BF16),
            ((F, RD, D), BF16),
            ((S, T, D), BF16),
            ((L, D), BF16),
            ((L, 3 * W), BF16),
            ((L, W), BF16),
            ((heads // 2, 2, L), F32),
        ],
        [VM, VM, HB, HB, HB, HB, HB, HB, VM, VM, VM],
        [
            pltpu.VMEM((L, D), BF16),
            pltpu.VMEM((L, D), BF16),
            pltpu.VMEM((S, F, R, 3 * W), BF16),
            pltpu.VMEM((F, R, D), BF16),
            pltpu.VMEM((S, F, 16, 128), F32),
            pltpu.VMEM((S, R, U), BF16),
            pltpu.VMEM((L, D), BF16),
        ]
        + relay_scratch(n, T, D),
    )
    gain_values, bias_values = vectors[:2], vectors[2:12]
    mine = lambda row, width: lax.dynamic_slice_in_dim(row.reshape(-1), s_at * width, width)
    mix_own = mix_full.reshape(D, 3 * W)
    out_own = out_full.reshape(W, D)
    row_values = tokens[0].astype(F32)
    hidden_in = row_values + attn_sum + bias_values[3]
    normed_two = layer_norm(hidden_in, gain_values[1], bias_values[4]).astype(BF16)

    B = 2 * T
    UT = min(256, U)
    down_items, items = U // UT, U // UT + S

    def middle_kernel(
        rows,
        up,
        down,
        cot,
        bias,
        total,
        result_out,
        up_out,
        down_out,
        sums,
        send,
        recv,
        near,
        two,
        up_v,
        down_v,
        cot_v,
        act,
        pre,
        turn,
        part_n,
        part_r,
        *room,
    ):
        net = Net(send, recv, near)
        ro = line_of("seq")
        p, q = ro.p, ro.q
        other = ro.dev(p, 1 - q)
        loads = [net.local(up, up_v), net.local(down, down_v), net.local(cot, cot_v)]
        sums[...] = jnp.zeros_like(sums)
        greet(ro.partners())
        block = lambda ref, i: ref.at[pl.ds(pl.multiple_of(i * T, T), T)]
        place = lambda k, side: block(two, ro.index(k, side))
        loads.append(net.local(rows, place(p, q)))
        ag_r, ag_l, over = net.take(n - 1), net.take(n - 1), net.take(n)
        sums_of = Direct(net, ro, lambda i: block(part_n, i), room)
        ag_right = lambda k, src: net.copy(ag_r + p - k, src, place(k, q), ro.dev(p + 1, q))
        ag_left = lambda k, src: net.copy(ag_l + k - p, src, place(k, q), ro.dev(p - 1, q))
        ag_over = lambda k, src: net.copy(over + k, src, place(k, q), other)
        leave = lambda k: pltpu.make_async_copy(
            part_r.at[pl.ds(pl.multiple_of(k * B, B), B)],
            result_out.at[pl.ds(pl.multiple_of(k * B, B), B)],
            near.at[8 + k],
        )

        pl.when(p + 1 < n)(lambda: ag_right(p, rows).start())
        pl.when(p > 0)(lambda: ag_left(p, rows).start())
        ag_over(p, rows).start()
        for made in loads:
            made.wait()

        def arrive(e):
            @pl.when((e > 0) & (p - e >= 0))
            def _():
                k = p - e
                net.copy(ag_r + e - 1, place(k, q), place(k, q), other).wait_recv()
                pl.when(p + 1 < n)(lambda: ag_right(k, place(k, q)).start())
                ag_over(k, place(k, q)).start()

            @pl.when((e > 0) & (p + e < n))
            def _():
                k = p + e
                net.copy(ag_l + e - 1, place(k, q), place(k, q), other).wait_recv()
                pl.when(p > 0)(lambda: ag_left(k, place(k, q)).start())
                ag_over(k, place(k, q)).start()

        def feed_forward(k):
            net.copy(over + k, place(k, 1 - q), place(k, 1 - q), other).wait_recv()
            here = pl.ds(pl.multiple_of(k * B, B), B)

            def hidden(i, _):
                at = pl.ds(pl.multiple_of(i * UT, UT), UT)
                value = jnp.dot(two[here, :], up_v[:, at], preferred_element_type=F32) + bias[:, at]
                chance = 0.5 + 0.5 * lax.erf(value * 0.5**0.5)
                slope = chance + value * (jnp.exp(value * value * -0.5) * (2 * math.pi) ** -0.5)
                act[here, at] = (value * chance).astype(BF16)
                grad = lax.dot_general(
                    cot_v[here, :], down_v[at, :], (((1,), (1,)), ((), ())), preferred_element_type=F32
                )
                low = (grad * slope).astype(BF16)
                pre[here, at] = low
                sums[:, at] += jnp.sum(low.astype(F32), axis=0, keepdims=True)
                return 0

            lax.fori_loop(0, U // UT, hidden, 0)

            def back(i, _):
                at = pl.ds(pl.multiple_of(i * 512, 512), 512)
                part_n[here, at] = lax.dot_general(
                    pre[here, :], up_v[at, :], (((1,), (1,)), ((), ())), preferred_element_type=F32
                ).astype(BF16)
                return 0

            lax.fori_loop(0, D // 512, back, 0)
            sums_of.swap(k).start()

            def forth(i, _):
                at = pl.ds(pl.multiple_of(i * 512, 512), 512)
                part_r[here, at] = jnp.dot(
                    act[here, :], down_v[:, at], preferred_element_type=F32
                ).astype(BF16)
                return 0

            lax.fori_loop(0, D // 512, forth, 0)
            leave(k).start()
            sums_of.ship(k)

        def outward(e, _):
            arrive(e)
            for side in (-1, 1):
                k = p + side * e
                pl.when((k >= 0) & (k < n) & ((e > 0) | (side > 0)))(lambda: feed_forward(k))
            return 0

        lax.fori_loop(0, n, outward, 0)
        up_leave = lambda i: pltpu.make_async_copy(
            up_v.at[pl.ds(pl.multiple_of(i * G, G), G)],
            up_out.at[pl.ds(pl.multiple_of(i * G, G), G)],
            near.at[16 + i],
        )
        down_leave = lambda i: pltpu.make_async_copy(
            down_v.at[pl.ds(pl.multiple_of(i * UT, UT), UT)],
            down_out.at[pl.ds(pl.multiple_of(i * UT, UT), UT)],
            near.at[4 + i],
        )

        def item(i, _):
            @pl.when(i < down_items)
            def _():
                here = pl.ds(pl.multiple_of(i * UT, UT), UT)
                turn[:UT, :] = act[:, here].T

                def one(j, _):
                    at = pl.ds(pl.multiple_of(j * 512, 512), 512)
                    down_v[here, at] = jnp.dot(
                        turn[:UT, :], cot_v[:, at], preferred_element_type=F32
                    ).astype(BF16)
                    return 0

                lax.fori_loop(0, D // 512, one, 0)
                down_leave(i).start()

            @pl.when((i >= down_items) & (i < items))
            def _():
                c = i - down_items
                here = pl.ds(pl.multiple_of(c * G, G), G)
                turn[:G, :] = two[:, here].T

                def one(j, _):
                    at = pl.ds(pl.multiple_of(j * UT, UT), UT)
                    up_v[here, at] = jnp.dot(
                        turn[:G, :], pre[:, at], preferred_element_type=F32
                    ).astype(BF16)
                    return 0

                lax.fori_loop(0, U // UT, one, 0)
                up_leave(c).start()

            return 0

        lax.fori_loop(0, items, item, 0)
        sums_of.total(total)

        def last(k, _):
            ag_over(k, place(k, q)).wait_send()
            leave(k).wait()
            pl.when((k <= p) & (p + 1 < n))(lambda: ag_right(k, place(k, q)).wait_send())
            pl.when((k >= p) & (p > 0))(lambda: ag_left(k, place(k, q)).wait_send())
            return 0

        lax.fori_loop(0, n, last, 0)
        sums_of.finish()
        for i in range(down_items):
            down_leave(i).wait()
        for i in range(S):
            up_leave(i).wait()

    two_grad, result_part, up_part, down_part, pre_sum = call(
        middle_kernel,
        3,
        (
            normed_two,
            up_full.reshape(D, U),
            down_full.reshape(U, D),
            cot_full.reshape(L, D),
            mine(bias_values[6:10], U)[None],
        ),
        [HB] * 4 + [VM],
        [((T, D), F32), ((L, D), BF16), ((D, U), BF16), ((U, D), BF16), ((1, U), F32)],
        [VM, HB, HB, HB, VM],
        [
            pltpu.VMEM((L, D), BF16),
            pltpu.VMEM((D, U), BF16),
            pltpu.VMEM((U, D), BF16),
            pltpu.VMEM((L, D), BF16),
            pltpu.VMEM((L, U), BF16),
            pltpu.VMEM((L, U), BF16),
            pltpu.VMEM((256, L), BF16),
            pltpu.VMEM((L, D), BF16),
            pltpu.VMEM((L, D), BF16),
        ]
        + direct_scratch(n, T, D),
    )
    upstream_float = cotangent[0].astype(F32)
    second_pull = jax.vjp(layer_norm, hidden_in, gain_values[1], bias_values[4])[1]
    hidden_part, gain_two_gradient, shift_two_gradient = second_pull(two_grad)
    hidden_gradient = upstream_float + hidden_part
    hidden_low = hidden_gradient.astype(BF16)

    def fifth_kernel(
        slope_values,
        rows,
        part,
        up,
        down,
        out_w,
        mixed_v,
        att,
        lse,
        begin,
        total,
        up_s,
        down_s,
        grads,
        out_p,
        send,
        recv,
        near,
        hidden,
        att_grad,
        dk,
        dv,
        up_r,
        *room,
    ):
        net = Net(send, recv, near)
        seq, sides = line_of("seq"), both_of("fsdp")
        s = lax.axis_index("seq")
        greet(everyone("seq") + everyone("fsdp"))
        block = lambda i: hidden.at[pl.ds(pl.multiple_of(i * T, T), T)]
        own = net.local(rows, block(s))

        def up_half(k):
            at = pl.ds(k * (S // 2), S // 2)
            return scatter(
                net, sides[k], lambda i: up.at[at, i], up_r.at[at], room[3 + 3 * k : 6 + 3 * k], 0, 12, 20
            )

        def down_half(k):
            at = pl.ds(k * (D // 2), D // 2)
            return scatter(
                net,
                sides[k],
                lambda i: down.at[i, :, at],
                down_s.at[:, at],
                room[9 + 3 * k : 12 + 3 * k],
                28,
                14,
                60,
                True,
            )

        def work():
            yield 49.0
            own.wait()

            def one(i, _):
                here = pl.ds(pl.multiple_of(i * 2 * T, 2 * T), 2 * T)
                att_grad[here, :] = lax.dot_general(
                    hidden[here, :], out_w[...], (((1,), (1,)), ((), ())), preferred_element_type=F32
                ).astype(BF16)
                return 0

            lax.fori_loop(0, S // 2, one, 0)
            attend_back(
                min(256, L), slope_values, begin, mixed_v, att, att_grad, lse, grads, dk, dv
            )

            def two(i, _):
                at = pl.ds(pl.multiple_of(i * 256, 256), 256)
                out_p[:, at] = lax.dot_general(
                    att[...], hidden[:, at], (((0,), (0,)), ((), ())), preferred_element_type=F32
                ).astype(BF16)
                return 0

            lax.fori_loop(0, D // 256, two, 0)

        run(
            net,
            gather(net, seq, rows, block, 0, 14),
            relay(net, seq, lambda i: part.at[i], total, room[:3], None, 30, 14, 500, True),
            follow(
                [up_half(0), up_half(1)],
                [lambda: exchange(net, "seq", lambda i: up_r.at[i], lambda i: up_s.at[i], 0, 300)],
            ),
            down_half(0),
            down_half(1),
            work(),
        )

    result_sum, up_share, down_share, mixed_grad, out_grad = call(
        fifth_kernel,
        5,
        (
            slopes,
            hidden_low,
            result_part.reshape(S, T, D),
            up_part.reshape(S, F, R, U),
            down_part.reshape(F, RD, D),
            out_own,
            mixed,
            attended,
            log_sums,
            start,
        ),
        [pl.BlockSpec(memory_space=pltpu.SMEM), HB] + [VM] * 8,
        [
            ((T, D), F32),
            ((S, R, U), BF16),
            ((RD, D), F32),
            ((L, 3 * W), BF16),
            ((W, D), BF16),
        ],
        [VM, HB, VM, VM, VM],
        [
            pltpu.VMEM((L, D), BF16),
            pltpu.VMEM((L, W), BF16),
            pltpu.VMEM((L, 2 * HD), F32),
            pltpu.VMEM((L, 2 * HD), F32),
            pltpu.VMEM((S, R, U), BF16),
        ]
        + relay_scratch(S // 2, T, D)
        + 2 * scatter_scratch(F // 2, S // 2, R, U)
        + 2 * scatter_scratch(F // 2, RD, D // 2),
    )
    output = (hidden_in + result_sum + bias_values[5]).astype(BF16)[None]

    def sixth_kernel(
        grads,
        mix_w,
        first,
        out_p,
        total,
        mix_s,
        out_s,
        sums,
        send,
        recv,
        near,
        one_v,
        part,
        turn,
        mix_p,
        mix_r,
        *room,
    ):
        net = Net(send, recv, near)
        seq, sides = line_of("seq"), both_of("fsdp")
        greet(everyone("seq") + everyone("fsdp"))
        load = net.local(first, one_v)
        block = lambda i: part.at[pl.ds(pl.multiple_of(i * T, T), T)]

        def ready(d):
            here = pl.ds(pl.multiple_of(d * 2 * T, 2 * T), 2 * T)

            def one(i, _):
                at = pl.ds(pl.multiple_of(i * 512, 512), 512)
                part[here, at] = lax.dot_general(
                    grads[here, :], mix_w[at, :], (((1,), (1,)), ((), ())), preferred_element_type=F32
                ).astype(BF16)
                return 0

            lax.fori_loop(0, D // 512, one, 0)

        def mix_half(k):
            at = pl.ds(k * (S // 2), S // 2)
            yield 9.0 + 2 * k
            if k == 0:
                load.wait()

            def one(i, _):
                turn[...] = one_v[:, pl.ds(pl.multiple_of(i * G, G), G)].T
                got = jnp.dot(turn[...], grads[...], preferred_element_type=F32).astype(BF16)
                for f in range(F):
                    mix_p[i, f] = got[f * R : (f + 1) * R]
                return 0

            lax.fori_loop(k * (S // 2), (k + 1) * (S // 2), one, 0)
            yield from scatter(
                net, sides[k], lambda i: mix_p.at[at, i], mix_r.at[at], room[3 + 3 * k : 6 + 3 * k], 14, 8, 14
            )

        def out_half(k):
            at = pl.ds(k * (D // 2), D // 2)
            return scatter(
                net,
                sides[k],
                lambda i: out_p.at[i, :, at],
                out_s.at[:, at],
                room[9 + 3 * k : 12 + 3 * k],
                30,
                12,
                20,
                True,
            )

        def columns():
            yield 16.0
            sums[...] = jnp.zeros_like(sums)

            def one(i, _):
                here = pl.ds(pl.multiple_of(i * T, T), T)
                sums[...] += jnp.sum(grads[here, :].astype(F32), axis=0, keepdims=True)
                return 0

            lax.fori_loop(0, S, one, 0)

        run(
            net,
            relay(net, seq, block, total, room[:3], ready, 0, 15, 75),
            follow(
                [mix_half(0), mix_half(1)],
                [lambda: exchange(net, "seq", lambda i: mix_r.at[i], lambda i: mix_s.at[i], 0, 60)],
            ),
            out_half(0),
            out_half(1),
            columns(),
        )

    one_grad, mix_share, out_share, mixed_sum = call(
        sixth_kernel,
        6,
        (mixed_grad, mix_own, normed, out_grad.reshape(F, R, D)),
        [VM, VM, HB, VM],
        [((T, D), F32), ((S, R, 3 * W), BF16), ((R, D), F32), ((1, 3 * W), F32)],
        [VM, HB, VM, VM],
        [
            pltpu.VMEM((L, D), BF16),
            pltpu.VMEM((L, D), BF16),
            pltpu.VMEM((G, L), BF16),
            pltpu.VMEM((S, F, R, 3 * W), BF16),
            pltpu.VMEM((S, R, 3 * W), BF16),
        ]
        + relay_scratch(S // 2, T, D)
        + 2 * scatter_scratch(F // 2, S // 2, R, 3 * W)
        + 2 * scatter_scratch(F // 2, R, D // 2),
    )
    mixed_sum = mixed_sum[0]
    first_pull = jax.vjp(layer_norm, row_values, gain_values[0], bias_values[0])[1]
    rows_part, gain_one_gradient, shift_one_gradient = first_pull(one_grad)
    tokens_grad = (hidden_gradient + rows_part).astype(BF16)[None]

    def spread(row, count):
        return lax.dynamic_update_slice_in_dim(
            jnp.zeros((count * S * row.shape[0] // count,), F32), row, s_at * row.shape[0], 0
        ).reshape(count, D)

    small_gradient = jnp.concatenate(
        [
            gain_one_gradient[None],
            gain_two_gradient[None],
            shift_one_gradient[None],
            spread(mixed_sum[:W], 1),
            spread(mixed_sum[2 * W :], 1),
            jnp.sum(hidden_gradient, axis=0)[None],
            shift_two_gradient[None],
            jnp.sum(upstream_float, axis=0)[None],
            spread(pre_sum[0], 4),
        ],
        axis=0,
    )
    small_gradient = jnp.pad(
        small_gradient.reshape(12, S, F, R).transpose(1, 2, 0, 3),
        ((0, 0), (0, 0), (0, 4), (0, 128 - R)),
    )

    def last_kernel(vec, total, send, recv, near, got, mid, got_two):
        net = Net(send, recv, near)
        greet(everyone("seq") + everyone("fsdp"))
        for _ in exchange(net, "seq", lambda i: vec.at[i], lambda i: got.at[i]):
            pass
        mid[...] = jnp.sum(got[...], axis=0)
        for _ in exchange(net, "fsdp", lambda i: mid.at[i], lambda i: got_two.at[i]):
            pass
        total[...] = jnp.sum(got_two[...], axis=0)
        run(net)

    (small_share,) = call(
        last_kernel,
        7,
        (small_gradient,),
        [VM],
        [((16, 128), F32)],
        [VM],
        [
            pltpu.VMEM((S, F, 16, 128), F32),
            pltpu.VMEM((F, 16, 128), F32),
            pltpu.VMEM((F, 16, 128), F32),
        ],
    )
    mix_final = mix_share.astype(F32).reshape(S, R, 3, W).transpose(1, 2, 0, 3).reshape(R, 3 * D)
    up_final = up_share.astype(F32).transpose(1, 0, 2).reshape(R, FF)
    step_rate = base_rate / math.sqrt(owners * T)
    vector_step = vector_rate / math.sqrt(owners * T)
    rate_list = (step_rate, step_rate, step_rate, step_rate, vector_step, vector_step)
    masters = (mix_weight, out_weight, up_weight, down_weight, norm_gains, biases)
    shares = (mix_final, out_share, up_final, down_share, small_share[:2, :R], small_share[2:12, :R])
    moments = (mix_moment, out_moment, up_moment, down_moment, gain_moment, bias_moment)
    averages = (mix_average, out_average, up_average, down_average, gain_average, bias_average)
    updated = []
    for master, moment, average, share, rate in zip(masters, moments, averages, shares, rate_list):
        new_moment = mom_decay * moment + share
        new_weight = master - rate * (share + mom_decay * new_moment)
        new_average = avg_decay * average + (1.0 - avg_decay) * new_weight
        updated += [new_moment, new_weight, new_average]
    return (output, tokens_grad, *updated)


def solution(mesh):
    rows = P("fsdp", "seq", None)
    param = P(("seq", "fsdp"), None)
    vector = P(None, ("seq", "fsdp"))
    return jax.shard_map(
        body,
        mesh=mesh,
        in_specs=(rows, P("fsdp", None), rows) + (param,) * 12 + (vector,) * 6,
        out_specs=(rows, rows) + (param,) * 12 + (vector,) * 6,
        check_vma=False,
    )
```
